32 devices in a mesh: items: 32 (over z, y, x, core).
Axes of the slice: x: 2, y: 2, z: 4, core: 2. Of those that a mesh axis runs over, the one named last changes fastest.
Arguments:
- frames_in: float32 [32, 1024, 512], P('items'), may hold values from -6 to 6
- conditioning: float32 [32, 1024, 512], P('items'), may hold values from -6 to 6
- prompt: float32 [32, 896, 512], P(None, 'items'), may hold values from -6 to 6
- item_lengths: int32 [32], P('items'), may hold values from 128 to 1024, as said below
- prompt_lengths: int32 [32], replicated, may hold values from 89 to 896, as said below
- key_mask: int32 [32, 896], P(None, 'items'), may hold values 0 or 1
- diffusion_steps: int32 [32], P('items'), may hold values from 0 to 999
- step_proj: float32 [2, 512, 512], P(None, 'items'), may hold values from -0.25 to 0.25
- conv_weight: float32 [2, 1536, 1024], P(None, 'items'), may hold values from -0.15625 to 0.15625
- cond_proj: float32 [2, 512, 1024], P(None, 'items'), may hold values from -0.25 to 0.25
- out_proj: float32 [2, 512, 1024], P(None, 'items'), may hold values from -0.25 to 0.25
- query_seeds: float32 [2, 512, 32], P(None, 'items'), may hold values from -6 to 6
- query_proj: float32 [2, 512, 512], P(None, 'items'), may hold values from -0.25 to 0.25
- key_proj: float32 [2, 512, 512], P(None, 'items'), may hold values from -0.25 to 0.25
- value_proj: float32 [2, 512, 512], P(None, 'items'), may hold values from -0.25 to 0.25
- mixing_proj: float32 [2, 512, 512], P(None, 'items'), may hold values from -1 to 1
- film_proj: float32 [2, 512, 1024], P(None, 'items'), may hold values from -2 to 2
- cot_frames: float32 [32, 1024, 512], P('items'), may hold values from -6 to 6
- cot_skip: float32 [32, 1024, 512], P('items'), may hold values from -6 to 6
Outputs:
- frames_out: float32 [32, 1024, 512], P('items')
- skip_out: float32 [32, 1024, 512], P('items')
- grad_frames: float32 [32, 1024, 512], P('items')
- grad_step_proj: float32 [2, 512, 512], P(None, 'items')
- grad_conv_weight: float32 [2, 1536, 1024], P(None, 'items')
- grad_cond_proj: float32 [2, 512, 1024], P(None, 'items')
- grad_out_proj: float32 [2, 512, 1024], P(None, 'items')
- grad_query_seeds: float32 [2, 512, 32], P(None, 'items')
- grad_query_proj: float32 [2, 512, 512], P(None, 'items')
- grad_key_proj: float32 [2, 512, 512], P(None, 'items')
- grad_value_proj: float32 [2, 512, 512], P(None, 'items')
- grad_mixing_proj: float32 [2, 512, 512], P(None, 'items')
- grad_film_proj: float32 [2, 512, 1024], P(None, 'items')
The draws below stay inside these ranges and needn't reach their ends.
Inputs may be any that keep to these rules, and one draw needn't show every extreme that they name: `item_lengths`: some item has exactly 1024 live frames and another exactly 128. `prompt_lengths`: some item has exactly 896 prompt frames and another exactly 89.
All inputs are finite; a program needn't handle non-finite values. No bound on the sum of `key_mask` on one device may be relied on, other than what follows from the above.
Results may differ from the reference program's by a relative error of at most 0.0003.
Values sent between devices are 32-bit elements; how exact they have to be, the bound alone decides.
No kernel may reach another device: no remote copies, remote signals or barrier semaphores. Data moves between devices by JAX's collectives and lax.ppermute only.
A program may use at most 256 MiB of HBM per device.

```python
import math
import jax
import jax.numpy as jnp
from jax import lax

WIDTH = 512
HEADS = 8
QUERIES = 32
FRAMES = 1024
PROMPT = 896
LAYERS = 2
ITEMS = 32


def ragged_lengths(key, total_items, least, most):
    lengths_raw = jax.random.randint(key, (total_items,), least, most + 1)
    longest = jax.random.randint(jax.random.fold_in(key, 11), (), 0, total_items)
    shortest = (longest + jax.random.randint(jax.random.fold_in(key, 12), (), 1, total_items)) % total_items
    positions = jnp.arange(total_items)
    lengths_raw = jnp.where(positions == longest, most, lengths_raw)
    return jnp.where(positions == shortest, least, lengths_raw).astype(jnp.int32)


def draw_item_lengths(key, part):
    key = jax.random.fold_in(key, 1)
    return ragged_lengths(key, ITEMS, FRAMES // 8, FRAMES)


def draw_prompt_lengths(key, part):
    key = jax.random.fold_in(key, 2)
    return ragged_lengths(key, ITEMS, PROMPT // 10, PROMPT)


def plant(values, rng, low, high):
    longest = values.shape.index(max(values.shape))
    spots = []
    for shift in (0, 1):
        where = [jax.random.randint(jax.random.fold_in(rng, axis), (), 0, length) for axis, length in enumerate(values.shape)]
        where[longest] = (where[longest] + shift) % values.shape[longest]
        spots.append(tuple(where))
    return values.at[spots[0]].set(low).at[spots[1]].set(high)


def block_scale(key, extent, split, smallest, high):
    gain, own = 1.0, jax.random.fold_in(key, 6)
    for dim, shards_of in split:
        draws = jnp.exp(jax.random.uniform(jax.random.fold_in(own, dim), (shards_of,), jnp.float32, smallest / len(split), high / len(split)))
        gain = gain * jnp.repeat(draws, extent[dim] // shards_of).reshape([-1 if axis == dim else 1 for axis in range(len(extent))])
    return gain


def noise(own_key, shape, scale, bound, cuts=(), held_as=jnp.bfloat16):
    loudness = block_scale(own_key, shape, cuts, -0.22, 0.18) if cuts else 1.0
    result = jax.random.normal(own_key, shape, jnp.float32) * scale * loudness
    return jnp.minimum(jnp.maximum(result, -bound), bound).astype(held_as)


def setup_inputs(seed: int = 0) -> dict:
    key_list = jax.random.split(jax.random.key(seed), 20)
    frames_in = noise(key_list[0], (ITEMS, FRAMES, WIDTH), 1.0, 6.0, ((0, 32),), jnp.float32)
    conditioning = noise(key_list[1], (ITEMS, FRAMES, WIDTH), 1.0, 6.0, ((0, 32),), jnp.float32)
    prompt = noise(key_list[2], (ITEMS, PROMPT, WIDTH), 1.0, 6.0, ((1, 32),), jnp.float32)
    item_lengths = draw_item_lengths(jax.random.fold_in(key_list[19], 71), 0)
    prompt_lengths = draw_prompt_lengths(jax.random.fold_in(key_list[19], 71), 0)
    key_mask = plant((jax.random.randint(key_list[5], (ITEMS, PROMPT), 0, 8) < 7).astype(jnp.int32), jax.random.fold_in(key_list[5], 1), 0, 1)
    diffusion_steps = plant(jax.random.randint(key_list[6], (ITEMS,), 0, 1000), jax.random.fold_in(key_list[6], 1), 0, 999).astype(jnp.int32)
    step_proj = noise(key_list[7], (LAYERS, WIDTH, WIDTH), WIDTH ** -0.5, 0.25, ((1, 32),), jnp.float32)
    conv_weight = noise(key_list[8], (LAYERS, 3 * WIDTH, 2 * WIDTH), (3 * WIDTH) ** -0.5, 0.15625, ((1, 32),), jnp.float32)
    cond_proj = noise(key_list[9], (LAYERS, WIDTH, 2 * WIDTH), WIDTH ** -0.5, 0.25, ((1, 32),), jnp.float32)
    out_proj = noise(key_list[10], (LAYERS, WIDTH, 2 * WIDTH), WIDTH ** -0.5, 0.25, ((1, 32),), jnp.float32)
    query_seeds = noise(key_list[11], (LAYERS, WIDTH, QUERIES), 1.0, 6.0, ((1, 32),), jnp.float32)
    query_proj = noise(key_list[12], (LAYERS, WIDTH, WIDTH), WIDTH ** -0.5, 0.25, ((1, 32),), jnp.float32)
    key_proj = noise(key_list[13], (LAYERS, WIDTH, WIDTH), WIDTH ** -0.5, 0.25, ((1, 32),), jnp.float32)
    value_proj = noise(key_list[14], (LAYERS, WIDTH, WIDTH), WIDTH ** -0.5, 0.25, ((1, 32),), jnp.float32)
    mixing_proj = noise(key_list[15], (LAYERS, WIDTH, WIDTH), (WIDTH // 16) ** -0.5, 1.0, ((1, 32),), jnp.float32)
    film_proj = noise(key_list[16], (LAYERS, WIDTH, 2 * WIDTH), (WIDTH // 64) ** -0.5, 2.0, ((1, 32),), jnp.float32)
    cot_frames = noise(key_list[17], (ITEMS, FRAMES, WIDTH), 1.0, 6.0, ((0, 32),), jnp.float32)
    cot_skip = noise(key_list[18], (ITEMS, FRAMES, WIDTH), 1.0, 6.0, ((0, 32),), jnp.float32)
    return {"frames_in": frames_in, "conditioning": conditioning, "prompt": prompt, "item_lengths": item_lengths, "prompt_lengths": prompt_lengths, "key_mask": key_mask, "diffusion_steps": diffusion_steps, "step_proj": step_proj, "conv_weight": conv_weight, "cond_proj": cond_proj, "out_proj": out_proj, "query_seeds": query_seeds, "query_proj": query_proj, "key_proj": key_proj, "value_proj": value_proj, "mixing_proj": mixing_proj, "film_proj": film_proj, "cot_frames": cot_frames, "cot_skip": cot_skip}


@jax.custom_vjp
def low(v):
    return lax.optimization_barrier(v.astype(jnp.bfloat16)).astype(jnp.float32)

@jax.custom_vjp
def low_back(v):
    return v

def low_keep(v):
    return (low(v), None)

def low_pass(kept, grad):
    return (grad,)

def back_keep(v):
    return (v, None)

def back_low(kept, grad):
    return (low(grad),)
low.defvjp(low_keep, low_pass)
low_back.defvjp(back_keep, back_low)
CLIP_NORM = 1.0

def matmul(left, right):
    return jnp.dot(left, right, precision=lax.Precision.HIGHEST)

def step_embedding(diffusion_step):
    half_width = WIDTH // 2
    ramp = jnp.arange(half_width, dtype=jnp.int32).astype(jnp.float32) / (half_width - 1)
    angles = diffusion_step.astype(jnp.float32) / 1000.0 * jnp.exp(ramp * math.log(100.0))
    return jnp.concatenate([jnp.sin(angles), jnp.cos(angles)])

def wavenet_layer(frames, skip_sum, conditioning, prompt, frame_live, key_live, step_embed, params, dilation):
    step_proj, conv_weight, cond_proj, out_proj, query_seeds, query_proj, key_proj, value_proj, mixing_proj, film_proj = params
    frame_count = frames.shape[0]
    head_dim = WIDTH // HEADS
    hidden_in = (frames + matmul(step_embed[None, :], step_proj)) * frame_live[:, None]
    zero_rim = jnp.zeros((dilation, WIDTH), hidden_in.dtype)
    padded = jnp.concatenate([zero_rim, hidden_in, zero_rim], axis=0)
    conv_taps = jnp.concatenate([padded[:frame_count], hidden_in, padded[2 * dilation:]], axis=1)
    pre_gate = matmul(conv_taps, conv_weight) + matmul(conditioning, cond_proj)
    query_rows = matmul(query_seeds.T, query_proj).reshape(-1, HEADS, head_dim)
    key_rows = matmul(prompt, key_proj).reshape(-1, HEADS, head_dim)
    value_rows = matmul(prompt, value_proj).reshape(-1, HEADS, head_dim)
    scores = jnp.einsum('qhe,khe->hqk', query_rows, key_rows, precision=lax.Precision.HIGHEST) / math.sqrt(head_dim)
    scores = jnp.where(key_live[None, None, :], scores, -1e+30)
    top_score = lax.optimization_barrier(jnp.max(scores, axis=2, keepdims=True))
    exp_scores = jnp.exp(scores - top_score)
    attn_probs = exp_scores / lax.optimization_barrier(jnp.sum(exp_scores, axis=2, keepdims=True))
    attended = jnp.einsum('hqk,khe->qhe', attn_probs, value_rows, precision=lax.Precision.HIGHEST).reshape(-1, WIDTH)
    mixed_rows = matmul(attended, mixing_proj)
    film_params = matmul(lax.optimization_barrier(jnp.mean(mixed_rows, axis=0, keepdims=True)), film_proj)[0]
    gate_act = jnp.tanh(pre_gate[:, :WIDTH]) * jax.nn.sigmoid(pre_gate[:, WIDTH:])
    modulated = gate_act * (1.0 + film_params[:WIDTH]) + film_params[WIDTH:]
    post_gate = matmul(modulated, out_proj)
    frames_next = (frames + post_gate[:, :WIDTH]) * frame_live[:, None] * math.sqrt(0.5)
    skip_next = skip_sum + post_gate[:, WIDTH:] * frame_live[:, None]
    return (frames_next, skip_next)

def reference(frames_in, conditioning, prompt, item_lengths, prompt_lengths, key_mask, diffusion_steps, step_proj, conv_weight, cond_proj, out_proj, query_seeds, query_proj, key_proj, value_proj, mixing_proj, film_proj, cot_frames, cot_skip):
    frame_live = (jnp.arange(FRAMES, dtype=jnp.int32)[None, :] < item_lengths[:, None]).astype(jnp.float32)
    key_place = jnp.arange(PROMPT, dtype=jnp.int32)[None, :]
    key_live = (key_place < prompt_lengths[:, None]) & ((key_mask == 1) | (key_place == 0))
    embeds = jax.vmap(step_embedding)(diffusion_steps)
    params = (step_proj, conv_weight, cond_proj, out_proj, query_seeds, query_proj, key_proj, value_proj, mixing_proj, film_proj)

    def whole_forward(frames_start, weights):

        def one_item(inputs):
            frames, cond_item, prompt_item, live_item, keys_item, embed_item = inputs
            skip_sum = jnp.zeros_like(frames)
            for layer_index in range(LAYERS):
                layer_params = tuple((member[layer_index] for member in weights))
                frames, skip_sum = wavenet_layer(frames, skip_sum, cond_item, prompt_item, live_item, keys_item, embed_item, layer_params, 2 ** layer_index)
            return (frames, skip_sum)
        return lax.map(jax.checkpoint(one_item), (frames_start, conditioning, prompt, frame_live, key_live, embeds))
    (frames_out, skip_out), pullback = jax.vjp(whole_forward, frames_in, params)
    grad_frames, grads = pullback((cot_frames, cot_skip))
    norm_square = sum((jnp.sum(member * member) for member in grads))
    clip_factor = jnp.minimum(1.0, CLIP_NORM / jnp.sqrt(norm_square))
    return (frames_out, skip_out, grad_frames, grads[0] * clip_factor, grads[1] * clip_factor, grads[2] * clip_factor, grads[3] * clip_factor, grads[4] * clip_factor, grads[5] * clip_factor, grads[6] * clip_factor, grads[7] * clip_factor, grads[8] * clip_factor, grads[9] * clip_factor)
```

```python
import math

import jax
import jax.numpy as jnp
from jax import lax
from jax.sharding import PartitionSpec as P

WIDTH = 512
GATES = 2 * WIDTH
HEADS = 8
HEAD_DIM = WIDTH // HEADS
QUERIES = 32
LAYERS = 2
CLIP_NORM = 1.0
AXIS = "items"
HIGH = lax.Precision.HIGH
HIGHEST = lax.Precision.HIGHEST
ROOT_HALF = math.sqrt(0.5)


def big_dot(left, right, left_dim=1, right_dim=0):
    return lax.dot_general(left, right, (((left_dim,), (right_dim,)), ((), ())), precision=HIGH)


def small_dot(left, right, left_dim=1, right_dim=0):
    return lax.dot_general(left, right, (((left_dim,), (right_dim,)), ((), ())), precision=HIGHEST)


def step_embedding(diffusion_step):
    half_width = WIDTH // 2
    ramp = jnp.arange(half_width, dtype=jnp.int32).astype(jnp.float32) / (half_width - 1)
    angles = diffusion_step.astype(jnp.float32) / 1000.0 * jnp.exp(ramp * math.log(100.0))
    return jnp.concatenate([jnp.sin(angles), jnp.cos(angles)])


class Ring:
    def __init__(self, count, size, stride):
        self.count, self.size, self.stride = count, size, stride
        self.digit = (lax.axis_index(AXIS) // stride) % size

    def shift(self, block, steps):
        perm = []
        for device in range(self.count):
            digit = (device // self.stride) % self.size
            target = (digit + steps) % self.size
            perm.append((device, device + (target - digit) * self.stride))
        return lax.ppermute(block, AXIS, perm)

    def gather(self, block):
        if self.size == 1:
            return block[None]
        others = [self.shift(block, steps) for steps in range(1, self.size)]
        if self.size == 2:
            first = jnp.where(self.digit == 0, block, others[0])
            second = jnp.where(self.digit == 0, others[0], block)
            return jnp.stack([first, second])
        out = jnp.broadcast_to(block, (self.size,) + block.shape)
        for steps, other in enumerate(others, 1):
            place = (self.digit - steps) % self.size
            out = lax.dynamic_update_index_in_dim(out, other, place, 0)
        return out

    def scatter_sum(self, blocks, dim):
        own = lax.dynamic_index_in_dim(blocks, self.digit, dim, keepdims=False)
        for steps in range(1, self.size):
            place = (self.digit + steps) % self.size
            own = own + self.shift(lax.dynamic_index_in_dim(blocks, place, dim, keepdims=False), steps)
        return own


def rings_of(count):
    bits = (count // 2).bit_length() - 1
    sizes = [2 ** ((bits + 2) // 3), 2 ** ((bits + 1) // 3), 2 ** (bits // 3), 2]
    rings, stride = [], count
    for size in sizes:
        stride //= size
        rings.append(Ring(count, size, stride))
    return rings


def gather_rows(shard, rings):
    far, mid, near, core = rings
    rows, columns = shard.shape
    half = rows // 2
    block = far.gather(shard)
    top = mid.gather(near.gather(block[:, :half]))
    low = near.gather(mid.gather(block[:, half:]))
    top = jnp.transpose(top, (2, 0, 1, 3, 4))
    low = jnp.transpose(low, (2, 1, 0, 3, 4))
    rail = jnp.concatenate([top, low], axis=3)
    both = core.gather(rail)
    return jnp.transpose(both, (1, 2, 3, 0, 4, 5)).reshape(-1, rows, columns)


def pick(terms, place, dim):
    return [lax.dynamic_index_in_dim(term, place, dim, keepdims=False) for term in terms]


def hop(terms, ring, dim):
    stays = pick(terms, ring.digit, dim)
    for steps in range(1, ring.size):
        goes = sum(pick(terms, (ring.digit + steps) % ring.size, dim))
        stays.append(ring.shift(goes, steps))
    return stays


class RowSum:
    def __init__(self, arrays, rings):
        self.rings = rings
        sizes = tuple(ring.size for ring in rings)
        self.state = [[array.reshape(sizes + array.shape[1:])] for array in arrays]

    def core(self):
        self.state = [hop(terms, self.rings[3], 3) for terms in self.state]

    def join(self):
        rows = [jnp.concatenate(parts, axis=3) for parts in zip(*self.state)]
        half = rows[0].shape[3] // 2
        self.state = [[term[:, :, :, :half] for term in rows], [term[:, :, :, half:] for term in rows]]

    def first(self):
        far, mid, near, core = self.rings
        top, low = self.state
        self.state = [hop(top, mid, 1), hop(low, near, 2)]

    def second(self):
        far, mid, near, core = self.rings
        top, low = self.state
        top, low = sum(hop(top, near, 1)), sum(hop(low, mid, 1))
        self.state = [[jnp.concatenate([top, low], axis=1)]]

    def last(self):
        self.state = sum(hop(self.state[0], self.rings[0], 0))


def tie(*groups):
    leaves, tree = jax.tree.flatten(groups)
    return jax.tree.unflatten(tree, lax.optimization_barrier(leaves))


def exchange(*parts):
    devices = parts[0].shape[0]
    parts = [part.reshape(devices, -1) for part in parts]
    sizes = [part.shape[1] for part in parts]
    joined = jnp.concatenate(parts, axis=1)
    joined = jnp.pad(joined, ((0, 0), (0, -joined.shape[1] % 1024))).reshape(devices, -1, 128)
    came = lax.all_to_all(joined, AXIS, split_axis=0, concat_axis=0, tiled=True).reshape(devices, -1)
    out, start = [], 0
    for size in sizes:
        out.append(came[:, start : start + size])
        start += size
    return out


def to_all(part, devices):
    return jnp.broadcast_to(part.reshape(1, -1), (devices, part.size))


def by_column(part, devices):
    cut = part.reshape(part.shape[:-1] + (devices, -1))
    return jnp.moveaxis(cut, -2, 0).reshape(devices, -1)


def head_rows(row):
    head = jnp.arange(WIDTH, dtype=jnp.int32)[None, :] // HEAD_DIM
    own = head == jnp.arange(HEADS, dtype=jnp.int32)[:, None]
    return jnp.where(own, row, 0.0)


def attention_back(weights, keys, probs, grad_film):
    grad_mixed = small_dot(grad_film, weights["film"], 1, 1)
    grad_row = small_dot(grad_mixed / QUERIES, weights["mixing"], 1, 1)
    grad_pooled = small_dot(head_rows(grad_row), weights["value"], 1, 1)
    grad_probs = small_dot(grad_pooled, keys, 1, 1)
    weighted = probs * grad_probs[:, None, :]
    row_terms = jnp.sum(weighted, axis=2, keepdims=True)
    grad_scores = (weighted - probs * row_terms) / math.sqrt(HEAD_DIM)
    grad_scores = grad_scores.reshape(HEADS * QUERIES, -1)
    grad_absorbed = small_dot(keys, grad_scores, 0, 1)
    key_heads = weights["key"].reshape(WIDTH, HEADS, HEAD_DIM)
    grad_query = jnp.einsum(
        "whq,whe->qhe", grad_absorbed.reshape(WIDTH, HEADS, QUERIES), key_heads, precision=HIGHEST
    ).reshape(QUERIES, WIDTH)
    return grad_absorbed, grad_query, grad_row, grad_mixed


def shifted(rows, steps):
    if steps > 0:
        return jnp.concatenate([jnp.zeros_like(rows[:steps]), rows[:-steps]], axis=0)
    return jnp.concatenate([rows[-steps:], jnp.zeros_like(rows[:-steps])], axis=0)


def taps_of(frames, step_row, live, dilation):
    hidden = (frames + step_row) * live
    return jnp.concatenate([shifted(hidden, dilation), hidden, shifted(hidden, -dilation)], axis=1)


def layer_gates(weights, taps, conditioning):
    pre_gate = big_dot(taps, weights["conv"]) + big_dot(conditioning, weights["cond"])
    return jnp.tanh(pre_gate[:, :WIDTH]), jax.nn.sigmoid(pre_gate[:, WIDTH:])


def layer_forward(weights, frames, skip, tanh, sig, live, film):
    modulated = tanh * sig * (1.0 + film[:, :WIDTH]) + film[:, WIDTH:]
    post = big_dot(modulated, weights["out"])
    frames = (frames + post[:, :WIDTH]) * (live * ROOT_HALF)
    skip = skip + post[:, WIDTH:] * live
    return frames, skip, modulated


def layer_back_gates(weights, tanh, sig, modulated, grad_frames, grad_skip, live, film):
    grad_post = jnp.concatenate([grad_frames * (live * ROOT_HALF), grad_skip * live], axis=1)
    grad_mod = big_dot(grad_post, weights["out"], 1, 1)
    grad_gamma = jnp.sum(grad_mod * (tanh * sig), axis=0, keepdims=True)
    grad_beta = jnp.sum(grad_mod, axis=0, keepdims=True)
    grad_gate = grad_mod * (1.0 + film[:, :WIDTH])
    grad_pre = jnp.concatenate(
        [grad_gate * sig * (1.0 - tanh * tanh), grad_gate * tanh * sig * (1.0 - sig)], axis=1
    )
    return grad_post, grad_pre, jnp.concatenate([grad_gamma, grad_beta], axis=1)


def layer_back_frames(weights, grad_pre, grad_frames, live, dilation):
    grad_taps = big_dot(grad_pre, weights["conv"], 1, 1)
    grad_hidden = (
        shifted(grad_taps[:, :WIDTH], -dilation)
        + grad_taps[:, WIDTH : 2 * WIDTH]
        + shifted(grad_taps[:, 2 * WIDTH :], dilation)
    ) * live
    return grad_frames * (live * ROOT_HALF) + grad_hidden, jnp.sum(grad_hidden, axis=0, keepdims=True)


def on_device(
    frames_in,
    conditioning,
    prompt,
    item_lengths,
    prompt_lengths,
    key_mask,
    diffusion_steps,
    step_proj,
    conv_weight,
    cond_proj,
    out_proj,
    query_seeds,
    query_proj,
    key_proj,
    value_proj,
    mixing_proj,
    film_proj,
    cot_frames,
    cot_skip,
    devices,
):
    rings = rings_of(devices)
    share = step_proj.shape[1]
    key_count = prompt.shape[1]
    extra_rows = -(-(key_count + LAYERS * share * QUERIES) // WIDTH)
    key_rows = -(-(key_count + extra_rows) // 8) * 8
    me = lax.axis_index(AXIS)

    frame_packs = [
        jnp.concatenate(
            [conv_weight[layer], cond_proj[layer], out_proj[layer], step_proj[layer].reshape(-1, GATES)], axis=0
        )
        for layer in range(LAYERS)
    ]
    frame_whole_0 = lax.all_gather(frame_packs[0], AXIS, axis=0, tiled=False)

    extra = jnp.concatenate(
        [key_mask.astype(jnp.float32), to_all(query_seeds, prompt.shape[0])], axis=1
    )
    extra = jnp.pad(extra, ((0, 0), (0, (key_rows - key_count) * WIDTH - extra.shape[1])))
    sent = jnp.concatenate([prompt, extra.reshape(prompt.shape[0], -1, WIDTH)], axis=1)
    query_key = jnp.concatenate([query_proj, key_proj], axis=2).reshape(LAYERS * share, GATES)
    query_key, sent = tie(query_key, sent)
    keys = lax.all_to_all(sent, AXIS, split_axis=0, concat_axis=0, tiled=True)
    extra = keys[:, key_count : key_count + extra_rows].reshape(devices, -1)
    key_place = (
        jnp.arange(devices, dtype=jnp.int32)[:, None] * key_count
        + jnp.arange(key_rows, dtype=jnp.int32)[None, :]
    )
    masked_in = jnp.pad(extra[:, :key_count], ((0, 0), (0, key_rows - key_count)))
    live_keys = (
        (jnp.arange(key_rows, dtype=jnp.int32)[None, :] < key_count)
        & (key_place < lax.dynamic_index_in_dim(prompt_lengths, me, 0, keepdims=False))
        & ((masked_in == 1.0) | (key_place == 0))
    ).reshape(-1)
    seeds = extra[:, key_count : key_count + LAYERS * share * QUERIES]
    seeds = jnp.moveaxis(seeds.reshape(devices, LAYERS, share, QUERIES), 1, 0)
    seeds = seeds.reshape(LAYERS, WIDTH, QUERIES)
    keys = keys.reshape(-1, WIDTH)

    query_key = gather_rows(query_key, rings).reshape(devices, LAYERS, share, GATES)
    query_key = jnp.moveaxis(query_key, 1, 0).reshape(LAYERS, WIDTH, GATES)
    query_rows = jnp.einsum("lwq,lwx->lqx", seeds, query_key[:, :, :WIDTH], precision=HIGHEST)
    query_heads = query_rows.reshape(LAYERS, QUERIES, HEADS, HEAD_DIM)
    key_heads = query_key[:, :, WIDTH:].reshape(LAYERS, WIDTH, HEADS, HEAD_DIM)
    absorbed = jnp.einsum("lqhe,lwhe->lhqw", query_heads, key_heads, precision=HIGHEST)
    absorbed = absorbed.reshape(LAYERS * HEADS * QUERIES, WIDTH) / math.sqrt(HEAD_DIM)

    scores = jnp.where(live_keys[None, :], small_dot(absorbed, keys, 1, 1), -1e30)
    exps = jnp.exp(scores - jnp.max(scores, axis=1, keepdims=True))
    probs = exps / jnp.sum(exps, axis=1, keepdims=True)
    probs = probs.reshape(LAYERS, HEADS, QUERIES, -1)
    pooled = jnp.mean(probs, axis=2).reshape(LAYERS * HEADS, -1)
    pooled_keys = small_dot(pooled, keys)

    frame_pack_1, frame_whole_0, pooled_keys = tie(frame_packs[1], frame_whole_0, pooled_keys)
    frame_whole_1 = lax.all_gather(frame_pack_1, AXIS, axis=0, tiled=False)

    (pooled_cut,) = exchange(by_column(pooled_keys, devices))
    pooled_cut = pooled_cut.reshape(devices, LAYERS, HEADS, share)
    value_heads = value_proj.reshape(LAYERS, share, HEADS, HEAD_DIM)
    mean_part = jnp.einsum("blhw,lwhe->blhe", pooled_cut, value_heads, precision=HIGHEST)
    (mean_cut,) = exchange(by_column(mean_part.reshape(devices, LAYERS, WIDTH), devices))
    mean_cut = jnp.sum(mean_cut, axis=0).reshape(devices, LAYERS, share)
    mixed_part = jnp.einsum("blw,lwx->blx", mean_cut, mixing_proj, precision=HIGHEST)
    (mixed_cut,) = exchange(by_column(mixed_part, devices))
    mixed_cut = jnp.sum(mixed_cut, axis=0).reshape(devices, LAYERS, share)
    film_part = jnp.einsum("blw,lwx->blx", mixed_cut, film_proj, precision=HIGHEST)
    (films,) = exchange(film_part)
    films = jnp.sum(films, axis=0).reshape(LAYERS, 1, GATES)

    attention_pack = jnp.concatenate(
        [
            part
            for layer in range(LAYERS)
            for part in (film_proj[layer], jnp.concatenate([value_proj[layer], mixing_proj[layer]], axis=1))
        ],
        axis=0,
    )
    attention_pack, frame_whole_1 = tie(attention_pack, frame_whole_1)
    weights = []
    for whole in (frame_whole_0, frame_whole_1):
        weights.append(
            {
                "conv": whole[:, : 3 * share].reshape(-1, GATES),
                "cond": whole[:, 3 * share : 4 * share].reshape(-1, GATES),
                "out": whole[:, 4 * share : 5 * share].reshape(-1, GATES),
                "step": whole[:, 5 * share :].reshape(-1, WIDTH),
            }
        )
    attention_whole = lax.all_gather(attention_pack, AXIS, axis=0, tiled=False)
    attention_whole = attention_whole.reshape(devices, LAYERS, -1, GATES)
    for layer in range(LAYERS):
        value_mixing = attention_whole[:, layer, share:]
        weights[layer]["film"] = attention_whole[:, layer, :share].reshape(-1, GATES)
        weights[layer]["value"] = value_mixing[:, :, :WIDTH].reshape(-1, WIDTH)
        weights[layer]["mixing"] = value_mixing[:, :, WIDTH:].reshape(-1, WIDTH)
        weights[layer]["key"] = query_key[layer, :, WIDTH:]

    live = (jnp.arange(frames_in.shape[1], dtype=jnp.int32) < item_lengths[0]).astype(jnp.float32)[:, None]
    embed = step_embedding(diffusion_steps[0])[None, :]
    frames, skip = frames_in[0], jnp.zeros_like(frames_in[0])
    kept = []
    for layer in range(LAYERS):
        step_row = small_dot(embed, weights[layer]["step"])
        taps = taps_of(frames, step_row, live, 2**layer)
        tanh, sig = layer_gates(weights[layer], taps, conditioning[0])
        frames, skip, modulated = layer_forward(weights[layer], frames, skip, tanh, sig, live, films[layer])
        kept.append((taps, tanh, sig, modulated))

    def by_device(grad):
        return grad.reshape(devices, -1, GATES)

    taps, tanh, sig, modulated = kept[1]
    grad_post, grad_pre_1, grad_film_1 = layer_back_gates(
        weights[1], tanh, sig, modulated, cot_frames[0], cot_skip[0], live, films[1]
    )
    grad_out = big_dot(modulated, grad_post, 0, 0)
    grad_cond = big_dot(conditioning[0], grad_pre_1, 0, 0)
    grad_conv = big_dot(taps, grad_pre_1, 0, 0)
    sum_1 = RowSum([by_device(grad_conv), by_device(grad_cond), by_device(grad_out)], rings)
    sum_1.core()
    grad_frames, step_sum_1 = layer_back_frames(weights[1], grad_pre_1, cot_frames[0], live, 2)
    sum_1.join()
    sum_1.first()

    taps, tanh, sig, modulated = kept[0]
    grad_post, grad_pre_0, grad_film_0 = layer_back_gates(
        weights[0], tanh, sig, modulated, grad_frames, cot_skip[0], live, films[0]
    )
    absorbed_1, query_1, row_1, mixed_1 = attention_back(weights[1], keys, probs[1], grad_film_1)
    grad_out = big_dot(modulated, grad_post, 0, 0)
    grad_cond = big_dot(conditioning[0], grad_pre_0, 0, 0)
    absorbed_0, query_0, row_0, mixed_0 = attention_back(weights[0], keys, probs[0], grad_film_0)
    absorbed_0, absorbed_1, taps, sum_1.state = tie(absorbed_0, absorbed_1, taps, sum_1.state)
    sum_1.second()
    grad_conv = big_dot(taps, grad_pre_0, 0, 0)
    sum_1.last()
    absorbed_grad = jnp.concatenate([absorbed_0, absorbed_1], axis=1)
    sum_0 = RowSum([by_device(grad) for grad in (grad_conv, grad_cond, grad_out, absorbed_grad)], rings)
    sum_0.core()
    sum_0.join()
    sum_0.first()
    grad_frames, step_sum_0 = layer_back_frames(weights[0], grad_pre_0, grad_frames, live, 1)
    sum_0.second()
    (query_cut,) = exchange(by_column(jnp.stack([query_0, query_1]), devices))
    query_cut = jnp.sum(query_cut, axis=0)
    sum_0.last()
    whole_rows = (row_0, row_1, mixed_0, mixed_1, grad_film_0, grad_film_1, step_sum_0, step_sum_1, query_cut)
    row_0, row_1, mixed_0, mixed_1, grad_film_0, grad_film_1, step_sum_0, step_sum_1, query_cuts, own_embeds = exchange(
        *(to_all(part, devices) for part in whole_rows), by_column(embed, devices)
    )
    query_grads = jnp.moveaxis(query_cuts.reshape(devices, LAYERS, QUERIES, share), 0, 2)
    query_grads = query_grads.reshape(LAYERS, QUERIES, WIDTH)
    absorbed_sums = jnp.moveaxis(sum_0.state[5 * share :].reshape(share, LAYERS, HEADS, QUERIES), 1, 0)

    frame_sums = [sum_0.state, sum_1.state]
    conv_grad = jnp.stack([sums[: 3 * share] for sums in frame_sums])
    cond_grad = jnp.stack([sums[3 * share : 4 * share] for sums in frame_sums])
    out_grad = jnp.stack([sums[4 * share : 5 * share] for sums in frame_sums])
    step_grad = jnp.einsum("bw,lbx->lwx", own_embeds, jnp.stack([step_sum_0, step_sum_1]), precision=HIGHEST)
    seeds_grad = jnp.einsum("lwx,lqx->lwq", query_proj, query_grads, precision=HIGHEST)
    query_grad = jnp.einsum("lwq,lqx->lwx", query_seeds, query_grads, precision=HIGHEST)
    key_grad = jnp.einsum("lwhq,lqhe->lwhe", absorbed_sums, query_heads, precision=HIGHEST)
    rows = jnp.stack([row_0, row_1]).reshape(LAYERS, devices, HEADS, HEAD_DIM)
    value_grad = QUERIES * jnp.einsum("blhw,lbhe->lwhe", pooled_cut, rows, precision=HIGHEST)
    mixing_grad = jnp.einsum("blw,lbx->lwx", mean_cut, jnp.stack([mixed_0, mixed_1]), precision=HIGHEST)
    film_grad = jnp.einsum(
        "blw,lbx->lwx", mixed_cut, jnp.stack([grad_film_0, grad_film_1]), precision=HIGHEST
    )
    grads = (
        step_grad,
        conv_grad,
        cond_grad,
        out_grad,
        seeds_grad,
        query_grad,
        key_grad.reshape(LAYERS, share, WIDTH),
        value_grad.reshape(LAYERS, share, WIDTH),
        mixing_grad,
        film_grad,
    )
    local_square = sum(jnp.sum(grad * grad) for grad in grads)
    squares = lax.all_to_all(
        jnp.full((devices, 8, 128), local_square), AXIS, split_axis=0, concat_axis=0, tiled=True
    )
    norm_square = jnp.sum(squares[:, 0, 0])
    clip_factor = jnp.minimum(1.0, CLIP_NORM / jnp.sqrt(norm_square))
    return (frames[None], skip[None], grad_frames[None]) + tuple(grad * clip_factor for grad in grads)


def solution(mesh):
    devices = mesh.shape[AXIS]

    def run(*args):
        return on_device(*args, devices=devices)

    items, rows = P(AXIS, None, None), P(None, AXIS, None)
    return jax.shard_map(
        run,
        mesh=mesh,
        in_specs=(items, items, rows, P(AXIS), P(), P(None, AXIS), P(AXIS)) + (rows,) * 10 + (items, items),
        out_specs=(items,) * 3 + (rows,) * 10,
        check_vma=False,
    )
```

```python
import functools
import math

import jax
import jax.numpy as jnp
from jax import lax
from jax.experimental import pallas as pl
from jax.experimental.pallas import tpu as pltpu
from jax.sharding import PartitionSpec as P

WIDTH = 512
GATES = 2 * WIDTH
HEADS = 8
HEAD_DIM = WIDTH // HEADS
QUERIES = 32
LAYERS = 2
CLIP_NORM = 1.0
AXIS = "items"
HIGH = lax.Precision.HIGH
HIGHEST = lax.Precision.HIGHEST
ROOT_HALF = math.sqrt(0.5)


def big_dot(left, right, left_dim=1, right_dim=0):
    return lax.dot_general(left, right, (((left_dim,), (right_dim,)), ((), ())), precision=HIGH)


def small_dot(left, right, left_dim=1, right_dim=0):
    return lax.dot_general(left, right, (((left_dim,), (right_dim,)), ((), ())), precision=HIGHEST)


def step_embedding(diffusion_step):
    half_width = WIDTH // 2
    ramp = jnp.arange(half_width, dtype=jnp.int32).astype(jnp.float32) / (half_width - 1)
    angles = diffusion_step.astype(jnp.float32) / 1000.0 * jnp.exp(ramp * math.log(100.0))
    return jnp.concatenate([jnp.sin(angles), jnp.cos(angles)])


class Ring:
    def __init__(self, count, size, stride):
        self.count, self.size, self.stride = count, size, stride
        self.digit = (lax.axis_index(AXIS) // stride) % size

    def shift(self, block, steps):
        perm = []
        for device in range(self.count):
            digit = (device // self.stride) % self.size
            target = (digit + steps) % self.size
            perm.append((device, device + (target - digit) * self.stride))
        return lax.ppermute(block, AXIS, perm)

    def gather(self, block):
        if self.size == 1:
            return block[None]
        others = [self.shift(block, steps) for steps in range(1, self.size)]
        if self.size == 2:
            first = jnp.where(self.digit == 0, block, others[0])
            second = jnp.where(self.digit == 0, others[0], block)
            return jnp.stack([first, second])
        out = jnp.broadcast_to(block, (self.size,) + block.shape)
        for steps, other in enumerate(others, 1):
            place = (self.digit - steps) % self.size
            out = lax.dynamic_update_index_in_dim(out, other, place, 0)
        return out

    def scatter_sum(self, blocks, dim):
        own = lax.dynamic_index_in_dim(blocks, self.digit, dim, keepdims=False)
        for steps in range(1, self.size):
            place = (self.digit + steps) % self.size
            own = own + self.shift(lax.dynamic_index_in_dim(blocks, place, dim, keepdims=False), steps)
        return own


def rings_of(count):
    bits = (count // 2).bit_length() - 1
    sizes = [2 ** ((bits + 2) // 3), 2 ** ((bits + 1) // 3), 2 ** (bits // 3), 2]
    rings, stride = [], count
    for size in sizes:
        stride //= size
        rings.append(Ring(count, size, stride))
    return rings


def pairs_of(count):
    return [Ring(count, 2, 2**bit) for bit in reversed(range(count.bit_length() - 1))]


def gather_rows(shard, rings):
    far, mid, near, core = rings
    rows, columns = shard.shape
    half = rows // 2
    block = far.gather(shard)
    top = mid.gather(near.gather(block[:, :half]))
    low = near.gather(mid.gather(block[:, half:]))
    top = jnp.transpose(top, (2, 0, 1, 3, 4))
    low = jnp.transpose(low, (2, 1, 0, 3, 4))
    rail = jnp.concatenate([top, low], axis=3)
    both = core.gather(rail)
    return jnp.transpose(both, (1, 2, 3, 0, 4, 5)).reshape(-1, rows, columns)


def hop(terms, ring, dim, gates=()):
    def pick(place):
        return [lax.dynamic_index_in_dim(term, place, dim, keepdims=False) for term in terms]

    goes, gates = tie(sum(pick(1 - ring.digit)), gates) if gates else (sum(pick(1 - ring.digit)), gates)
    return pick(ring.digit) + [ring.shift(goes, 1)], gates


class RowSum:
    def __init__(self, arrays, pairs, far_first=False):
        count = len(pairs)
        self.pairs, self.at, bits = pairs, 0, list(range(count))
        self.orders = []
        for k in range(len(arrays)):
            near = bits[-3:-1] if k % 2 == 0 else bits[-3:-1][::-1]
            far = bits[:-3][::-1]
            self.orders.append(bits[-1:] + (far + near if far_first else near + far))
        self.left = [list(bits) for _ in arrays]
        self.state = [[array.reshape((2,) * count + array.shape[1:])] for array in arrays]

    def add(self, other):
        self.state, self.orders, self.left = (
            self.state + other.state,
            self.orders + other.orders,
            self.left + other.left,
        )

    def join(self):
        parts = self.state if self.at == 1 else [[sum(terms)] for terms in self.state]
        axis = parts[0][0].ndim - 2
        self.state = [[jnp.concatenate(terms, axis=axis) for terms in zip(*parts)]]

    def halve(self):
        (terms,) = self.state
        half = terms[0].shape[-2] // 2
        self.state = [[term[..., :half, :] for term in terms], [term[..., half:, :] for term in terms]]

    def step(self, *gates):
        for k, terms in enumerate(self.state):
            bit = self.orders[k][self.at]
            if self.at >= 3:
                terms = [sum(terms)]
            self.state[k], gates = hop(terms, self.pairs[bit], self.left[k].index(bit), gates)
            self.left[k].remove(bit)
        self.at += 1
        return gates

    def result(self):
        while self.at < len(self.pairs):
            self.step()
        (terms,) = self.state
        return sum(terms)


def beside(sums, work, *inputs):
    for rows in sums:
        inputs = rows.step(*inputs)
    out = work(*inputs)
    came, out = tie([[terms[-1] for terms in rows.state] for rows in sums], out)
    for rows, last in zip(sums, came):
        rows.state = [terms[:-1] + [term] for terms, term in zip(rows.state, last)]
    return out


def tie(*groups):
    leaves, tree = jax.tree.flatten(groups)
    return jax.tree.unflatten(tree, lax.optimization_barrier(leaves))


def exchange(*parts):
    devices = parts[0].shape[0]
    parts = [part.reshape(devices, -1) for part in parts]
    sizes = [part.shape[1] for part in parts]
    joined = jnp.concatenate(parts, axis=1)
    joined = jnp.pad(joined, ((0, 0), (0, -joined.shape[1] % 1024))).reshape(devices, -1, 128)
    came = lax.all_to_all(joined, AXIS, split_axis=0, concat_axis=0, tiled=True).reshape(devices, -1)
    out, start = [], 0
    for size in sizes:
        out.append(came[:, start : start + size])
        start += size
    return out


def to_all(part, devices):
    return jnp.broadcast_to(part.reshape(1, -1), (devices, part.size))


def regrouped(whole, share):
    sizes, start, pieces = (3 * share, share, share, share // 2), 0, []
    for size in sizes:
        pieces.append(whole[:, start : start + size].reshape(PARTS, -1, GATES))
        start += size
    return jnp.concatenate(pieces, axis=1)


def by_column(part, devices):
    cut = part.reshape(part.shape[:-1] + (devices, -1))
    return jnp.moveaxis(cut, -2, 0).reshape(devices, -1)


def head_rows(row):
    head = jnp.arange(WIDTH, dtype=jnp.int32)[None, :] // HEAD_DIM
    own = head == jnp.arange(HEADS, dtype=jnp.int32)[:, None]
    return jnp.where(own, row, 0.0)


def exact_dot(left, right, left_dim=1, right_dim=0):
    return lax.dot_general(
        left, right, (((left_dim,), (right_dim,)), ((), ())), precision=HIGHEST, preferred_element_type=jnp.float32
    )


def head_of(shape, dim, per_head):
    return lax.broadcasted_iota(jnp.int32, shape, dim) // per_head


def attention_back_kernel(
    grad_film, film_w, value_mixing, key_w, probs, keys, absorbed_out, query_out, row_out, mixed_out
):
    film = film_w[...].reshape(WIDTH, GATES)
    value = value_mixing[..., :WIDTH].reshape(WIDTH, WIDTH)
    mixing = value_mixing[..., WIDTH:].reshape(WIDTH, WIDTH)
    grad_mixed = exact_dot(jnp.broadcast_to(grad_film[...], (8, GATES)), film, 1, 1)
    grad_row = exact_dot(grad_mixed * (1.0 / QUERIES), mixing, 1, 1)
    mixed_out[...] = grad_mixed[:1]
    row_out[...] = grad_row[:1]
    own = head_of((HEADS, WIDTH), 1, HEAD_DIM) == head_of((HEADS, WIDTH), 0, 1)
    grad_pooled = exact_dot(jnp.where(own, grad_row, 0.0), value, 1, 1)
    grad_probs = exact_dot(grad_pooled, keys[...], 1, 1)
    prob = probs[0]
    weighted = prob * grad_probs[:, None, :]
    row_terms = jnp.sum(weighted, axis=2, keepdims=True)
    grad_scores = (weighted - prob * row_terms) * (1.0 / math.sqrt(HEAD_DIM))
    grad_scores = grad_scores.reshape(HEADS * QUERIES, -1)
    grad_absorbed = exact_dot(grad_scores, keys[...])
    absorbed_out[...] = grad_absorbed.T
    grad_query = exact_dot(grad_absorbed, key_w[0])
    shape = grad_query.shape
    grad_query = jnp.where(head_of(shape, 1, HEAD_DIM) == head_of(shape, 0, QUERIES), grad_query, 0.0)
    query_out[...] = jnp.sum(grad_query.reshape(HEADS, QUERIES, WIDTH), axis=0)


def attention_back(layer, grad_film, attention_whole, key_w, probs, keys):
    parts, _, _, rows, _ = attention_whole.shape
    count = keys.shape[0]

    def one(shape):
        return pl.BlockSpec((1,) + shape, lambda k: (layer,) + (0,) * len(shape))

    return kernel_call(
        attention_back_kernel,
        (1,),
        [
            fixed(1, GATES),
            pl.BlockSpec((parts, 1, 1, rows, GATES), lambda k: (0, layer, 0, 0, 0)),
            pl.BlockSpec((parts, 1, 1, rows, GATES), lambda k: (0, layer, 1, 0, 0)),
            one((WIDTH, WIDTH)),
            one((HEADS, QUERIES, count)),
            fixed(count, WIDTH),
        ],
        [fixed(WIDTH, HEADS * QUERIES), fixed(QUERIES, WIDTH), fixed(1, WIDTH), fixed(1, WIDTH)],
        [(WIDTH, HEADS * QUERIES), (QUERIES, WIDTH), (1, WIDTH), (1, WIDTH)],
        [],
        10 * WIDTH * HEADS * QUERIES * count // 4,
    )(grad_film, attention_whole, attention_whole, key_w, probs, keys)


def factor_kernel(
    rows, pooled, means, mixeds, embeds, absorbed, query_rows, seeds, query_w,
    step_out, seeds_out, query_out, key_out, value_out, mixing_out, film_out, square_out,
):
    share = embeds.shape[1]
    at = {}
    start = 0
    for name, size in (("row", WIDTH), ("mixed", WIDTH), ("film", GATES), ("step", WIDTH)):
        for layer in range(LAYERS):
            at[name, layer] = rows[:, start : start + size]
            start += size
    square = jnp.zeros((1, 1), jnp.float32)
    own = head_of((HEADS, share, WIDTH), 2, HEAD_DIM) == head_of((HEADS, share, WIDTH), 0, 1)
    near = head_of((HEADS * QUERIES, WIDTH), 1, HEAD_DIM) == head_of((HEADS * QUERIES, WIDTH), 0, QUERIES)
    for layer in range(LAYERS):
        value = exact_dot(pooled[layer], at["row", layer], 0, 0).reshape(HEADS, share, WIDTH)
        spread = jnp.where(near, jnp.concatenate([query_rows[0, layer]] * HEADS, axis=0), 0.0)
        grads = (
            (step_out, exact_dot(embeds[...], at["step", layer], 0, 0)),
            (seeds_out, exact_dot(query_w[layer], query_rows[1, layer], 1, 1)),
            (query_out, exact_dot(seeds[layer], query_rows[1, layer])),
            (key_out, exact_dot(absorbed[layer], spread)),
            (value_out, QUERIES * jnp.sum(jnp.where(own, value, 0.0), axis=0)),
            (mixing_out, exact_dot(means[layer], at["mixed", layer], 0, 0)),
            (film_out, exact_dot(mixeds[layer], at["film", layer], 0, 0)),
        )
        for out, grad in grads:
            out[layer] = grad
            square = square + jnp.sum(jnp.sum(grad * grad, axis=1, keepdims=True), axis=0, keepdims=True)
    square_out[...] = square


def square_kernel(square, *refs):
    *sums, out = refs
    total = square[...]
    for part in sums:
        total = total + jnp.sum(jnp.sum(part[...] * part[...], axis=1, keepdims=True), axis=0, keepdims=True)
    out[...] = jnp.broadcast_to(total[None], out.shape)


def clip_kernel(squares, sums_0, sums_1, *refs):
    places = squares[:, 0, :1]
    norm_square = jnp.sum(places, axis=0, keepdims=True)
    factor = jnp.minimum(1.0, CLIP_NORM / jnp.sqrt(norm_square))
    count = (len(refs) - 3) // 2
    grads, outs = refs[:count], refs[count : 2 * count]
    conv_out, cond_out, out_out = refs[2 * count :]
    for grad, out in zip(grads, outs):
        for layer in range(LAYERS):
            out[layer] = grad[layer] * factor
    share = cond_out.shape[1]
    for layer, sums in enumerate((sums_0, sums_1)):
        conv_out[layer] = sums[: 3 * share] * factor
        cond_out[layer] = sums[3 * share : 4 * share] * factor
        out_out[layer] = sums[4 * share :] * factor


def shapes_of(*shapes):
    return [jax.ShapeDtypeStruct(shape, jnp.float32) for shape in shapes]


HALF = jnp.bfloat16
PARTS = 32
CONV_ROWS, PART_ROWS, STEP_ROWS = 3 * WIDTH // PARTS, WIDTH // PARTS, WIDTH // PARTS // 2
TILE = 256


def halves_of(array):
    high = array.astype(HALF)
    return high, (array - high.astype(jnp.float32)).astype(HALF)


def three_dots(left, right, left_dim, right_dim):
    def dot(one, other):
        dims = (((left_dim,), (right_dim,)), ((), ()))
        return lax.dot_general(one, other, dims, preferred_element_type=jnp.float32)

    return dot(left[0], right[0]) + (dot(left[0], right[1]) + dot(left[1], right[0]))


def tile_of(pair, start, dim, size=TILE):
    return tuple(lax.slice_in_dim(half, start, start + size, axis=dim) for half in pair)


def moved(rows, steps):
    count = rows.shape[0]
    place = lax.broadcasted_iota(jnp.int32, rows.shape, 0) - steps
    return jnp.where((place >= 0) & (place < count), pltpu.roll(rows, steps % count, 0), 0.0)


def kernel_call(kernel, grid, in_specs, out_specs, out_shapes, scratch, macs):
    return pl.pallas_call(
        kernel,
        grid=grid,
        in_specs=in_specs,
        out_specs=out_specs,
        out_shape=[jax.ShapeDtypeStruct(shape, jnp.float32) for shape in out_shapes],
        scratch_shapes=scratch,
        compiler_params=pltpu.CompilerParams(vmem_limit_bytes=60 * 2**20),
        cost_estimate=pl.CostEstimate(flops=6 * macs, bytes_accessed=16 * 2**20, transcendentals=0),
    )


def fixed(*shape):
    return pl.BlockSpec(shape, lambda k: (0,) * len(shape))


def part_rows(size, at):
    return pl.BlockSpec((PARTS, size, GATES), lambda k: (0, at, 0))


CONV_SPEC = pl.BlockSpec((PARTS // 2, CONV_ROWS, GATES), lambda k: (jnp.minimum(k, 1), 0, 0))
COND_SPEC = part_rows(PART_ROWS, 3)
OUT_SPEC = part_rows(PART_ROWS, 4)


def gates_kernel(dilation, frames, cond, conv_w, cond_w, step_w, embed, live, tanh, sig, step_row, total):
    k = pl.program_id(0)

    @pl.when(k == 0)
    def _():
        pairs = step_w[...].reshape(-1, GATES)
        row = exact_dot(jnp.broadcast_to(embed[:1], (8, embed.shape[1])), pairs[:, :WIDTH])
        row = row + exact_dot(jnp.broadcast_to(embed[1:], (8, embed.shape[1])), pairs[:, WIDTH:])
        step_row[...] = row[:1]

    def add(left, right, first):
        for start in range(0, GATES, TILE):
            part = three_dots(left, tile_of(right, start, 1), 1, 0)
            total[:, start : start + TILE] = part if first else total[:, start : start + TILE] + part

    @pl.when(k == 0)
    def _():
        hidden = (frames[...] + step_row[...]) * live[...]
        taps = jnp.concatenate([moved(hidden, dilation), hidden[:, : WIDTH // 2]], axis=1)
        add(halves_of(taps), halves_of(conv_w[...].reshape(-1, GATES)), True)

    @pl.when(k == 1)
    def _():
        hidden = (frames[...] + step_row[...]) * live[...]
        taps = jnp.concatenate([hidden[:, WIDTH // 2 :], moved(hidden, -dilation)], axis=1)
        add(halves_of(taps), halves_of(conv_w[...].reshape(-1, GATES)), False)

    @pl.when(k == 2)
    def _():
        left, right = halves_of(cond[...]), halves_of(cond_w[...].reshape(-1, GATES))
        for start in range(0, WIDTH, TILE):
            part = three_dots(left, tile_of(right, start, 1), 1, 0)
            tanh[:, start : start + TILE] = jnp.tanh(total[:, start : start + TILE] + part)
        for start in range(0, WIDTH, TILE):
            part = three_dots(left, tile_of(right, WIDTH + start, 1), 1, 0)
            sig[:, start : start + TILE] = jax.nn.sigmoid(total[:, WIDTH + start : WIDTH + start + TILE] + part)


def layer_gates(whole, frames, cond, embed, live, dilation):
    count = frames.shape[0]
    return kernel_call(
        functools.partial(gates_kernel, dilation),
        (3,),
        [fixed(count, WIDTH)] * 2
        + [CONV_SPEC, COND_SPEC, part_rows(STEP_ROWS, 10), fixed(2, WIDTH // 2), fixed(count, 1)],
        [fixed(count, WIDTH)] * 2 + [fixed(1, WIDTH)],
        [(count, WIDTH)] * 2 + [(1, WIDTH)],
        [pltpu.VMEM((count, GATES), jnp.float32)],
        4 * count * WIDTH * GATES,
    )(frames, cond, whole, whole, whole, embed, live)


def post_kernel(tanh, sig, film, out_w, frames, skip, live, frames_next, skip_next, high, low):
    @pl.when(pl.program_id(0) == 0)
    def _():
        high[...], low[...] = halves_of(out_w[...].reshape(-1, GATES))

    modulated = halves_of(tanh[...] * sig[...] * (1.0 + film[:1]) + film[1:])
    for start in range(0, WIDTH, TILE):
        cut = slice(start, start + TILE)
        post = three_dots(modulated, (high[:, cut], low[:, cut]), 1, 0)
        frames_next[:, cut] = (frames[:, cut] + post) * (live[...] * ROOT_HALF)
    for start in range(0, WIDTH, TILE):
        cut, far = slice(start, start + TILE), slice(WIDTH + start, WIDTH + start + TILE)
        post = three_dots(modulated, (high[:, far], low[:, far]), 1, 0)
        skip_next[:, cut] = skip[:, cut] + post * live[...]


def layer_post(whole, tanh, sig, film, frames, skip, live):
    count = frames.shape[0]
    rows = pl.BlockSpec((count // 2, WIDTH), lambda k: (k, 0))
    return kernel_call(
        post_kernel,
        (2,),
        [rows, rows, fixed(2, WIDTH), OUT_SPEC, rows, rows, pl.BlockSpec((count // 2, 1), lambda k: (k, 0))],
        [rows, rows],
        [(count, WIDTH)] * 2,
        [pltpu.VMEM((WIDTH, GATES), HALF)] * 2,
        count * WIDTH * GATES,
    )(tanh, sig, film.reshape(2, WIDTH), whole, frames, skip, live)


def back_gates_kernel(grad_frames, grad_skip, live, tanh, sig, film, out_w, grad_pre, grad_film, grad_out, high, low):
    k = pl.program_id(0)

    @pl.when(k == 0)
    def _():
        high[...], low[...] = halves_of(out_w[...].reshape(-1, GATES))
        grad_film[...] = jnp.zeros_like(grad_film)

    post = jnp.concatenate([grad_frames[...] * (live[...] * ROOT_HALF), grad_skip[...] * live[...]], axis=1)
    post = halves_of(post)
    for start in range(0, WIDTH, TILE):
        cut, far = slice(start, start + TILE), slice(WIDTH + start, WIDTH + start + TILE)
        grad_mod = three_dots(post, (high[cut, :], low[cut, :]), 1, 1)
        t, s = tanh[:, cut], sig[:, cut]
        gate = t * s
        grad_film[0:1, cut] += jnp.sum(grad_mod * gate, axis=0, keepdims=True)
        grad_film[1:2, cut] += jnp.sum(grad_mod, axis=0, keepdims=True)
        grad_gate = grad_mod * (1.0 + film[:1, cut])
        grad_pre[:, cut] = grad_gate * (s * (1.0 - t * t))
        grad_pre[:, far] = grad_gate * (gate * (1.0 - s))
    modulated = tanh[...] * sig[...] * (1.0 + film[:1]) + film[1:]
    modulated = halves_of(modulated.T)

    @pl.when(k == 0)
    def _():
        for start in range(0, GATES, TILE):
            grad_out[:, start : start + TILE] = three_dots(modulated, tile_of(post, start, 1), 1, 0)

    @pl.when(k > 0)
    def _():
        for start in range(0, GATES, TILE):
            grad_out[:, start : start + TILE] += three_dots(modulated, tile_of(post, start, 1), 1, 0)


def layer_back_gates(whole, tanh, sig, film, grad_frames, grad_skip, live):
    count = tanh.shape[0]
    rows = pl.BlockSpec((count // 2, WIDTH), lambda k: (k, 0))
    return kernel_call(
        back_gates_kernel,
        (2,),
        [rows, rows, pl.BlockSpec((count // 2, 1), lambda k: (k, 0)), rows, rows, fixed(2, WIDTH), OUT_SPEC],
        [pl.BlockSpec((count // 2, GATES), lambda k: (k, 0)), fixed(2, WIDTH), fixed(WIDTH, GATES)],
        [(count, GATES), (2, WIDTH), (WIDTH, GATES)],
        [pltpu.VMEM((WIDTH, GATES), HALF)] * 2,
        2 * count * WIDTH * GATES,
    )(grad_frames, grad_skip, live, tanh, sig, film.reshape(2, WIDTH), whole)


def back_weights_kernel(dilation, frames, cond, step_row, live, grad_pre, grad_conv, grad_cond, high, low):
    @pl.when(pl.program_id(0) == 0)
    def _():
        hidden = ((frames[...] + step_row[...]) * live[...]).T
        count = hidden.shape[1]
        for tap, steps in enumerate((dilation, 0, -dilation)):
            moved_rows = hidden
            if steps:
                place = lax.broadcasted_iota(jnp.int32, hidden.shape, 1) - steps
                moved_rows = pltpu.roll(hidden, steps % count, 1)
                moved_rows = jnp.where((place >= 0) & (place < count), moved_rows, 0.0)
            cut = slice(tap * WIDTH, (tap + 1) * WIDTH)
            high[cut, :], low[cut, :] = halves_of(moved_rows)
        cut = slice(3 * WIDTH, 4 * WIDTH)
        high[cut, :], low[cut, :] = halves_of(cond[...].T)

    grad = halves_of(grad_pre[...])
    for start in range(0, 4 * WIDTH, 2 * TILE):
        cut = slice(start, start + 2 * TILE)
        part = three_dots((high[cut, :], low[cut, :]), grad, 1, 0)
        if start < 3 * WIDTH:
            grad_conv[cut, :] = part
        else:
            grad_cond[start - 3 * WIDTH : start - 3 * WIDTH + 2 * TILE, :] = part


def layer_back_weights(frames, cond, step_row, live, grad_pre, dilation):
    count = frames.shape[0]
    return kernel_call(
        functools.partial(back_weights_kernel, dilation),
        (GATES // TILE,),
        [fixed(count, WIDTH)] * 2
        + [fixed(1, WIDTH), fixed(count, 1), pl.BlockSpec((count, TILE), lambda k: (0, k))],
        [pl.BlockSpec((3 * WIDTH, TILE), lambda k: (0, k)), pl.BlockSpec((WIDTH, TILE), lambda k: (0, k))],
        [(3 * WIDTH, GATES), (WIDTH, GATES)],
        [pltpu.VMEM((4 * WIDTH, count), HALF)] * 2,
        4 * count * WIDTH * GATES,
    )(frames, cond, step_row, live, grad_pre)


def back_frames_kernel(dilation, grad_pre, conv_w, grad_frames, live, grad_next, step_sum, high, low, total):
    k = pl.program_id(0)
    middle = WIDTH // 2

    @pl.when(k == 0)
    def _():
        high[...], low[...] = halves_of(grad_pre[...])

    grad, weight = (high[...], low[...]), halves_of(conv_w[...].reshape(-1, GATES))

    def taps(start):
        return three_dots(grad, tile_of(weight, start, 0), 1, 1)

    @pl.when(k == 0)
    def _():
        for start in range(0, WIDTH, TILE):
            total[:, start : start + TILE] = moved(taps(start), -dilation)
        total[:, :middle] += taps(WIDTH)

    @pl.when(k == 1)
    def _():
        total[:, middle:] += taps(0)
        for start in range(0, WIDTH, TILE):
            cut = slice(start, start + TILE)
            hidden = (total[:, cut] + moved(taps(middle + start), dilation)) * live[...]
            step_sum[:, cut] = jnp.sum(hidden, axis=0, keepdims=True)
            grad_next[:, cut] = grad_frames[:, cut] * (live[...] * ROOT_HALF) + hidden


def layer_back_frames(whole, grad_pre, grad_frames, live, dilation):
    count = grad_pre.shape[0]
    return kernel_call(
        functools.partial(back_frames_kernel, dilation),
        (2,),
        [fixed(count, GATES), CONV_SPEC, fixed(count, WIDTH), fixed(count, 1)],
        [fixed(count, WIDTH), fixed(1, WIDTH)],
        [(count, WIDTH), (1, WIDTH)],
        [pltpu.VMEM((count, GATES), HALF)] * 2 + [pltpu.VMEM((count, WIDTH), jnp.float32)],
        3 * count * WIDTH * GATES,
    )(grad_pre, whole, grad_frames, live)


def on_device(
    frames_in,
    conditioning,
    prompt,
    item_lengths,
    prompt_lengths,
    key_mask,
    diffusion_steps,
    step_proj,
    conv_weight,
    cond_proj,
    out_proj,
    query_seeds,
    query_proj,
    key_proj,
    value_proj,
    mixing_proj,
    film_proj,
    cot_frames,
    cot_skip,
    devices,
):
    rings, pairs = rings_of(devices), pairs_of(devices)
    share = step_proj.shape[1]
    key_count = prompt.shape[1]
    extra_rows = -(-(key_count + LAYERS * share * QUERIES) // WIDTH)
    key_rows = -(-(key_count + extra_rows) // 8) * 8
    me = lax.axis_index(AXIS)

    frame_packs = [
        jnp.concatenate(
            [conv_weight[layer], cond_proj[layer], out_proj[layer], step_proj[layer].reshape(-1, GATES)], axis=0
        )
        for layer in range(LAYERS)
    ]
    frame_whole_0 = lax.all_gather(frame_packs[0], AXIS, axis=0, tiled=False)

    extra = jnp.concatenate(
        [key_mask.astype(jnp.float32), to_all(query_seeds, prompt.shape[0])], axis=1
    )
    extra = jnp.pad(extra, ((0, 0), (0, (key_rows - key_count) * WIDTH - extra.shape[1])))
    sent = jnp.concatenate([prompt, extra.reshape(prompt.shape[0], -1, WIDTH)], axis=1)
    query_key = jnp.concatenate([query_proj, key_proj], axis=2).reshape(LAYERS * share, GATES)
    query_key, sent = tie(query_key, sent)
    keys = lax.all_to_all(sent, AXIS, split_axis=0, concat_axis=0, tiled=True)
    extra = keys[:, key_count : key_count + extra_rows].reshape(devices, -1)
    key_place = (
        jnp.arange(devices, dtype=jnp.int32)[:, None] * key_count
        + jnp.arange(key_rows, dtype=jnp.int32)[None, :]
    )
    masked_in = jnp.pad(extra[:, :key_count], ((0, 0), (0, key_rows - key_count)))
    live_keys = (
        (jnp.arange(key_rows, dtype=jnp.int32)[None, :] < key_count)
        & (key_place < lax.dynamic_index_in_dim(prompt_lengths, me, 0, keepdims=False))
        & ((masked_in == 1.0) | (key_place == 0))
    ).reshape(-1)
    seeds = extra[:, key_count : key_count + LAYERS * share * QUERIES]
    seeds = jnp.moveaxis(seeds.reshape(devices, LAYERS, share, QUERIES), 1, 0)
    seeds = seeds.reshape(LAYERS, WIDTH, QUERIES)
    keys = keys.reshape(-1, WIDTH)

    query_key = gather_rows(query_key, rings).reshape(devices, LAYERS, share, GATES)
    query_key = jnp.moveaxis(query_key, 1, 0).reshape(LAYERS, WIDTH, GATES)
    query_rows = jnp.einsum("lwq,lwx->lqx", seeds, query_key[:, :, :WIDTH], precision=HIGHEST)
    query_heads = query_rows.reshape(LAYERS, QUERIES, HEADS, HEAD_DIM)
    key_heads = query_key[:, :, WIDTH:].reshape(LAYERS, WIDTH, HEADS, HEAD_DIM)
    absorbed = jnp.einsum("lqhe,lwhe->lhqw", query_heads, key_heads, precision=HIGHEST)
    absorbed = absorbed.reshape(LAYERS * HEADS * QUERIES, WIDTH) / math.sqrt(HEAD_DIM)

    scores = jnp.where(live_keys[None, :], small_dot(absorbed, keys, 1, 1), -1e30)
    exps = jnp.exp(scores - jnp.max(scores, axis=1, keepdims=True))
    probs = exps / jnp.sum(exps, axis=1, keepdims=True)
    probs = probs.reshape(LAYERS, HEADS, QUERIES, -1)
    pooled = jnp.mean(probs, axis=2).reshape(LAYERS * HEADS, -1)
    pooled_keys = small_dot(pooled, keys)

    frame_pack_1, frame_whole_0, pooled_keys = tie(frame_packs[1], frame_whole_0, pooled_keys)
    frame_whole_1 = lax.all_gather(frame_pack_1, AXIS, axis=0, tiled=False)

    (pooled_cut,) = exchange(by_column(pooled_keys, devices))
    pooled_cut = pooled_cut.reshape(devices, LAYERS, HEADS, share)
    pooled_cut, frame_whole_0, frames_in, conditioning = tie(pooled_cut, frame_whole_0, frames_in, conditioning)
    value_heads = value_proj.reshape(LAYERS, share, HEADS, HEAD_DIM)
    mean_part = jnp.einsum("blhw,lwhe->blhe", pooled_cut, value_heads, precision=HIGHEST)
    (mean_cut,) = exchange(by_column(mean_part.reshape(devices, LAYERS, WIDTH), devices))
    mean_cut = jnp.sum(mean_cut, axis=0).reshape(devices, LAYERS, share)
    mixed_part = jnp.einsum("blw,lwx->blx", mean_cut, mixing_proj, precision=HIGHEST)
    (mixed_cut,) = exchange(by_column(mixed_part, devices))
    mixed_cut = jnp.sum(mixed_cut, axis=0).reshape(devices, LAYERS, share)
    film_part = jnp.einsum("blw,lwx->blx", mixed_cut, film_proj, precision=HIGHEST)
    (films,) = exchange(film_part)
    films = jnp.sum(films, axis=0).reshape(LAYERS, 1, GATES)
    films, cot_frames, cot_skip = tie(films, cot_frames, cot_skip)

    live = (jnp.arange(frames_in.shape[1], dtype=jnp.int32) < item_lengths[0]).astype(jnp.float32)[:, None]
    embed = step_embedding(diffusion_steps[0])[None, :]
    embed_pairs = embed.reshape(-1, 2).T
    frames, cond, cot, cot_last = frames_in[0], conditioning[0], cot_frames[0], cot_skip[0]
    if devices != PARTS:
        frame_whole_0 = regrouped(frame_whole_0, share)
    tanh_0, sig_0, step_row_0 = layer_gates(frame_whole_0, frames, cond, embed_pairs, live, 1)
    frames_1, skip = layer_post(frame_whole_0, tanh_0, sig_0, films[0], frames, jnp.zeros_like(frames), live)

    attention_pack = jnp.concatenate(
        [
            part
            for layer in range(LAYERS)
            for part in (film_proj[layer], jnp.concatenate([value_proj[layer], mixing_proj[layer]], axis=1))
        ],
        axis=0,
    )
    attention_pack, frame_whole_1, frames_1 = tie(attention_pack, frame_whole_1, frames_1)
    attention_whole = lax.all_gather(attention_pack, AXIS, axis=0, tiled=False)
    attention_whole = attention_whole.reshape(devices, LAYERS, 2, share, GATES)
    if devices != PARTS:
        attention_whole = jnp.transpose(attention_whole, (1, 2, 0, 3, 4)).reshape(1, LAYERS, 2, WIDTH, GATES)
        frame_whole_1 = regrouped(frame_whole_1, share)

    tanh_1, sig_1, step_row_1 = layer_gates(frame_whole_1, frames_1, cond, embed_pairs, live, 2)

    def by_device(grad):
        return grad.reshape(devices, -1, GATES)

    def by_share(grad):
        return grad.reshape(devices, share, -1)

    grad_pre_1, grad_film_1, grad_out = layer_back_gates(frame_whole_1, tanh_1, sig_1, films[1], cot, cot_last, live)
    sum_2 = RowSum([by_device(grad_out)], pairs)

    def weights_1(grad_pre):
        return layer_back_weights(frames_1, cond, step_row_1, live, grad_pre, 2), grad_pre

    (grad_conv, grad_cond), grad_pre_1 = beside([sum_2], weights_1, grad_pre_1)
    sum_1 = RowSum([by_device(grad_conv), by_device(grad_cond)], pairs)

    def post_1(tanh, sig, grad_pre):
        return layer_post(frame_whole_1, tanh, sig, films[1], frames_1, skip, live), grad_pre

    (frames, skip), grad_pre_1 = beside([sum_1], post_1, tanh_1, sig_1, grad_pre_1)
    sum_1.add(sum_2)
    sum_1.join()
    sum_1.halve()

    def frames_and_gates(grad_pre):
        grad_frames, step_sum = layer_back_frames(frame_whole_1, grad_pre, cot, live, 2)
        gates = layer_back_gates(frame_whole_0, tanh_0, sig_0, films[0], grad_frames, cot_last, live)
        return grad_frames, step_sum, *gates

    grad_frames, step_sum_1, grad_pre_0, grad_film_0, grad_out = beside([sum_1], frames_and_gates, grad_pre_1)
    sum_a = RowSum([by_device(grad_out)], pairs)

    def weights_0(grad_pre):
        return layer_back_weights(frames_in[0], cond, step_row_0, live, grad_pre, 1), grad_pre

    (grad_conv, grad_cond), grad_pre_0 = beside([sum_1, sum_a], weights_0, grad_pre_0)
    sum_1.join()
    sum_b = RowSum([by_device(grad_conv), by_device(grad_cond)], pairs)
    key_w = query_key[:, :, WIDTH:]

    def attention_1(grad_film):
        return attention_back(1, grad_film, attention_whole, key_w, probs, keys)

    grad_film_0, grad_film_1 = grad_film_0.reshape(1, GATES), grad_film_1.reshape(1, GATES)
    absorbed_1, query_1, row_1, mixed_1 = beside([sum_b, sum_1], attention_1, grad_film_1)
    sum_b.add(sum_a)
    sum_b.join()
    sum_b.halve()

    def attention_and_frames(grad_film, grad_pre):
        attention = attention_back(0, grad_film, attention_whole, key_w, probs, keys)
        return *attention, *layer_back_frames(frame_whole_0, grad_pre, grad_frames, live, 1)

    absorbed_0, query_0, row_0, mixed_0, grad_frames, step_sum_0 = beside(
        [sum_b, sum_1], attention_and_frames, grad_film_0, grad_pre_0
    )
    sum_d = RowSum([by_share(absorbed_0), by_share(absorbed_1)], pairs, far_first=True)
    sum_d.step()
    query_parts = jnp.stack([query_0, query_1]).reshape(devices, -1)
    (query_cut,) = beside([sum_d, sum_b], exchange, query_parts)
    query_cut = jnp.sum(query_cut, axis=0)
    sum_d.step()
    sum_b.join()
    parts = (row_0, row_1, mixed_0, mixed_1, grad_film_0, grad_film_1, step_sum_0, step_sum_1, query_cut)
    whole_rows = jnp.concatenate([part.reshape(-1) for part in parts])
    rows, own_embeds = beside([sum_d, sum_b], exchange, to_all(whole_rows, devices), by_column(embed, devices))
    while sum_d.at < len(pairs):
        sum_d.step()
    sum_d.join()
    query_start = whole_rows.size - query_cut.size
    query_grads = rows[:, query_start:].reshape(LAYERS, QUERIES, WIDTH)
    absorbed_sums = sum_d.result().reshape(LAYERS, share, HEADS * QUERIES)

    small = [(LAYERS, share, columns) for columns in (WIDTH, QUERIES, WIDTH, WIDTH, WIDTH, WIDTH, GATES)]
    *factored, square = pl.pallas_call(factor_kernel, out_shape=shapes_of(*small, (1, 1)))(
        rows[:, :query_start],
        jnp.moveaxis(pooled_cut.reshape(devices, LAYERS, HEADS * share), 1, 0),
        jnp.moveaxis(mean_cut, 1, 0),
        jnp.moveaxis(mixed_cut, 1, 0),
        own_embeds,
        absorbed_sums,
        jnp.stack([query_rows, query_grads]),
        query_seeds,
        query_proj,
    )
    frame_sums = (sum_b.result(), sum_1.result())
    squares = pl.pallas_call(square_kernel, out_shape=shapes_of((devices, 8, 128))[0])(square, *frame_sums)
    squares = lax.all_to_all(squares, AXIS, split_axis=0, concat_axis=0, tiled=True)
    frame_shapes = [(LAYERS, rows_of * share, GATES) for rows_of in (3, 1, 1)]
    outs = pl.pallas_call(clip_kernel, out_shape=shapes_of(*small, *frame_shapes))(squares, *frame_sums, *factored)
    step_grad, seeds_grad, query_grad, key_grad, value_grad, mixing_grad, film_grad, conv_grad, cond_grad, out_grad = outs
    return (
        frames[None],
        skip[None],
        grad_frames[None],
        step_grad,
        conv_grad,
        cond_grad,
        out_grad,
        seeds_grad,
        query_grad,
        key_grad,
        value_grad,
        mixing_grad,
        film_grad,
    )


def solution(mesh):
    devices = mesh.shape[AXIS]

    def run(*args):
        return on_device(*args, devices=devices)

    items, rows = P(AXIS, None, None), P(None, AXIS, None)
    return jax.shard_map(
        run,
        mesh=mesh,
        in_specs=(items, items, rows, P(AXIS), P(), P(None, AXIS), P(AXIS)) + (rows,) * 10 + (items, items),
        out_specs=(items,) * 3 + (rows,) * 10,
        check_vma=False,
    )
```

```python
import functools
import math

import jax
import jax.numpy as jnp
from jax import lax
from jax.experimental import pallas as pl
from jax.experimental.pallas import tpu as pltpu
from jax.sharding import PartitionSpec as P

WIDTH = 512
GATES = 2 * WIDTH
HEADS = 8
HEAD_DIM = WIDTH // HEADS
QUERIES = 32
LAYERS = 2
CLIP_NORM = 1.0
AXIS = "items"
HIGH = lax.Precision.HIGH
HIGHEST = lax.Precision.HIGHEST
ROOT_HALF = math.sqrt(0.5)


def big_dot(left, right, left_dim=1, right_dim=0):
    return lax.dot_general(left, right, (((left_dim,), (right_dim,)), ((), ())), precision=HIGH)


def small_dot(left, right, left_dim=1, right_dim=0):
    return lax.dot_general(left, right, (((left_dim,), (right_dim,)), ((), ())), precision=HIGHEST)


def step_embedding(diffusion_step):
    half_width = WIDTH // 2
    ramp = jnp.arange(half_width, dtype=jnp.int32).astype(jnp.float32) / (half_width - 1)
    angles = diffusion_step.astype(jnp.float32) / 1000.0 * jnp.exp(ramp * math.log(100.0))
    return jnp.concatenate([jnp.sin(angles), jnp.cos(angles)])


class Ring:
    def __init__(self, count, size, stride):
        self.count, self.size, self.stride = count, size, stride
        self.digit = (lax.axis_index(AXIS) // stride) % size

    def shift(self, block, steps):
        perm = []
        for device in range(self.count):
            digit = (device // self.stride) % self.size
            target = (digit + steps) % self.size
            perm.append((device, device + (target - digit) * self.stride))
        return lax.ppermute(block, AXIS, perm)

    def gather(self, block):
        if self.size == 1:
            return block[None]
        others = [self.shift(block, steps) for steps in range(1, self.size)]
        if self.size == 2:
            first = jnp.where(self.digit == 0, block, others[0])
            second = jnp.where(self.digit == 0, others[0], block)
            return jnp.stack([first, second])
        out = jnp.broadcast_to(block, (self.size,) + block.shape)
        for steps, other in enumerate(others, 1):
            place = (self.digit - steps) % self.size
            out = lax.dynamic_update_index_in_dim(out, other, place, 0)
        return out

    def scatter_sum(self, blocks, dim):
        own = lax.dynamic_index_in_dim(blocks, self.digit, dim, keepdims=False)
        for steps in range(1, self.size):
            place = (self.digit + steps) % self.size
            own = own + self.shift(lax.dynamic_index_in_dim(blocks, place, dim, keepdims=False), steps)
        return own


def rings_of(count):
    bits = (count // 2).bit_length() - 1
    sizes = [2 ** ((bits + 2) // 3), 2 ** ((bits + 1) // 3), 2 ** (bits // 3), 2]
    rings, stride = [], count
    for size in sizes:
        stride //= size
        rings.append(Ring(count, size, stride))
    return rings


def pairs_of(count):
    return [Ring(count, 2, 2**bit) for bit in reversed(range(count.bit_length() - 1))]


def gather_rows(shard, rings):
    far, mid, near, core = rings
    rows, columns = shard.shape
    half = rows // 2
    block = far.gather(shard)
    top = mid.gather(near.gather(block[:, :half]))
    low = near.gather(mid.gather(block[:, half:]))
    top = jnp.transpose(top, (2, 0, 1, 3, 4))
    low = jnp.transpose(low, (2, 1, 0, 3, 4))
    rail = jnp.concatenate([top, low], axis=3)
    both = core.gather(rail)
    return jnp.transpose(both, (1, 2, 3, 0, 4, 5)).reshape(-1, rows, columns)


def hop(terms, ring, dim, gates=()):
    def pick(place):
        return [lax.dynamic_index_in_dim(term, place, dim, keepdims=False) for term in terms]

    goes, gates = tie(sum(pick(1 - ring.digit)), gates) if gates else (sum(pick(1 - ring.digit)), gates)
    return pick(ring.digit) + [ring.shift(goes, 1)], gates


class RowSum:
    parts = None

    def __init__(self, arrays, pairs, far_first=False):
        count = len(pairs)
        self.pairs, self.at, bits = pairs, 0, list(range(count))
        self.orders = []
        for k in range(len(arrays)):
            near = bits[-3:-1] if k % 2 == 0 else bits[-3:-1][::-1]
            far = bits[:-3][::-1]
            self.orders.append(bits[-1:] + (far + near if far_first else near + far))
        self.left = [list(bits) for _ in arrays]
        self.state = [[array.reshape((2,) * count + array.shape[1:])] for array in arrays]

    @classmethod
    def of_parts(cls, top_stays, low_stays, top_goes, low_goes, pairs):
        if PARTS == 2 ** len(pairs):
            sums = cls([top_goes, low_goes], pairs[:-1])
            sums.parts, sums.pairs = (top_stays, low_stays), pairs
            count = len(pairs)
            sums.orders = [[count - 1, count - 3, count - 2, 1, 0], [count - 1, count - 2, count - 3, 1, 0]]
            sums.left = [order[1:] for order in sums.orders]
            return sums
        halves = (
            [jnp.stack([half[place] for place in places]) for half in pair]
            for pair, places in zip(((top_stays, top_goes), (low_stays, low_goes)), PLACES)
        )
        whole = jnp.concatenate([jnp.stack(pair, axis=1) for pair in halves], axis=2).reshape(PARTS, -1, GATES)
        cuts = jnp.split(whole, [CONV_ROWS, CONV_ROWS + PART_ROWS], axis=1)
        sums = cls([jnp.concatenate([cut.reshape(2 ** len(pairs), -1, GATES) for cut in cuts], axis=1)], pairs)
        sums.halve()
        return sums

    def core(self, *gates):
        if self.parts is None:
            return self.step(*gates)
        goes, gates = tie([terms[0] for terms in self.state], gates)
        stays = [part.reshape(term.shape) for part, term in zip(self.parts, goes)]
        self.state = [[part, self.pairs[-1].shift(term, 1)] for part, term in zip(stays, goes)]
        self.at = 1
        return gates

    def join(self):
        parts = self.state if self.at == 1 else [[sum(terms)] for terms in self.state]
        axis = parts[0][0].ndim - 2
        self.state = [[jnp.concatenate(terms, axis=axis) for terms in zip(*parts)]]

    def halve(self):
        (terms,) = self.state
        half = terms[0].shape[-2] // 2
        self.state = [[term[..., :half, :] for term in terms], [term[..., half:, :] for term in terms]]
        ((*order,),) = self.orders
        self.orders = [order, order[:1] + order[2:0:-1] + order[3:]]
        self.left = [list(self.left[0]), list(self.left[0])]

    def step(self, *gates):
        for k, terms in enumerate(self.state):
            bit = self.orders[k][self.at]
            if self.at >= 3:
                terms = [sum(terms)]
            self.state[k], gates = hop(terms, self.pairs[bit], self.left[k].index(bit), gates)
            self.left[k].remove(bit)
        self.at += 1
        return gates

    def result(self):
        while self.at < len(self.pairs):
            self.step()
        (terms,) = self.state
        return sum(terms)


def beside(sums, work, *inputs):
    for rows in sums:
        inputs = rows.core(*inputs) if rows.at == 0 else rows.step(*inputs)
    out = work(*inputs)
    came, out = tie([[terms[-1] for terms in rows.state] for rows in sums], out)
    for rows, last in zip(sums, came):
        rows.state = [terms[:-1] + [term] for terms, term in zip(rows.state, last)]
    return out


def tie(*groups):
    leaves, tree = jax.tree.flatten(groups)
    return jax.tree.unflatten(tree, lax.optimization_barrier(leaves))


def exchange(*parts):
    devices = parts[0].shape[0]
    parts = [part.reshape(devices, -1) for part in parts]
    sizes = [part.shape[1] for part in parts]
    joined = jnp.concatenate(parts, axis=1)
    joined = jnp.pad(joined, ((0, 0), (0, -joined.shape[1] % 1024))).reshape(devices, -1, 128)
    came = lax.all_to_all(joined, AXIS, split_axis=0, concat_axis=0, tiled=True).reshape(devices, -1)
    out, start = [], 0
    for size in sizes:
        out.append(came[:, start : start + size])
        start += size
    return out


def to_all(part, devices):
    return jnp.broadcast_to(part.reshape(1, -1), (devices, part.size))


def regrouped(whole, share):
    sizes, start, pieces = (3 * share, share, share), 0, []
    for size in sizes:
        pieces.append(whole[:, start : start + size].reshape(PARTS, -1, GATES))
        start += size
    return jnp.concatenate(pieces, axis=1)


def by_column(part, devices):
    cut = part.reshape(part.shape[:-1] + (devices, -1))
    return jnp.moveaxis(cut, -2, 0).reshape(devices, -1)


def head_rows(row):
    head = jnp.arange(WIDTH, dtype=jnp.int32)[None, :] // HEAD_DIM
    own = head == jnp.arange(HEADS, dtype=jnp.int32)[:, None]
    return jnp.where(own, row, 0.0)


def exact_dot(left, right, left_dim=1, right_dim=0):
    return lax.dot_general(
        left, right, (((left_dim,), (right_dim,)), ((), ())), precision=HIGHEST, preferred_element_type=jnp.float32
    )


def split_dot(left, right, left_dim=1, right_dim=0):
    return three_dots(halves_of(left), halves_of(right), left_dim, right_dim)


def head_of(shape, dim, per_head):
    return lax.broadcasted_iota(jnp.int32, shape, dim) // per_head


def attention_back_kernel(
    grad_film, film_w, value_mixing, key_w, probs, keys, absorbed_out, query_out, row_out, mixed_out
):
    film = film_w[...].reshape(WIDTH, GATES)
    value = value_mixing[..., :WIDTH].reshape(WIDTH, WIDTH)
    mixing = value_mixing[..., WIDTH:].reshape(WIDTH, WIDTH)
    grad_mixed = split_dot(jnp.broadcast_to(grad_film[...], (16, GATES)), film, 1, 1)
    grad_row = split_dot(grad_mixed * (1.0 / QUERIES), mixing, 1, 1)
    mixed_out[...] = grad_mixed[:1]
    row_out[...] = grad_row[:1]
    own = head_of((16, WIDTH), 1, HEAD_DIM) == head_of((16, WIDTH), 0, 1)
    grad_pooled = split_dot(jnp.where(own, grad_row, 0.0), value, 1, 1)
    grad_probs = split_dot(grad_pooled, keys[...], 1, 1)
    prob = probs[0]
    weighted = prob * grad_probs[:HEADS][:, None, :]
    row_terms = jnp.sum(weighted, axis=2, keepdims=True)
    grad_scores = (weighted - prob * row_terms) * (1.0 / math.sqrt(HEAD_DIM))
    grad_scores = grad_scores.reshape(HEADS * QUERIES, -1)
    grad_absorbed = split_dot(grad_scores, keys[...])
    absorbed_out[...] = grad_absorbed.T
    grad_query = split_dot(grad_absorbed, key_w[0])
    shape = grad_query.shape
    grad_query = jnp.where(head_of(shape, 1, HEAD_DIM) == head_of(shape, 0, QUERIES), grad_query, 0.0)
    query_out[...] = jnp.sum(grad_query.reshape(HEADS, QUERIES, WIDTH), axis=0)


def attention_back(layer, grad_film, attention_whole, key_w, probs, keys):
    parts, _, _, rows, _ = attention_whole.shape
    count = keys.shape[0]

    def one(shape):
        return pl.BlockSpec((1,) + shape, lambda k: (layer,) + (0,) * len(shape))

    return kernel_call(
        attention_back_kernel,
        (1,),
        [
            fixed(1, GATES),
            pl.BlockSpec((parts, 1, 1, rows, GATES), lambda k: (0, layer, 0, 0, 0)),
            pl.BlockSpec((parts, 1, 1, rows, GATES), lambda k: (0, layer, 1, 0, 0)),
            one((WIDTH, WIDTH)),
            one((HEADS, QUERIES, count)),
            fixed(count, WIDTH),
        ],
        [fixed(WIDTH, HEADS * QUERIES), fixed(QUERIES, WIDTH), fixed(1, WIDTH), fixed(1, WIDTH)],
        [(WIDTH, HEADS * QUERIES), (QUERIES, WIDTH), (1, WIDTH), (1, WIDTH)],
        [],
        10 * WIDTH * HEADS * QUERIES * count // 4,
    )(grad_film, attention_whole, attention_whole, key_w, probs, keys)


def factor_kernel(
    rows, step_rows, pooled, means, mixeds, embeds, absorbed, query_rows, seeds, query_w,
    step_out, seeds_out, query_out, key_out, value_out, mixing_out, film_out, square_out,
):
    share = embeds.shape[1]
    at = {}
    start = 0
    for name, size in (("row", WIDTH), ("mixed", WIDTH), ("film", GATES)):
        for layer in range(LAYERS):
            at[name, layer] = rows[:, start : start + size]
            start += size
    for layer in range(LAYERS):
        at["step", layer] = step_rows[:, layer * WIDTH : (layer + 1) * WIDTH]
    square = jnp.zeros((1, 1), jnp.float32)
    own = head_of((HEADS, share, WIDTH), 2, HEAD_DIM) == head_of((HEADS, share, WIDTH), 0, 1)
    near = head_of((HEADS * QUERIES, WIDTH), 1, HEAD_DIM) == head_of((HEADS * QUERIES, WIDTH), 0, QUERIES)
    for layer in range(LAYERS):
        value = exact_dot(pooled[layer], at["row", layer], 0, 0).reshape(HEADS, share, WIDTH)
        spread = jnp.where(near, jnp.concatenate([query_rows[0, layer]] * HEADS, axis=0), 0.0)
        grads = (
            (step_out, exact_dot(embeds[...], at["step", layer], 0, 0)),
            (seeds_out, exact_dot(query_w[layer], query_rows[1, layer], 1, 1)),
            (query_out, exact_dot(seeds[layer], query_rows[1, layer])),
            (key_out, exact_dot(absorbed[layer], spread)),
            (value_out, QUERIES * jnp.sum(jnp.where(own, value, 0.0), axis=0)),
            (mixing_out, exact_dot(means[layer], at["mixed", layer], 0, 0)),
            (film_out, exact_dot(mixeds[layer], at["film", layer], 0, 0)),
        )
        for out, grad in grads:
            out[layer] = grad
            square = square + jnp.sum(jnp.sum(grad * grad, axis=1, keepdims=True), axis=0, keepdims=True)
    square_out[...] = square


def square_kernel(square, *refs):
    *sums, out = refs
    total = square[...]
    for part in sums:
        total = total + jnp.sum(jnp.sum(part[...] * part[...], axis=1, keepdims=True), axis=0, keepdims=True)
    out[...] = jnp.broadcast_to(total[None], out.shape)


def clip_kernel(squares, sums_0, sums_1, *refs):
    places = squares[:, 0, :1]
    norm_square = jnp.sum(places, axis=0, keepdims=True)
    factor = jnp.minimum(1.0, CLIP_NORM / jnp.sqrt(norm_square))
    count = (len(refs) - 3) // 2
    grads, outs = refs[:count], refs[count : 2 * count]
    conv_out, cond_out, out_out = refs[2 * count :]
    for grad, out in zip(grads, outs):
        for layer in range(LAYERS):
            out[layer] = grad[layer] * factor
    share = cond_out.shape[1]
    for layer, sums in enumerate((sums_0, sums_1)):
        conv_out[layer] = sums[: 3 * share] * factor
        cond_out[layer] = sums[3 * share : 4 * share] * factor
        out_out[layer] = sums[4 * share :] * factor


def shapes_of(*shapes):
    return [jax.ShapeDtypeStruct(shape, jnp.float32) for shape in shapes]


HALF = jnp.bfloat16
PARTS = 32
PLACES = (
    [(pair // 2 % 2) * 8 + pair % 2 * 4 + pair // 4 % 2 * 2 + pair // 8 for pair in range(PARTS // 2)],
    [pair % 2 * 8 + (pair // 2 % 2) * 4 + pair // 4 % 2 * 2 + pair // 8 for pair in range(PARTS // 2)],
)
CONV_ROWS, PART_ROWS = 3 * WIDTH // PARTS, WIDTH // PARTS
TILE = 256


def halves_of(array):
    high = array.astype(HALF)
    return high, (array - high.astype(jnp.float32)).astype(HALF)


def three_dots(left, right, left_dim, right_dim):
    def dot(one, other):
        dims = (((left_dim,), (right_dim,)), ((), ()))
        return lax.dot_general(one, other, dims, preferred_element_type=jnp.float32)

    return dot(left[0], right[0]) + (dot(left[0], right[1]) + dot(left[1], right[0]))


def tile_of(pair, start, dim, size=TILE):
    return tuple(lax.slice_in_dim(half, start, start + size, axis=dim) for half in pair)


def moved(rows, steps):
    count = rows.shape[0]
    place = lax.broadcasted_iota(jnp.int32, rows.shape, 0) - steps
    return jnp.where((place >= 0) & (place < count), pltpu.roll(rows, steps % count, 0), 0.0)


def shape_of(*sizes):
    dtype = jnp.float32 if isinstance(sizes[-1], int) else sizes[-1]
    return jax.ShapeDtypeStruct(tuple(size for size in sizes if isinstance(size, int)), dtype)


def kernel_call(kernel, grid, in_specs, out_specs, out_shapes, scratch, macs):
    return pl.pallas_call(
        kernel,
        grid=grid,
        in_specs=in_specs,
        out_specs=out_specs,
        out_shape=[shape_of(*shape) for shape in out_shapes],
        scratch_shapes=scratch,
        compiler_params=pltpu.CompilerParams(vmem_limit_bytes=60 * 2**20),
        cost_estimate=pl.CostEstimate(flops=6 * macs, bytes_accessed=16 * 2**20, transcendentals=0),
    )


def fixed(*shape):
    return pl.BlockSpec(shape, lambda k: (0,) * len(shape))


def part_rows(size, at):
    return pl.BlockSpec((PARTS, size, GATES), lambda k: (0, at, 0))


CONV_SPEC = pl.BlockSpec((PARTS // 2, CONV_ROWS, GATES), lambda k: (jnp.minimum(k, 1), 0, 0))
COND_SPEC = part_rows(PART_ROWS, 3)
OUT_SPEC = part_rows(PART_ROWS, 4)


def gates_kernel(dilation, frames, cond, conv_w, cond_w, step_row, live, tanh, sig, total):
    k = pl.program_id(0)

    def add(left, right, first):
        for start in range(0, GATES, TILE):
            part = three_dots(left, tile_of(right, start, 1), 1, 0)
            total[:, start : start + TILE] = part if first else total[:, start : start + TILE] + part

    @pl.when(k == 0)
    def _():
        hidden = (frames[...] + step_row[...]) * live[...]
        taps = jnp.concatenate([moved(hidden, dilation), hidden[:, : WIDTH // 2]], axis=1)
        add(halves_of(taps), halves_of(conv_w[...].reshape(-1, GATES)), True)

    @pl.when(k == 1)
    def _():
        hidden = (frames[...] + step_row[...]) * live[...]
        taps = jnp.concatenate([hidden[:, WIDTH // 2 :], moved(hidden, -dilation)], axis=1)
        add(halves_of(taps), halves_of(conv_w[...].reshape(-1, GATES)), False)

    @pl.when(k == 2)
    def _():
        left, right = halves_of(cond[...]), halves_of(cond_w[...].reshape(-1, GATES))
        for start in range(0, WIDTH, TILE):
            part = three_dots(left, tile_of(right, start, 1), 1, 0)
            tanh[:, start : start + TILE] = jnp.tanh(total[:, start : start + TILE] + part)
        for start in range(0, WIDTH, TILE):
            part = three_dots(left, tile_of(right, WIDTH + start, 1), 1, 0)
            sig[:, start : start + TILE] = jax.nn.sigmoid(total[:, WIDTH + start : WIDTH + start + TILE] + part)


def layer_gates(whole, frames, cond, step_row, live, dilation):
    count = frames.shape[0]
    return kernel_call(
        functools.partial(gates_kernel, dilation),
        (3,),
        [fixed(count, WIDTH)] * 2 + [CONV_SPEC, COND_SPEC, fixed(1, WIDTH), fixed(count, 1)],
        [fixed(count, WIDTH)] * 2,
        [(count, WIDTH)] * 2,
        [pltpu.VMEM((count, GATES), jnp.float32)],
        4 * count * WIDTH * GATES,
    )(frames, cond, whole, whole, step_row, live)


def post_kernel(tanh, sig, film, out_w, frames, skip, live, frames_next, skip_next, high, low):
    @pl.when(pl.program_id(0) == 0)
    def _():
        high[...], low[...] = halves_of(out_w[...].reshape(-1, GATES))

    modulated = halves_of(tanh[...] * sig[...] * (1.0 + film[:1]) + film[1:])
    for start in range(0, WIDTH, TILE):
        cut = slice(start, start + TILE)
        post = three_dots(modulated, (high[:, cut], low[:, cut]), 1, 0)
        frames_next[:, cut] = (frames[:, cut] + post) * (live[...] * ROOT_HALF)
    for start in range(0, WIDTH, TILE):
        cut, far = slice(start, start + TILE), slice(WIDTH + start, WIDTH + start + TILE)
        post = three_dots(modulated, (high[:, far], low[:, far]), 1, 0)
        skip_next[:, cut] = skip[:, cut] + post * live[...]


def layer_post(whole, tanh, sig, film, frames, skip, live):
    count = frames.shape[0]
    rows = pl.BlockSpec((count // 2, WIDTH), lambda k: (k, 0))
    return kernel_call(
        post_kernel,
        (2,),
        [rows, rows, fixed(2, WIDTH), OUT_SPEC, rows, rows, pl.BlockSpec((count // 2, 1), lambda k: (k, 0))],
        [rows, rows],
        [(count, WIDTH)] * 2,
        [pltpu.VMEM((WIDTH, GATES), HALF)] * 2,
        count * WIDTH * GATES,
    )(tanh, sig, film.reshape(2, WIDTH), whole, frames, skip, live)


def back_gates_kernel(
    grad_frames, grad_skip, live, tanh, sig, film, out_w, pre_high, pre_low, grad_film, grad_out, high, low
):
    k = pl.program_id(0)

    @pl.when(k == 0)
    def _():
        high[...], low[...] = halves_of(out_w[...].reshape(-1, GATES))
        grad_film[...] = jnp.zeros_like(grad_film)

    post = jnp.concatenate([grad_frames[...] * (live[...] * ROOT_HALF), grad_skip[...] * live[...]], axis=1)
    post = halves_of(post)
    for start in range(0, WIDTH, TILE):
        cut, far = slice(start, start + TILE), slice(WIDTH + start, WIDTH + start + TILE)
        grad_mod = three_dots(post, (high[cut, :], low[cut, :]), 1, 1)
        t, s = tanh[:, cut], sig[:, cut]
        gate = t * s
        grad_film[0:1, cut] += jnp.sum(grad_mod * gate, axis=0, keepdims=True)
        grad_film[1:2, cut] += jnp.sum(grad_mod, axis=0, keepdims=True)
        grad_gate = grad_mod * (1.0 + film[:1, cut])
        pre_high[:, cut], pre_low[:, cut] = halves_of(grad_gate * (s * (1.0 - t * t)))
        pre_high[:, far], pre_low[:, far] = halves_of(grad_gate * (gate * (1.0 - s)))
    modulated = tanh[...] * sig[...] * (1.0 + film[:1]) + film[1:]
    modulated = halves_of(modulated.T)

    @pl.when(k == 0)
    def _():
        for start in range(0, GATES, TILE):
            grad_out[:, start : start + TILE] = three_dots(modulated, tile_of(post, start, 1), 1, 0)

    @pl.when(k > 0)
    def _():
        for start in range(0, GATES, TILE):
            grad_out[:, start : start + TILE] += three_dots(modulated, tile_of(post, start, 1), 1, 0)


def layer_back_gates(whole, tanh, sig, film, grad_frames, grad_skip, live):
    count = tanh.shape[0]
    rows = pl.BlockSpec((count // 2, WIDTH), lambda k: (k, 0))
    return kernel_call(
        back_gates_kernel,
        (2,),
        [rows, rows, pl.BlockSpec((count // 2, 1), lambda k: (k, 0)), rows, rows, fixed(2, WIDTH), OUT_SPEC],
        [pl.BlockSpec((count // 2, GATES), lambda k: (k, 0))] * 2 + [fixed(2, WIDTH), fixed(WIDTH, GATES)],
        [(count, GATES, HALF)] * 2 + [(2, WIDTH), (WIDTH, GATES)],
        [pltpu.VMEM((WIDTH, GATES), HALF)] * 2,
        2 * count * WIDTH * GATES,
    )(grad_frames, grad_skip, live, tanh, sig, film.reshape(2, WIDTH), whole)


def back_weights_kernel(
    dilation, core, frames, cond, step_row, live, pre_high, pre_low, grad_out,
    top_stays, low_stays, top_goes, low_goes, high, low, conv_rows, cond_rows,
):
    @pl.when(pl.program_id(0) == 0)
    def _():
        hidden = ((frames[...] + step_row[...]) * live[...]).T
        count = hidden.shape[1]
        for tap, steps in enumerate((dilation, 0, -dilation)):
            moved_rows = hidden
            if steps:
                place = lax.broadcasted_iota(jnp.int32, hidden.shape, 1) - steps
                moved_rows = pltpu.roll(hidden, steps % count, 1)
                moved_rows = jnp.where((place >= 0) & (place < count), moved_rows, 0.0)
            cut = slice(tap * WIDTH, (tap + 1) * WIDTH)
            high[cut, :], low[cut, :] = halves_of(moved_rows)
        cut = slice(3 * WIDTH, 4 * WIDTH)
        high[cut, :], low[cut, :] = halves_of(cond[...].T)

    grad = (pre_high[...], pre_low[...])
    for start in range(0, 4 * WIDTH, 2 * TILE):
        cut = slice(start, start + 2 * TILE)
        part = three_dots((high[cut, :], low[cut, :]), grad, 1, 0)
        if start < 3 * WIDTH:
            conv_rows[cut, :] = part
        else:
            cond_rows[start - 3 * WIDTH : start - 3 * WIDTH + 2 * TILE, :] = part
    half = top_goes.shape[1]
    rest = CONV_ROWS - half
    for top_out, low_out, parity in ((top_stays, low_stays, core[0]), (top_goes, low_goes, 1 - core[0])):
        for pair in range(PARTS // 2):
            part = 2 * pair + parity
            rows = pl.multiple_of(part * CONV_ROWS, 8)
            top_out[PLACES[0][pair]] = conv_rows[pl.ds(rows, half), :]
            place = PLACES[1][pair]
            low_out[place, :rest, :] = conv_rows[pl.ds(rows + half, rest), :]
            rows = pl.multiple_of(part * PART_ROWS, 8)
            low_out[place, rest : rest + PART_ROWS, :] = cond_rows[pl.ds(rows, PART_ROWS), :]
            low_out[place, rest + PART_ROWS :, :] = grad_out[pl.ds(rows, PART_ROWS), :]


def layer_back_weights(core, frames, cond, step_row, live, grad_pre, grad_out, dilation):
    count = frames.shape[0]
    part = (PARTS // 2, (CONV_ROWS + 2 * PART_ROWS) // 2)
    columns = pl.BlockSpec(part + (TILE,), lambda k: (0, 0, k))
    return kernel_call(
        functools.partial(back_weights_kernel, dilation),
        (GATES // TILE,),
        [pl.BlockSpec(memory_space=pltpu.SMEM)]
        + [fixed(count, WIDTH)] * 2
        + [fixed(1, WIDTH), fixed(count, 1)]
        + [pl.BlockSpec((rows, TILE), lambda k: (0, k)) for rows in (count, count, WIDTH)],
        [columns] * 4,
        [part + (GATES,)] * 4,
        [pltpu.VMEM((4 * WIDTH, count), HALF)] * 2
        + [pltpu.VMEM((rows, TILE), jnp.float32) for rows in (3 * WIDTH, WIDTH)],
        4 * count * WIDTH * GATES,
    )(core, frames, cond, step_row, live, *grad_pre, grad_out)


def back_frames_kernel(dilation, pre_high, pre_low, conv_w, grad_frames, live, grad_next, step_sum, total):
    k = pl.program_id(0)
    middle = WIDTH // 2
    grad, weight = (pre_high[...], pre_low[...]), halves_of(conv_w[...].reshape(-1, GATES))

    def taps(start):
        return three_dots(grad, tile_of(weight, start, 0), 1, 1)

    @pl.when(k == 0)
    def _():
        for start in range(0, WIDTH, TILE):
            total[:, start : start + TILE] = moved(taps(start), -dilation)
        total[:, :middle] += taps(WIDTH)

    @pl.when(k == 1)
    def _():
        total[:, middle:] += taps(0)
        for start in range(0, WIDTH, TILE):
            cut = slice(start, start + TILE)
            hidden = (total[:, cut] + moved(taps(middle + start), dilation)) * live[...]
            step_sum[:, cut] = jnp.sum(hidden, axis=0, keepdims=True)
            grad_next[:, cut] = grad_frames[:, cut] * (live[...] * ROOT_HALF) + hidden


def layer_back_frames(whole, grad_pre, grad_frames, live, dilation):
    count = grad_pre[0].shape[0]
    return kernel_call(
        functools.partial(back_frames_kernel, dilation),
        (2,),
        [fixed(count, GATES)] * 2 + [CONV_SPEC, fixed(count, WIDTH), fixed(count, 1)],
        [fixed(count, WIDTH), fixed(1, WIDTH)],
        [(count, WIDTH), (1, WIDTH)],
        [pltpu.VMEM((count, WIDTH), jnp.float32)],
        3 * count * WIDTH * GATES,
    )(*grad_pre, whole, grad_frames, live)


def on_device(
    frames_in,
    conditioning,
    prompt,
    item_lengths,
    prompt_lengths,
    key_mask,
    diffusion_steps,
    step_proj,
    conv_weight,
    cond_proj,
    out_proj,
    query_seeds,
    query_proj,
    key_proj,
    value_proj,
    mixing_proj,
    film_proj,
    cot_frames,
    cot_skip,
    devices,
):
    rings, pairs = rings_of(devices), pairs_of(devices)
    share = step_proj.shape[1]
    key_count = prompt.shape[1]
    extra_size = key_count + LAYERS * share * QUERIES
    extra_rows = -(-(extra_size + 1) // WIDTH)
    key_rows = -(-(key_count + extra_rows) // 8) * 8
    me = lax.axis_index(AXIS)

    frame_packs = [
        jnp.concatenate([conv_weight[layer], cond_proj[layer], out_proj[layer]], axis=0) for layer in range(LAYERS)
    ]
    frame_whole_0 = lax.all_gather(frame_packs[0], AXIS, axis=0, tiled=False)

    extra = (
        key_mask.astype(jnp.float32),
        to_all(query_seeds, devices),
        to_all(diffusion_steps.astype(jnp.float32), devices),
    )
    extra = jnp.concatenate(extra, axis=1)
    extra = jnp.pad(extra, ((0, 0), (0, (key_rows - key_count) * WIDTH - extra.shape[1])))
    sent = jnp.concatenate([prompt, extra.reshape(prompt.shape[0], -1, WIDTH)], axis=1)
    query_key = jnp.concatenate([query_proj, key_proj], axis=2).reshape(LAYERS * share, GATES)
    query_key, sent = tie(query_key, sent)
    keys = lax.all_to_all(sent, AXIS, split_axis=0, concat_axis=0, tiled=True)
    extra = keys[:, key_count : key_count + extra_rows].reshape(devices, -1)
    key_place = (
        jnp.arange(devices, dtype=jnp.int32)[:, None] * key_count
        + jnp.arange(key_rows, dtype=jnp.int32)[None, :]
    )
    masked_in = jnp.pad(extra[:, :key_count], ((0, 0), (0, key_rows - key_count)))
    live_keys = (
        (jnp.arange(key_rows, dtype=jnp.int32)[None, :] < key_count)
        & (key_place < lax.dynamic_index_in_dim(prompt_lengths, me, 0, keepdims=False))
        & ((masked_in == 1.0) | (key_place == 0))
    ).reshape(-1)
    seeds = extra[:, key_count:extra_size]
    seeds = jnp.moveaxis(seeds.reshape(devices, LAYERS, share, QUERIES), 1, 0)
    seeds = seeds.reshape(LAYERS, WIDTH, QUERIES)
    keys = keys.reshape(-1, WIDTH)

    embeds = jax.vmap(step_embedding)(extra[:, extra_size])
    own_embeds = lax.dynamic_slice_in_dim(embeds, me * share, share, 1)
    step_part = jnp.einsum("bw,lwx->blx", own_embeds, step_proj, precision=HIGHEST)

    query_key = gather_rows(query_key, rings).reshape(devices, LAYERS, share, GATES)
    query_key = jnp.moveaxis(query_key, 1, 0).reshape(LAYERS, WIDTH, GATES)
    query_rows = jnp.einsum("lwq,lwx->lqx", seeds, query_key[:, :, :WIDTH], precision=HIGHEST)
    query_heads = query_rows.reshape(LAYERS, QUERIES, HEADS, HEAD_DIM)
    key_heads = query_key[:, :, WIDTH:].reshape(LAYERS, WIDTH, HEADS, HEAD_DIM)
    absorbed = jnp.einsum("lqhe,lwhe->lhqw", query_heads, key_heads, precision=HIGHEST)
    absorbed = absorbed.reshape(LAYERS * HEADS * QUERIES, WIDTH) / math.sqrt(HEAD_DIM)

    scores = jnp.where(live_keys[None, :], small_dot(absorbed, keys, 1, 1), -1e30)
    exps = jnp.exp(scores - jnp.max(scores, axis=1, keepdims=True))
    probs = exps / jnp.sum(exps, axis=1, keepdims=True)
    probs = probs.reshape(LAYERS, HEADS, QUERIES, -1)
    pooled = jnp.mean(probs, axis=2).reshape(LAYERS * HEADS, -1)
    pooled_keys = small_dot(pooled, keys)

    frame_pack_1, frame_whole_0, pooled_keys = tie(frame_packs[1], frame_whole_0, pooled_keys)
    frame_whole_1 = lax.all_gather(frame_pack_1, AXIS, axis=0, tiled=False)

    pooled_cut, step_rows = exchange(by_column(pooled_keys, devices), step_part)
    step_rows = jnp.sum(step_rows, axis=0).reshape(LAYERS, 1, WIDTH)
    pooled_cut = pooled_cut.reshape(devices, LAYERS, HEADS, share)
    pooled_cut, frame_whole_0, frames_in, conditioning = tie(pooled_cut, frame_whole_0, frames_in, conditioning)
    value_heads = value_proj.reshape(LAYERS, share, HEADS, HEAD_DIM)
    mean_part = jnp.einsum("blhw,lwhe->blhe", pooled_cut, value_heads, precision=HIGHEST)
    (mean_cut,) = exchange(by_column(mean_part.reshape(devices, LAYERS, WIDTH), devices))
    mean_cut = jnp.sum(mean_cut, axis=0).reshape(devices, LAYERS, share)
    mixed_part = jnp.einsum("blw,lwx->blx", mean_cut, mixing_proj, precision=HIGHEST)
    (mixed_cut,) = exchange(by_column(mixed_part, devices))
    mixed_cut = jnp.sum(mixed_cut, axis=0).reshape(devices, LAYERS, share)
    film_part = jnp.einsum("blw,lwx->blx", mixed_cut, film_proj, precision=HIGHEST)
    (films,) = exchange(film_part)
    films = jnp.sum(films, axis=0).reshape(LAYERS, 1, GATES)
    films, cot_frames, cot_skip = tie(films, cot_frames, cot_skip)

    live = (jnp.arange(frames_in.shape[1], dtype=jnp.int32) < item_lengths[0]).astype(jnp.float32)[:, None]
    frames, cond, cot, cot_last = frames_in[0], conditioning[0], cot_frames[0], cot_skip[0]
    if devices != PARTS:
        frame_whole_0 = regrouped(frame_whole_0, share)
    tanh_0, sig_0 = layer_gates(frame_whole_0, frames, cond, step_rows[0], live, 1)
    frames_1, skip = layer_post(frame_whole_0, tanh_0, sig_0, films[0], frames, jnp.zeros_like(frames), live)

    attention_pack = jnp.concatenate(
        [
            part
            for layer in range(LAYERS)
            for part in (film_proj[layer], jnp.concatenate([value_proj[layer], mixing_proj[layer]], axis=1))
        ],
        axis=0,
    )
    attention_pack, frame_whole_1, frames_1 = tie(attention_pack, frame_whole_1, frames_1)
    attention_whole = lax.all_gather(attention_pack, AXIS, axis=0, tiled=False)
    attention_whole = attention_whole.reshape(devices, LAYERS, 2, share, GATES)
    if devices != PARTS:
        attention_whole = jnp.transpose(attention_whole, (1, 2, 0, 3, 4)).reshape(1, LAYERS, 2, WIDTH, GATES)
        frame_whole_1 = regrouped(frame_whole_1, share)

    tanh_1, sig_1 = layer_gates(frame_whole_1, frames_1, cond, step_rows[1], live, 2)

    def by_device(grad):
        return grad.reshape(devices, -1, GATES)

    def by_share(grad):
        return grad.reshape(devices, share, -1)

    core = (me % 2 if devices == PARTS else jnp.zeros_like(me)).astype(jnp.int32).reshape(1)
    *grad_pre_1, grad_film_1, grad_out = layer_back_gates(frame_whole_1, tanh_1, sig_1, films[1], cot, cot_last, live)
    parts = layer_back_weights(core, frames_1, cond, step_rows[1], live, grad_pre_1, grad_out, 2)
    sum_1 = RowSum.of_parts(*parts, pairs)

    def post_1(tanh, sig, grad_pre):
        return layer_post(frame_whole_1, tanh, sig, films[1], frames_1, skip, live), grad_pre

    (frames, skip), grad_pre_1 = beside([sum_1], post_1, tanh_1, sig_1, grad_pre_1)

    def frames_and_gates(grad_pre):
        grad_frames, step_sum = layer_back_frames(frame_whole_1, grad_pre, cot, live, 2)
        gates = layer_back_gates(frame_whole_0, tanh_0, sig_0, films[0], grad_frames, cot_last, live)
        return grad_frames, step_sum, *gates

    grad_frames, step_sum_1, *grad_pre_0, grad_film_0, grad_out = beside([sum_1], frames_and_gates, grad_pre_1)

    def weights_0(grad_pre):
        return layer_back_weights(core, frames_in[0], cond, step_rows[0], live, grad_pre, grad_out, 1), grad_pre

    parts, grad_pre_0 = beside([sum_1], weights_0, grad_pre_0)
    sum_1.join()
    sum_b = RowSum.of_parts(*parts, pairs)
    key_w = query_key[:, :, WIDTH:]

    def attention_1(grad_film):
        return attention_back(1, grad_film, attention_whole, key_w, probs, keys)

    grad_film_0, grad_film_1 = grad_film_0.reshape(1, GATES), grad_film_1.reshape(1, GATES)
    absorbed_1, query_1, row_1, mixed_1 = beside([sum_b, sum_1], attention_1, grad_film_1)

    def attention_and_frames(grad_film, grad_pre):
        attention = attention_back(0, grad_film, attention_whole, key_w, probs, keys)
        return *attention, *layer_back_frames(frame_whole_0, grad_pre, grad_frames, live, 1)

    absorbed_0, query_0, row_0, mixed_0, grad_frames, step_sum_0 = beside(
        [sum_b, sum_1], attention_and_frames, grad_film_0, grad_pre_0
    )
    sum_d = RowSum([by_share(absorbed_0), by_share(absorbed_1)], pairs, far_first=True)
    sum_d.step()
    query_parts = jnp.stack([query_0, query_1]).reshape(devices, -1)
    first_rows = jnp.concatenate(
        [part.reshape(-1) for part in (row_0, row_1, mixed_0, mixed_1, grad_film_0, grad_film_1)]
    )
    query_cut, first_rows = beside([sum_d, sum_b], exchange, query_parts, to_all(first_rows, devices))
    (query_cut,) = sum_d.step(jnp.sum(query_cut, axis=0))
    sum_b.join()
    last_rows = jnp.concatenate([part.reshape(-1) for part in (step_sum_0, step_sum_1, query_cut)])
    (last_rows,) = beside([sum_b], exchange, to_all(last_rows, devices))
    (sum_d.state,) = sum_b.step(sum_d.state)
    while sum_d.at < len(pairs):
        sum_d.step()
    sum_d.join()
    query_grads = last_rows[:, LAYERS * WIDTH :].reshape(LAYERS, QUERIES, WIDTH)
    absorbed_sums = sum_d.result().reshape(LAYERS, share, HEADS * QUERIES)

    small = [(LAYERS, share, columns) for columns in (WIDTH, QUERIES, WIDTH, WIDTH, WIDTH, WIDTH, GATES)]
    *factored, square = pl.pallas_call(factor_kernel, out_shape=shapes_of(*small, (1, 1)))(
        first_rows,
        last_rows[:, : LAYERS * WIDTH],
        jnp.moveaxis(pooled_cut.reshape(devices, LAYERS, HEADS * share), 1, 0),
        jnp.moveaxis(mean_cut, 1, 0),
        jnp.moveaxis(mixed_cut, 1, 0),
        own_embeds,
        absorbed_sums,
        jnp.stack([query_rows, query_grads]),
        query_seeds,
        query_proj,
    )
    frame_sums = (sum_b.result(), sum_1.result())
    squares = pl.pallas_call(square_kernel, out_shape=shapes_of((devices, 8, 128))[0])(square, *frame_sums)
    squares = lax.all_to_all(squares, AXIS, split_axis=0, concat_axis=0, tiled=True)
    frame_shapes = [(LAYERS, rows_of * share, GATES) for rows_of in (3, 1, 1)]
    outs = pl.pallas_call(clip_kernel, out_shape=shapes_of(*small, *frame_shapes))(squares, *frame_sums, *factored)
    step_grad, seeds_grad, query_grad, key_grad, value_grad, mixing_grad, film_grad, conv_grad, cond_grad, out_grad = outs
    return (
        frames[None],
        skip[None],
        grad_frames[None],
        step_grad,
        conv_grad,
        cond_grad,
        out_grad,
        seeds_grad,
        query_grad,
        key_grad,
        value_grad,
        mixing_grad,
        film_grad,
    )


def solution(mesh):
    devices = mesh.shape[AXIS]

    def run(*args):
        return on_device(*args, devices=devices)

    items, rows = P(AXIS, None, None), P(None, AXIS, None)
    return jax.shard_map(
        run,
        mesh=mesh,
        in_specs=(items, items, rows, P(AXIS), P(), P(None, AXIS), P(AXIS)) + (rows,) * 10 + (items, items),
        out_specs=(items,) * 3 + (rows,) * 10,
        check_vma=False,
    )
```

```python
import functools
import math

import jax
import jax.numpy as jnp
from jax import lax
from jax.experimental import pallas as pl
from jax.experimental.pallas import tpu as pltpu
from jax.sharding import PartitionSpec as P

WIDTH = 512
GATES = 2 * WIDTH
HEADS = 8
HEAD_DIM = WIDTH // HEADS
QUERIES = 32
LAYERS = 2
CLIP_NORM = 1.0
AXIS = "items"
HIGH = lax.Precision.HIGH
HIGHEST = lax.Precision.HIGHEST
ROOT_HALF = math.sqrt(0.5)


def big_dot(left, right, left_dim=1, right_dim=0):
    return lax.dot_general(left, right, (((left_dim,), (right_dim,)), ((), ())), precision=HIGH)


def small_dot(left, right, left_dim=1, right_dim=0):
    return lax.dot_general(left, right, (((left_dim,), (right_dim,)), ((), ())), precision=HIGHEST)


def step_embedding(diffusion_step):
    half_width = WIDTH // 2
    ramp = jnp.arange(half_width, dtype=jnp.int32).astype(jnp.float32) / (half_width - 1)
    angles = diffusion_step.astype(jnp.float32) / 1000.0 * jnp.exp(ramp * math.log(100.0))
    return jnp.concatenate([jnp.sin(angles), jnp.cos(angles)])


class Ring:
    def __init__(self, count, size, stride):
        self.count, self.size, self.stride = count, size, stride
        self.digit = (lax.axis_index(AXIS) // stride) % size

    def shift(self, block, steps):
        perm = []
        for device in range(self.count):
            digit = (device // self.stride) % self.size
            target = (digit + steps) % self.size
            perm.append((device, device + (target - digit) * self.stride))
        return lax.ppermute(block, AXIS, perm)

    def gather(self, block):
        if self.size == 1:
            return block[None]
        others = [self.shift(block, steps) for steps in range(1, self.size)]
        if self.size == 2:
            first = jnp.where(self.digit == 0, block, others[0])
            second = jnp.where(self.digit == 0, others[0], block)
            return jnp.stack([first, second])
        out = jnp.broadcast_to(block, (self.size,) + block.shape)
        for steps, other in enumerate(others, 1):
            place = (self.digit - steps) % self.size
            out = lax.dynamic_update_index_in_dim(out, other, place, 0)
        return out

    def scatter_sum(self, blocks, dim):
        own = lax.dynamic_index_in_dim(blocks, self.digit, dim, keepdims=False)
        for steps in range(1, self.size):
            place = (self.digit + steps) % self.size
            own = own + self.shift(lax.dynamic_index_in_dim(blocks, place, dim, keepdims=False), steps)
        return own


def rings_of(count):
    bits = (count // 2).bit_length() - 1
    sizes = [2 ** ((bits + 2) // 3), 2 ** ((bits + 1) // 3), 2 ** (bits // 3), 2]
    rings, stride = [], count
    for size in sizes:
        stride //= size
        rings.append(Ring(count, size, stride))
    return rings


def pairs_of(count):
    return [Ring(count, 2, 2**bit) for bit in reversed(range(count.bit_length() - 1))]


def gather_rows(shard, rings):
    far, mid, near, core = rings
    rows, columns = shard.shape
    half = rows // 2
    block = far.gather(shard)
    top = mid.gather(near.gather(block[:, :half]))
    low = near.gather(mid.gather(block[:, half:]))
    top = jnp.transpose(top, (2, 0, 1, 3, 4))
    low = jnp.transpose(low, (2, 1, 0, 3, 4))
    rail = jnp.concatenate([top, low], axis=3)
    both = core.gather(rail)
    return jnp.transpose(both, (1, 2, 3, 0, 4, 5)).reshape(-1, rows, columns)


def hop(terms, ring, dim, gates=()):
    def pick(place):
        return [lax.dynamic_index_in_dim(term, place, dim, keepdims=False) for term in terms]

    goes, gates = tie(sum(pick(1 - ring.digit)), gates) if gates else (sum(pick(1 - ring.digit)), gates)
    return pick(ring.digit) + [ring.shift(goes, 1)], gates


class RowSum:
    parts = None

    def __init__(self, arrays, pairs, far_first=False):
        count = len(pairs)
        self.pairs, self.at, bits = pairs, 0, list(range(count))
        self.orders = []
        for k in range(len(arrays)):
            near = bits[-3:-1] if k % 2 == 0 else bits[-3:-1][::-1]
            far = bits[:-3][::-1]
            self.orders.append(bits[-1:] + (far + near if far_first else near + far))
        self.left = [list(bits) for _ in arrays]
        self.state = [[array.reshape((2,) * count + array.shape[1:])] for array in arrays]

    @classmethod
    def of_parts(cls, top_stays, low_stays, top_goes, low_goes, pairs):
        if PARTS == 2 ** len(pairs):
            sums = cls([top_goes, low_goes], pairs[:-1])
            sums.parts, sums.pairs = (top_stays, low_stays), pairs
            count = len(pairs)
            sums.orders = [[count - 1, count - 3, count - 2, 1, 0], [count - 1, count - 2, count - 3, 1, 0]]
            sums.left = [order[1:] for order in sums.orders]
            return sums
        halves = (
            [jnp.stack([half[place] for place in places]) for half in pair]
            for pair, places in zip(((top_stays, top_goes), (low_stays, low_goes)), PLACES)
        )
        whole = jnp.concatenate([jnp.stack(pair, axis=1) for pair in halves], axis=2).reshape(PARTS, -1, GATES)
        cuts = jnp.split(whole, [CONV_ROWS, CONV_ROWS + PART_ROWS], axis=1)
        sums = cls([jnp.concatenate([cut.reshape(2 ** len(pairs), -1, GATES) for cut in cuts], axis=1)], pairs)
        sums.halve()
        return sums

    def core(self, *gates):
        if self.parts is None:
            return self.step(*gates)
        goes, gates = tie([terms[0] for terms in self.state], gates)
        stays = [part.reshape(term.shape) for part, term in zip(self.parts, goes)]
        self.state = [[part, self.pairs[-1].shift(term, 1)] for part, term in zip(stays, goes)]
        self.at = 1
        return gates

    def join(self):
        parts = self.state if self.at == 1 else [[sum(terms)] for terms in self.state]
        axis = parts[0][0].ndim - 2
        self.state = [[jnp.concatenate(terms, axis=axis) for terms in zip(*parts)]]

    def halve(self):
        (terms,) = self.state
        half = terms[0].shape[-2] // 2
        self.state = [[term[..., :half, :] for term in terms], [term[..., half:, :] for term in terms]]
        ((*order,),) = self.orders
        self.orders = [order, order[:1] + order[2:0:-1] + order[3:]]
        self.left = [list(self.left[0]), list(self.left[0])]

    def step(self, *gates):
        for k, terms in enumerate(self.state):
            bit = self.orders[k][self.at]
            if self.at >= 3:
                terms = [sum(terms)]
            self.state[k], gates = hop(terms, self.pairs[bit], self.left[k].index(bit), gates)
            self.left[k].remove(bit)
        self.at += 1
        return gates

    def result(self):
        while self.at < len(self.pairs):
            self.step()
        (terms,) = self.state
        return sum(terms)


def beside(sums, work, *inputs):
    for rows in sums:
        inputs = rows.core(*inputs) if rows.at == 0 else rows.step(*inputs)
    out = work(*inputs)
    came, out = tie([[terms[-1] for terms in rows.state] for rows in sums], out)
    for rows, last in zip(sums, came):
        rows.state = [terms[:-1] + [term] for terms, term in zip(rows.state, last)]
    return out


def tie(*groups):
    leaves, tree = jax.tree.flatten(groups)
    return jax.tree.unflatten(tree, lax.optimization_barrier(leaves))


def exchange(*parts):
    devices = parts[0].shape[0]
    parts = [part.reshape(devices, -1) for part in parts]
    sizes = [part.shape[1] for part in parts]
    joined = jnp.concatenate(parts, axis=1)
    joined = jnp.pad(joined, ((0, 0), (0, -joined.shape[1] % 1024))).reshape(devices, -1, 128)
    came = lax.all_to_all(joined, AXIS, split_axis=0, concat_axis=0, tiled=True).reshape(devices, -1)
    out, start = [], 0
    for size in sizes:
        out.append(came[:, start : start + size])
        start += size
    return out


def to_all(part, devices):
    return jnp.broadcast_to(part.reshape(1, -1), (devices, part.size))


def regrouped(whole, share):
    sizes, start, pieces = (3 * share, share, share), 0, []
    for size in sizes:
        pieces.append(whole[:, start : start + size].reshape(PARTS, -1, GATES))
        start += size
    return jnp.concatenate(pieces, axis=1)


def by_column(part, devices):
    cut = part.reshape(part.shape[:-1] + (devices, -1))
    return jnp.moveaxis(cut, -2, 0).reshape(devices, -1)


def head_rows(row):
    head = jnp.arange(WIDTH, dtype=jnp.int32)[None, :] // HEAD_DIM
    own = head == jnp.arange(HEADS, dtype=jnp.int32)[:, None]
    return jnp.where(own, row, 0.0)


def exact_dot(left, right, left_dim=1, right_dim=0):
    return lax.dot_general(
        left, right, (((left_dim,), (right_dim,)), ((), ())), precision=HIGHEST, preferred_element_type=jnp.float32
    )


def split_dot(left, right, left_dim=1, right_dim=0):
    return three_dots(halves_of(left), halves_of(right), left_dim, right_dim)


def head_of(shape, dim, per_head):
    return lax.broadcasted_iota(jnp.int32, shape, dim) // per_head


def attention_back_kernel(
    grad_film, film_w, value_mixing, key_w, probs, keys, absorbed_out, query_out, row_out, mixed_out
):
    film = film_w[...].reshape(WIDTH, GATES)
    value = value_mixing[..., :WIDTH].reshape(WIDTH, WIDTH)
    mixing = value_mixing[..., WIDTH:].reshape(WIDTH, WIDTH)
    grad_mixed = split_dot(jnp.broadcast_to(grad_film[...], (16, GATES)), film, 1, 1)
    grad_row = split_dot(grad_mixed * (1.0 / QUERIES), mixing, 1, 1)
    mixed_out[...] = grad_mixed[:1]
    row_out[...] = grad_row[:1]
    own = head_of((16, WIDTH), 1, HEAD_DIM) == head_of((16, WIDTH), 0, 1)
    grad_pooled = split_dot(jnp.where(own, grad_row, 0.0), value, 1, 1)
    grad_probs = split_dot(grad_pooled, keys[...], 1, 1)
    prob = probs[0]
    weighted = prob * grad_probs[:HEADS][:, None, :]
    row_terms = jnp.sum(weighted, axis=2, keepdims=True)
    grad_scores = (weighted - prob * row_terms) * (1.0 / math.sqrt(HEAD_DIM))
    grad_scores = grad_scores.reshape(HEADS * QUERIES, -1)
    grad_absorbed = split_dot(grad_scores, keys[...])
    absorbed_out[...] = grad_absorbed.T
    grad_query = split_dot(grad_absorbed, key_w[0])
    shape = grad_query.shape
    grad_query = jnp.where(head_of(shape, 1, HEAD_DIM) == head_of(shape, 0, QUERIES), grad_query, 0.0)
    query_out[...] = jnp.sum(grad_query.reshape(HEADS, QUERIES, WIDTH), axis=0)


def attention_back(layer, grad_film, attention_whole, key_w, probs, keys):
    parts, _, _, rows, _ = attention_whole.shape
    count = keys.shape[0]

    def one(shape):
        return pl.BlockSpec((1,) + shape, lambda k: (layer,) + (0,) * len(shape))

    return kernel_call(
        attention_back_kernel,
        (1,),
        [
            fixed(1, GATES),
            pl.BlockSpec((parts, 1, 1, rows, GATES), lambda k: (0, layer, 0, 0, 0)),
            pl.BlockSpec((parts, 1, 1, rows, GATES), lambda k: (0, layer, 1, 0, 0)),
            one((WIDTH, WIDTH)),
            one((HEADS, QUERIES, count)),
            fixed(count, WIDTH),
        ],
        [fixed(WIDTH, HEADS * QUERIES), fixed(QUERIES, WIDTH), fixed(1, WIDTH), fixed(1, WIDTH)],
        [(WIDTH, HEADS * QUERIES), (QUERIES, WIDTH), (1, WIDTH), (1, WIDTH)],
        [],
        10 * WIDTH * HEADS * QUERIES * count // 4,
    )(grad_film, attention_whole, attention_whole, key_w, probs, keys)


def factor_kernel(
    rows, step_rows, pooled, means, mixeds, embeds, absorbed, query_rows, seeds, query_w,
    step_out, seeds_out, query_out, key_out, value_out, mixing_out, film_out, square_out,
):
    share = embeds.shape[1]
    at = {}
    start = 0
    for name, size in (("row", WIDTH), ("mixed", WIDTH), ("film", GATES)):
        for layer in range(LAYERS):
            at[name, layer] = rows[:, start : start + size]
            start += size
    for layer in range(LAYERS):
        at["step", layer] = step_rows[:, layer * WIDTH : (layer + 1) * WIDTH]
    square = jnp.zeros((1, 1), jnp.float32)
    own = head_of((HEADS, share, WIDTH), 2, HEAD_DIM) == head_of((HEADS, share, WIDTH), 0, 1)
    near = head_of((HEADS * QUERIES, WIDTH), 1, HEAD_DIM) == head_of((HEADS * QUERIES, WIDTH), 0, QUERIES)
    for layer in range(LAYERS):
        value = exact_dot(pooled[layer], at["row", layer], 0, 0).reshape(HEADS, share, WIDTH)
        spread = jnp.where(near, jnp.concatenate([query_rows[0, layer]] * HEADS, axis=0), 0.0)
        grads = (
            (step_out, exact_dot(embeds[...], at["step", layer], 0, 0)),
            (seeds_out, exact_dot(query_w[layer], query_rows[1, layer], 1, 1)),
            (query_out, exact_dot(seeds[layer], query_rows[1, layer])),
            (key_out, exact_dot(absorbed[layer], spread)),
            (value_out, QUERIES * jnp.sum(jnp.where(own, value, 0.0), axis=0)),
            (mixing_out, exact_dot(means[layer], at["mixed", layer], 0, 0)),
            (film_out, exact_dot(mixeds[layer], at["film", layer], 0, 0)),
        )
        for out, grad in grads:
            out[layer] = grad
            square = square + jnp.sum(jnp.sum(grad * grad, axis=1, keepdims=True), axis=0, keepdims=True)
    square_out[...] = square


def square_kernel(square, *refs):
    *sums, out = refs
    total = square[...]
    for part in sums:
        total = total + jnp.sum(jnp.sum(part[...] * part[...], axis=1, keepdims=True), axis=0, keepdims=True)
    out[...] = jnp.broadcast_to(total[None], out.shape)


def clip_kernel(squares, sums_0, sums_1, *refs):
    places = squares[:, 0, :1]
    norm_square = jnp.sum(places, axis=0, keepdims=True)
    factor = jnp.minimum(1.0, CLIP_NORM / jnp.sqrt(norm_square))
    count = (len(refs) - 3) // 2
    grads, outs = refs[:count], refs[count : 2 * count]
    conv_out, cond_out, out_out = refs[2 * count :]
    for grad, out in zip(grads, outs):
        for layer in range(LAYERS):
            out[layer] = grad[layer] * factor
    share = cond_out.shape[1]
    for layer, sums in enumerate((sums_0, sums_1)):
        conv_out[layer] = sums[: 3 * share] * factor
        cond_out[layer] = sums[3 * share : 4 * share] * factor
        out_out[layer] = sums[4 * share :] * factor


def shapes_of(*shapes):
    return [jax.ShapeDtypeStruct(shape, jnp.float32) for shape in shapes]


HALF = jnp.bfloat16
PARTS = 32
PLACES = (
    [(pair // 2 % 2) * 8 + pair % 2 * 4 + pair // 4 % 2 * 2 + pair // 8 for pair in range(PARTS // 2)],
    [pair % 2 * 8 + (pair // 2 % 2) * 4 + pair // 4 % 2 * 2 + pair // 8 for pair in range(PARTS // 2)],
)
CONV_ROWS, PART_ROWS = 3 * WIDTH // PARTS, WIDTH // PARTS
TILE = 256


def halves_of(array):
    high = array.astype(HALF)
    return high, (array - high.astype(jnp.float32)).astype(HALF)


def three_dots(left, right, left_dim, right_dim):
    def dot(one, other):
        dims = (((left_dim,), (right_dim,)), ((), ()))
        return lax.dot_general(one, other, dims, preferred_element_type=jnp.float32)

    return dot(left[0], right[0]) + (dot(left[0], right[1]) + dot(left[1], right[0]))


def tile_of(pair, start, dim, size=TILE):
    return tuple(lax.slice_in_dim(half, start, start + size, axis=dim) for half in pair)


def moved(rows, steps):
    count = rows.shape[0]
    place = lax.broadcasted_iota(jnp.int32, rows.shape, 0) - steps
    return jnp.where((place >= 0) & (place < count), pltpu.roll(rows, steps % count, 0), 0.0)


def shape_of(*sizes):
    dtype = jnp.float32 if isinstance(sizes[-1], int) else sizes[-1]
    return jax.ShapeDtypeStruct(tuple(size for size in sizes if isinstance(size, int)), dtype)


def kernel_call(kernel, grid, in_specs, out_specs, out_shapes, scratch, macs, mebibytes=52):
    return pl.pallas_call(
        kernel,
        grid=grid,
        in_specs=in_specs,
        out_specs=out_specs,
        out_shape=[shape_of(*shape) for shape in out_shapes],
        scratch_shapes=scratch,
        compiler_params=pltpu.CompilerParams(vmem_limit_bytes=mebibytes * 2**20),
        cost_estimate=pl.CostEstimate(flops=1 * macs, bytes_accessed=16 * 2**20, transcendentals=0),
    )


def fixed(*shape):
    return pl.BlockSpec(shape, lambda k: (0,) * len(shape))


def part_rows(size, at):
    return pl.BlockSpec((PARTS, size, GATES), lambda k: (0, at, 0))


CONV_SPEC = pl.BlockSpec((PARTS // 2, CONV_ROWS, GATES), lambda k: (jnp.minimum(k, 1), 0, 0))
COND_SPEC = part_rows(PART_ROWS, 3)
OUT_SPEC = part_rows(PART_ROWS, 4)


def gates_kernel(dilation, frames, cond, conv_w, cond_w, step_row, live, tanh, sig, total):
    k = pl.program_id(0)

    def add(left, right, first):
        for start in range(0, GATES, TILE):
            part = three_dots(left, tile_of(right, start, 1), 1, 0)
            total[:, start : start + TILE] = part if first else total[:, start : start + TILE] + part

    @pl.when(k == 0)
    def _():
        hidden = (frames[...] + step_row[...]) * live[...]
        taps = jnp.concatenate([moved(hidden, dilation), hidden[:, : WIDTH // 2]], axis=1)
        add(halves_of(taps), halves_of(conv_w[...].reshape(-1, GATES)), True)

    @pl.when(k == 1)
    def _():
        hidden = (frames[...] + step_row[...]) * live[...]
        taps = jnp.concatenate([hidden[:, WIDTH // 2 :], moved(hidden, -dilation)], axis=1)
        add(halves_of(taps), halves_of(conv_w[...].reshape(-1, GATES)), False)

    @pl.when(k == 2)
    def _():
        left, right = halves_of(cond[...]), halves_of(cond_w[...].reshape(-1, GATES))
        for start in range(0, WIDTH, TILE):
            part = three_dots(left, tile_of(right, start, 1), 1, 0)
            tanh[:, start : start + TILE] = jnp.tanh(total[:, start : start + TILE] + part)
        for start in range(0, WIDTH, TILE):
            part = three_dots(left, tile_of(right, WIDTH + start, 1), 1, 0)
            sig[:, start : start + TILE] = jax.nn.sigmoid(total[:, WIDTH + start : WIDTH + start + TILE] + part)


def layer_gates(whole, frames, cond, step_row, live, dilation):
    count = frames.shape[0]
    return kernel_call(
        functools.partial(gates_kernel, dilation),
        (3,),
        [fixed(count, WIDTH)] * 2 + [CONV_SPEC, COND_SPEC, fixed(1, WIDTH), fixed(count, 1)],
        [fixed(count, WIDTH)] * 2,
        [(count, WIDTH)] * 2,
        [pltpu.VMEM((count, GATES), jnp.float32)],
        4 * count * WIDTH * GATES,
    )(frames, cond, whole, whole, step_row, live)


def post_kernel(tanh, sig, film, out_w, frames, skip, live, frames_next, skip_next, high, low):
    @pl.when(pl.program_id(0) == 0)
    def _():
        high[...], low[...] = halves_of(out_w[...].reshape(-1, GATES))

    modulated = halves_of(tanh[...] * sig[...] * (1.0 + film[:1]) + film[1:])
    for start in range(0, WIDTH, TILE):
        cut = slice(start, start + TILE)
        post = three_dots(modulated, (high[:, cut], low[:, cut]), 1, 0)
        frames_next[:, cut] = (frames[:, cut] + post) * (live[...] * ROOT_HALF)
    for start in range(0, WIDTH, TILE):
        cut, far = slice(start, start + TILE), slice(WIDTH + start, WIDTH + start + TILE)
        post = three_dots(modulated, (high[:, far], low[:, far]), 1, 0)
        skip_next[:, cut] = skip[:, cut] + post * live[...]


def layer_post(whole, tanh, sig, film, frames, skip, live):
    count = frames.shape[0]
    rows = pl.BlockSpec((count // 2, WIDTH), lambda k: (k, 0))
    return kernel_call(
        post_kernel,
        (2,),
        [rows, rows, fixed(2, WIDTH), OUT_SPEC, rows, rows, pl.BlockSpec((count // 2, 1), lambda k: (k, 0))],
        [rows, rows],
        [(count, WIDTH)] * 2,
        [pltpu.VMEM((WIDTH, GATES), HALF)] * 2,
        count * WIDTH * GATES,
    )(tanh, sig, film.reshape(2, WIDTH), whole, frames, skip, live)


def back_gates_kernel(
    grad_frames, grad_skip, live, tanh, sig, film, out_w, pre_high, pre_low, grad_film, grad_out, high, low
):
    k = pl.program_id(0)

    @pl.when(k == 0)
    def _():
        high[...], low[...] = halves_of(out_w[...].reshape(-1, GATES))
        grad_film[...] = jnp.zeros_like(grad_film)

    post = jnp.concatenate([grad_frames[...] * (live[...] * ROOT_HALF), grad_skip[...] * live[...]], axis=1)
    post = halves_of(post)
    for start in range(0, WIDTH, TILE):
        cut, far = slice(start, start + TILE), slice(WIDTH + start, WIDTH + start + TILE)
        grad_mod = three_dots(post, (high[cut, :], low[cut, :]), 1, 1)
        t, s = tanh[:, cut], sig[:, cut]
        gate = t * s
        grad_film[0:1, cut] += jnp.sum(grad_mod * gate, axis=0, keepdims=True)
        grad_film[1:2, cut] += jnp.sum(grad_mod, axis=0, keepdims=True)
        grad_gate = grad_mod * (1.0 + film[:1, cut])
        pre_high[:, cut], pre_low[:, cut] = halves_of(grad_gate * (s * (1.0 - t * t)))
        pre_high[:, far], pre_low[:, far] = halves_of(grad_gate * (gate * (1.0 - s)))
    modulated = tanh[...] * sig[...] * (1.0 + film[:1]) + film[1:]
    modulated = halves_of(modulated.T)

    @pl.when(k == 0)
    def _():
        for start in range(0, GATES, TILE):
            grad_out[:, start : start + TILE] = three_dots(modulated, tile_of(post, start, 1), 1, 0)

    @pl.when(k > 0)
    def _():
        for start in range(0, GATES, TILE):
            grad_out[:, start : start + TILE] += three_dots(modulated, tile_of(post, start, 1), 1, 0)


def layer_back_gates(whole, tanh, sig, film, grad_frames, grad_skip, live):
    count = tanh.shape[0]
    rows = pl.BlockSpec((count // 2, WIDTH), lambda k: (k, 0))
    return kernel_call(
        back_gates_kernel,
        (2,),
        [rows, rows, pl.BlockSpec((count // 2, 1), lambda k: (k, 0)), rows, rows, fixed(2, WIDTH), OUT_SPEC],
        [pl.BlockSpec((count // 2, GATES), lambda k: (k, 0))] * 2 + [fixed(2, WIDTH), fixed(WIDTH, GATES)],
        [(count, GATES, HALF)] * 2 + [(2, WIDTH), (WIDTH, GATES)],
        [pltpu.VMEM((WIDTH, GATES), HALF)] * 2,
        2 * count * WIDTH * GATES,
    )(grad_frames, grad_skip, live, tanh, sig, film.reshape(2, WIDTH), whole)


def back_weights_kernel(
    dilation, core, frames, cond, step_row, live, pre_high, pre_low, grad_out,
    top_stays, low_stays, top_goes, low_goes, high, low, conv_rows, cond_rows,
):
    @pl.when(pl.program_id(0) == 0)
    def _():
        hidden = ((frames[...] + step_row[...]) * live[...]).T
        count = hidden.shape[1]
        for tap, steps in enumerate((dilation, 0, -dilation)):
            moved_rows = hidden
            if steps:
                place = lax.broadcasted_iota(jnp.int32, hidden.shape, 1) - steps
                moved_rows = pltpu.roll(hidden, steps % count, 1)
                moved_rows = jnp.where((place >= 0) & (place < count), moved_rows, 0.0)
            cut = slice(tap * WIDTH, (tap + 1) * WIDTH)
            high[cut, :], low[cut, :] = halves_of(moved_rows)
        cut = slice(3 * WIDTH, 4 * WIDTH)
        high[cut, :], low[cut, :] = halves_of(cond[...].T)

    grad = (pre_high[...], pre_low[...])
    for start in range(0, 4 * WIDTH, 2 * TILE):
        cut = slice(start, start + 2 * TILE)
        part = three_dots((high[cut, :], low[cut, :]), grad, 1, 0)
        if start < 3 * WIDTH:
            conv_rows[cut, :] = part
        else:
            cond_rows[start - 3 * WIDTH : start - 3 * WIDTH + 2 * TILE, :] = part
    half = top_goes.shape[1]
    rest = CONV_ROWS - half
    for top_out, low_out, parity in ((top_stays, low_stays, core[0]), (top_goes, low_goes, 1 - core[0])):
        for pair in range(PARTS // 2):
            part = 2 * pair + parity
            rows = pl.multiple_of(part * CONV_ROWS, 8)
            top_out[PLACES[0][pair]] = conv_rows[pl.ds(rows, half), :]
            place = PLACES[1][pair]
            low_out[place, :rest, :] = conv_rows[pl.ds(rows + half, rest), :]
            rows = pl.multiple_of(part * PART_ROWS, 8)
            low_out[place, rest : rest + PART_ROWS, :] = cond_rows[pl.ds(rows, PART_ROWS), :]
            low_out[place, rest + PART_ROWS :, :] = grad_out[pl.ds(rows, PART_ROWS), :]


def layer_back_weights(core, frames, cond, step_row, live, grad_pre, grad_out, dilation):
    count = frames.shape[0]
    part = (PARTS // 2, (CONV_ROWS + 2 * PART_ROWS) // 2)
    columns = pl.BlockSpec(part + (TILE,), lambda k: (0, 0, k))
    return kernel_call(
        functools.partial(back_weights_kernel, dilation),
        (GATES // TILE,),
        [pl.BlockSpec(memory_space=pltpu.SMEM)]
        + [fixed(count, WIDTH)] * 2
        + [fixed(1, WIDTH), fixed(count, 1)]
        + [pl.BlockSpec((rows, TILE), lambda k: (0, k)) for rows in (count, count, WIDTH)],
        [columns] * 4,
        [part + (GATES,)] * 4,
        [pltpu.VMEM((4 * WIDTH, count), HALF)] * 2
        + [pltpu.VMEM((rows, TILE), jnp.float32) for rows in (3 * WIDTH, WIDTH)],
        4 * count * WIDTH * GATES,
    )(core, frames, cond, step_row, live, *grad_pre, grad_out)


def back_frames_kernel(dilation, pre_high, pre_low, conv_w, grad_frames, live, grad_next, step_sum, total):
    k = pl.program_id(0)
    middle = WIDTH // 2
    grad, weight = (pre_high[...], pre_low[...]), halves_of(conv_w[...].reshape(-1, GATES))

    def taps(start):
        return three_dots(grad, tile_of(weight, start, 0), 1, 1)

    @pl.when(k == 0)
    def _():
        for start in range(0, WIDTH, TILE):
            total[:, start : start + TILE] = moved(taps(start), -dilation)
        total[:, :middle] += taps(WIDTH)

    @pl.when(k == 1)
    def _():
        total[:, middle:] += taps(0)
        for start in range(0, WIDTH, TILE):
            cut = slice(start, start + TILE)
            hidden = (total[:, cut] + moved(taps(middle + start), dilation)) * live[...]
            step_sum[:, cut] = jnp.sum(hidden, axis=0, keepdims=True)
            grad_next[:, cut] = grad_frames[:, cut] * (live[...] * ROOT_HALF) + hidden


def layer_back_frames(whole, grad_pre, grad_frames, live, dilation):
    count = grad_pre[0].shape[0]
    return kernel_call(
        functools.partial(back_frames_kernel, dilation),
        (2,),
        [fixed(count, GATES)] * 2 + [CONV_SPEC, fixed(count, WIDTH), fixed(count, 1)],
        [fixed(count, WIDTH), fixed(1, WIDTH)],
        [(count, WIDTH), (1, WIDTH)],
        [pltpu.VMEM((count, WIDTH), jnp.float32)],
        3 * count * WIDTH * GATES,
    )(*grad_pre, whole, grad_frames, live)


def on_device(
    frames_in,
    conditioning,
    prompt,
    item_lengths,
    prompt_lengths,
    key_mask,
    diffusion_steps,
    step_proj,
    conv_weight,
    cond_proj,
    out_proj,
    query_seeds,
    query_proj,
    key_proj,
    value_proj,
    mixing_proj,
    film_proj,
    cot_frames,
    cot_skip,
    devices,
):
    rings, pairs = rings_of(devices), pairs_of(devices)
    share = step_proj.shape[1]
    key_count = prompt.shape[1]
    extra_size = key_count + LAYERS * share * QUERIES
    extra_rows = -(-(extra_size + 1) // WIDTH)
    key_rows = -(-(key_count + extra_rows) // 8) * 8
    me = lax.axis_index(AXIS)

    frame_packs = [
        jnp.concatenate([conv_weight[layer], cond_proj[layer], out_proj[layer]], axis=0) for layer in range(LAYERS)
    ]
    frame_whole_0 = lax.all_gather(frame_packs[0], AXIS, axis=0, tiled=False)

    extra = (
        key_mask.astype(jnp.float32),
        to_all(query_seeds, devices),
        to_all(diffusion_steps.astype(jnp.float32), devices),
    )
    extra = jnp.concatenate(extra, axis=1)
    extra = jnp.pad(extra, ((0, 0), (0, (key_rows - key_count) * WIDTH - extra.shape[1])))
    sent = jnp.concatenate([prompt, extra.reshape(prompt.shape[0], -1, WIDTH)], axis=1)
    query_key = jnp.concatenate([query_proj, key_proj], axis=2).reshape(LAYERS * share, GATES)
    query_key, sent = tie(query_key, sent)
    keys = lax.all_to_all(sent, AXIS, split_axis=0, concat_axis=0, tiled=True)
    extra = keys[:, key_count : key_count + extra_rows].reshape(devices, -1)
    key_place = (
        jnp.arange(devices, dtype=jnp.int32)[:, None] * key_count
        + jnp.arange(key_rows, dtype=jnp.int32)[None, :]
    )
    masked_in = jnp.pad(extra[:, :key_count], ((0, 0), (0, key_rows - key_count)))
    live_keys = (
        (jnp.arange(key_rows, dtype=jnp.int32)[None, :] < key_count)
        & (key_place < lax.dynamic_index_in_dim(prompt_lengths, me, 0, keepdims=False))
        & ((masked_in == 1.0) | (key_place == 0))
    ).reshape(-1)
    seeds = extra[:, key_count:extra_size]
    seeds = jnp.moveaxis(seeds.reshape(devices, LAYERS, share, QUERIES), 1, 0)
    seeds = seeds.reshape(LAYERS, WIDTH, QUERIES)
    keys = keys.reshape(-1, WIDTH)

    embeds = jax.vmap(step_embedding)(extra[:, extra_size])
    own_embeds = lax.dynamic_slice_in_dim(embeds, me * share, share, 1)
    step_part = jnp.einsum("bw,lwx->blx", own_embeds, step_proj, precision=HIGHEST)

    query_key = gather_rows(query_key, rings).reshape(devices, LAYERS, share, GATES)
    query_key = jnp.moveaxis(query_key, 1, 0).reshape(LAYERS, WIDTH, GATES)
    query_rows = jnp.einsum("lwq,lwx->lqx", seeds, query_key[:, :, :WIDTH], precision=HIGHEST)
    query_heads = query_rows.reshape(LAYERS, QUERIES, HEADS, HEAD_DIM)
    key_heads = query_key[:, :, WIDTH:].reshape(LAYERS, WIDTH, HEADS, HEAD_DIM)
    absorbed = jnp.einsum("lqhe,lwhe->lhqw", query_heads, key_heads, precision=HIGHEST)
    absorbed = absorbed.reshape(LAYERS * HEADS * QUERIES, WIDTH) / math.sqrt(HEAD_DIM)

    scores = jnp.where(live_keys[None, :], small_dot(absorbed, keys, 1, 1), -1e30)
    exps = jnp.exp(scores - jnp.max(scores, axis=1, keepdims=True))
    probs = exps / jnp.sum(exps, axis=1, keepdims=True)
    probs = probs.reshape(LAYERS, HEADS, QUERIES, -1)
    pooled = jnp.mean(probs, axis=2).reshape(LAYERS * HEADS, -1)
    pooled_keys = small_dot(pooled, keys)

    frame_pack_1, frame_whole_0, pooled_keys = tie(frame_packs[1], frame_whole_0, pooled_keys)
    frame_whole_1 = lax.all_gather(frame_pack_1, AXIS, axis=0, tiled=False)

    pooled_cut, step_rows = exchange(by_column(pooled_keys, devices), step_part)
    step_rows = jnp.sum(step_rows, axis=0).reshape(LAYERS, 1, WIDTH)
    pooled_cut = pooled_cut.reshape(devices, LAYERS, HEADS, share)
    pooled_cut, frame_whole_0, frames_in, conditioning = tie(pooled_cut, frame_whole_0, frames_in, conditioning)
    value_heads = value_proj.reshape(LAYERS, share, HEADS, HEAD_DIM)
    mean_part = jnp.einsum("blhw,lwhe->blhe", pooled_cut, value_heads, precision=HIGHEST)
    (mean_cut,) = exchange(by_column(mean_part.reshape(devices, LAYERS, WIDTH), devices))
    mean_cut = jnp.sum(mean_cut, axis=0).reshape(devices, LAYERS, share)
    mixed_part = jnp.einsum("blw,lwx->blx", mean_cut, mixing_proj, precision=HIGHEST)
    (mixed_cut,) = exchange(by_column(mixed_part, devices))
    mixed_cut = jnp.sum(mixed_cut, axis=0).reshape(devices, LAYERS, share)
    film_part = jnp.einsum("blw,lwx->blx", mixed_cut, film_proj, precision=HIGHEST)
    (films,) = exchange(film_part)
    films = jnp.sum(films, axis=0).reshape(LAYERS, 1, GATES)
    films, cot_frames, cot_skip = tie(films, cot_frames, cot_skip)

    live = (jnp.arange(frames_in.shape[1], dtype=jnp.int32) < item_lengths[0]).astype(jnp.float32)[:, None]
    frames, cond, cot, cot_last = frames_in[0], conditioning[0], cot_frames[0], cot_skip[0]
    if devices != PARTS:
        frame_whole_0 = regrouped(frame_whole_0, share)
    tanh_0, sig_0 = layer_gates(frame_whole_0, frames, cond, step_rows[0], live, 1)
    frames_1, skip = layer_post(frame_whole_0, tanh_0, sig_0, films[0], frames, jnp.zeros_like(frames), live)

    attention_pack = jnp.concatenate(
        [
            part
            for layer in range(LAYERS)
            for part in (film_proj[layer], jnp.concatenate([value_proj[layer], mixing_proj[layer]], axis=1))
        ],
        axis=0,
    )
    attention_pack, frame_whole_1, frames_1 = tie(attention_pack, frame_whole_1, frames_1)
    attention_whole = lax.all_gather(attention_pack, AXIS, axis=0, tiled=False)
    attention_whole = attention_whole.reshape(devices, LAYERS, 2, share, GATES)
    if devices != PARTS:
        attention_whole = jnp.transpose(attention_whole, (1, 2, 0, 3, 4)).reshape(1, LAYERS, 2, WIDTH, GATES)
        frame_whole_1 = regrouped(frame_whole_1, share)

    tanh_1, sig_1 = layer_gates(frame_whole_1, frames_1, cond, step_rows[1], live, 2)

    def by_device(grad):
        return grad.reshape(devices, -1, GATES)

    def by_share(grad):
        return grad.reshape(devices, share, -1)

    core = (me % 2 if devices == PARTS else jnp.zeros_like(me)).astype(jnp.int32).reshape(1)
    *grad_pre_1, grad_film_1, grad_out = layer_back_gates(frame_whole_1, tanh_1, sig_1, films[1], cot, cot_last, live)
    parts = layer_back_weights(core, frames_1, cond, step_rows[1], live, grad_pre_1, grad_out, 2)
    sum_1 = RowSum.of_parts(*parts, pairs)

    def post_1(tanh, sig, grad_pre):
        return layer_post(frame_whole_1, tanh, sig, films[1], frames_1, skip, live), grad_pre

    (frames, skip), grad_pre_1 = beside([sum_1], post_1, tanh_1, sig_1, grad_pre_1)

    def frames_and_gates(grad_pre):
        grad_frames, step_sum = layer_back_frames(frame_whole_1, grad_pre, cot, live, 2)
        gates = layer_back_gates(frame_whole_0, tanh_0, sig_0, films[0], grad_frames, cot_last, live)
        return grad_frames, step_sum, *gates

    grad_frames, step_sum_1, *grad_pre_0, grad_film_0, grad_out = beside([sum_1], frames_and_gates, grad_pre_1)

    def weights_0(grad_pre):
        return layer_back_weights(core, frames_in[0], cond, step_rows[0], live, grad_pre, grad_out, 1), grad_pre

    parts, grad_pre_0 = beside([sum_1], weights_0, grad_pre_0)
    sum_1.join()
    sum_b = RowSum.of_parts(*parts, pairs)
    key_w = query_key[:, :, WIDTH:]

    def attention_1(grad_film):
        return attention_back(1, grad_film, attention_whole, key_w, probs, keys)

    grad_film_0, grad_film_1 = grad_film_0.reshape(1, GATES), grad_film_1.reshape(1, GATES)
    absorbed_1, query_1, row_1, mixed_1 = beside([sum_b, sum_1], attention_1, grad_film_1)

    def attention_and_frames(grad_film, grad_pre):
        attention = attention_back(0, grad_film, attention_whole, key_w, probs, keys)
        return *attention, *layer_back_frames(frame_whole_0, grad_pre, grad_frames, live, 1)

    absorbed_0, query_0, row_0, mixed_0, grad_frames, step_sum_0 = beside(
        [sum_b, sum_1], attention_and_frames, grad_film_0, grad_pre_0
    )
    sum_d = RowSum([by_share(absorbed_0), by_share(absorbed_1)], pairs, far_first=True)
    sum_d.step()
    query_parts = jnp.stack([query_0, query_1]).reshape(devices, -1)
    first_rows = jnp.concatenate(
        [part.reshape(-1) for part in (row_0, row_1, mixed_0, mixed_1, grad_film_0, grad_film_1)]
    )
    query_cut, first_rows = beside([sum_d, sum_b], exchange, query_parts, to_all(first_rows, devices))
    (query_cut,) = sum_d.step(jnp.sum(query_cut, axis=0))
    sum_b.join()
    last_rows = jnp.concatenate([part.reshape(-1) for part in (step_sum_0, step_sum_1, query_cut)])
    (last_rows,) = beside([sum_b], exchange, to_all(last_rows, devices))
    (sum_d.state,) = sum_b.step(sum_d.state)
    while sum_d.at < len(pairs):
        sum_d.step()
    sum_d.join()
    query_grads = last_rows[:, LAYERS * WIDTH :].reshape(LAYERS, QUERIES, WIDTH)
    absorbed_sums = sum_d.result().reshape(LAYERS, share, HEADS * QUERIES)

    small = [(LAYERS, share, columns) for columns in (WIDTH, QUERIES, WIDTH, WIDTH, WIDTH, WIDTH, GATES)]
    *factored, square = pl.pallas_call(factor_kernel, out_shape=shapes_of(*small, (1, 1)))(
        first_rows,
        last_rows[:, : LAYERS * WIDTH],
        jnp.moveaxis(pooled_cut.reshape(devices, LAYERS, HEADS * share), 1, 0),
        jnp.moveaxis(mean_cut, 1, 0),
        jnp.moveaxis(mixed_cut, 1, 0),
        own_embeds,
        absorbed_sums,
        jnp.stack([query_rows, query_grads]),
        query_seeds,
        query_proj,
    )
    frame_sums = (sum_b.result(), sum_1.result())
    squares = pl.pallas_call(square_kernel, out_shape=shapes_of((devices, 8, 128))[0])(square, *frame_sums)
    squares = lax.all_to_all(squares, AXIS, split_axis=0, concat_axis=0, tiled=True)
    frame_shapes = [(LAYERS, rows_of * share, GATES) for rows_of in (3, 1, 1)]
    outs = pl.pallas_call(clip_kernel, out_shape=shapes_of(*small, *frame_shapes))(squares, *frame_sums, *factored)
    step_grad, seeds_grad, query_grad, key_grad, value_grad, mixing_grad, film_grad, conv_grad, cond_grad, out_grad = outs
    return (
        frames[None],
        skip[None],
        grad_frames[None],
        step_grad,
        conv_grad,
        cond_grad,
        out_grad,
        seeds_grad,
        query_grad,
        key_grad,
        value_grad,
        mixing_grad,
        film_grad,
    )


def solution(mesh):
    devices = mesh.shape[AXIS]

    def run(*args):
        return on_device(*args, devices=devices)

    items, rows = P(AXIS, None, None), P(None, AXIS, None)
    return jax.shard_map(
        run,
        mesh=mesh,
        in_specs=(items, items, rows, P(AXIS), P(), P(None, AXIS), P(AXIS)) + (rows,) * 10 + (items, items),
        out_specs=(items,) * 3 + (rows,) * 10,
        check_vma=False,
    )
```

```python
import functools
import math

import jax
import jax.numpy as jnp
from jax import lax
from jax.experimental import pallas as pl
from jax.experimental.pallas import tpu as pltpu
from jax.sharding import PartitionSpec as P

WIDTH = 512
GATES = 2 * WIDTH
HEADS = 8
HEAD_DIM = WIDTH // HEADS
QUERIES = 32
LAYERS = 2
CLIP_NORM = 1.0
AXIS = "items"
HIGH = lax.Precision.HIGH
HIGHEST = lax.Precision.HIGHEST
ROOT_HALF = math.sqrt(0.5)


def big_dot(left, right, left_dim=1, right_dim=0):
    return lax.dot_general(left, right, (((left_dim,), (right_dim,)), ((), ())), precision=HIGH)


def small_dot(left, right, left_dim=1, right_dim=0):
    return lax.dot_general(left, right, (((left_dim,), (right_dim,)), ((), ())), precision=HIGHEST)


def step_embedding(diffusion_step):
    half_width = WIDTH // 2
    ramp = jnp.arange(half_width, dtype=jnp.int32).astype(jnp.float32) / (half_width - 1)
    angles = diffusion_step.astype(jnp.float32) / 1000.0 * jnp.exp(ramp * math.log(100.0))
    return jnp.concatenate([jnp.sin(angles), jnp.cos(angles)])


class Ring:
    def __init__(self, count, size, stride):
        self.count, self.size, self.stride = count, size, stride
        self.digit = (lax.axis_index(AXIS) // stride) % size

    def shift(self, block, steps):
        perm = []
        for device in range(self.count):
            digit = (device // self.stride) % self.size
            target = (digit + steps) % self.size
            perm.append((device, device + (target - digit) * self.stride))
        return lax.ppermute(block, AXIS, perm)

    def gather(self, block):
        if self.size == 1:
            return block[None]
        others = [self.shift(block, steps) for steps in range(1, self.size)]
        if self.size == 2:
            first = jnp.where(self.digit == 0, block, others[0])
            second = jnp.where(self.digit == 0, others[0], block)
            return jnp.stack([first, second])
        out = jnp.broadcast_to(block, (self.size,) + block.shape)
        for steps, other in enumerate(others, 1):
            place = (self.digit - steps) % self.size
            out = lax.dynamic_update_index_in_dim(out, other, place, 0)
        return out

    def scatter_sum(self, blocks, dim):
        own = lax.dynamic_index_in_dim(blocks, self.digit, dim, keepdims=False)
        for steps in range(1, self.size):
            place = (self.digit + steps) % self.size
            own = own + self.shift(lax.dynamic_index_in_dim(blocks, place, dim, keepdims=False), steps)
        return own


def rings_of(count):
    bits = (count // 2).bit_length() - 1
    sizes = [2 ** ((bits + 2) // 3), 2 ** ((bits + 1) // 3), 2 ** (bits // 3), 2]
    rings, stride = [], count
    for size in sizes:
        stride //= size
        rings.append(Ring(count, size, stride))
    return rings


def pairs_of(count):
    return [Ring(count, 2, 2**bit) for bit in reversed(range(count.bit_length() - 1))]


def gather_rows(shard, rings):
    far, mid, near, core = rings
    rows, columns = shard.shape
    half = rows // 2
    block = far.gather(shard)
    top = mid.gather(near.gather(block[:, :half]))
    low = near.gather(mid.gather(block[:, half:]))
    top = jnp.transpose(top, (2, 0, 1, 3, 4))
    low = jnp.transpose(low, (2, 1, 0, 3, 4))
    rail = jnp.concatenate([top, low], axis=3)
    both = core.gather(rail)
    return jnp.transpose(both, (1, 2, 3, 0, 4, 5)).reshape(-1, rows, columns)


def hop(terms, ring, dim, gates=()):
    def pick(place):
        return [lax.dynamic_index_in_dim(term, place, dim, keepdims=False) for term in terms]

    goes, gates = tie(sum(pick(1 - ring.digit)), gates) if gates else (sum(pick(1 - ring.digit)), gates)
    return pick(ring.digit) + [ring.shift(goes, 1)], gates


class RowSum:
    parts = None

    def __init__(self, arrays, pairs, far_first=False):
        count = len(pairs)
        self.pairs, self.at, bits = pairs, 0, list(range(count))
        self.orders = []
        for k in range(len(arrays)):
            near = bits[-3:-1] if k % 2 == 0 else bits[-3:-1][::-1]
            far = bits[:-3][::-1]
            self.orders.append(bits[-1:] + (far + near if far_first else near + far))
        self.left = [list(bits) for _ in arrays]
        self.state = [[array.reshape((2,) * count + array.shape[1:])] for array in arrays]

    @classmethod
    def of_parts(cls, top_stays, low_stays, top_goes, low_goes, pairs):
        if PARTS == 2 ** len(pairs):
            sums = cls([top_goes, low_goes], pairs[:-1])
            sums.parts, sums.pairs = (top_stays, low_stays), pairs
            count = len(pairs)
            sums.orders = [[count - 1, count - 3, count - 2, 1, 0], [count - 1, count - 2, count - 3, 1, 0]]
            sums.left = [order[1:] for order in sums.orders]
            return sums
        halves = (
            [jnp.stack([half[place] for place in places]) for half in pair]
            for pair, places in zip(((top_stays, top_goes), (low_stays, low_goes)), PLACES)
        )
        whole = jnp.concatenate([jnp.stack(pair, axis=1) for pair in halves], axis=2).reshape(PARTS, -1, GATES)
        cuts = jnp.split(whole, [CONV_ROWS, CONV_ROWS + PART_ROWS], axis=1)
        sums = cls([jnp.concatenate([cut.reshape(2 ** len(pairs), -1, GATES) for cut in cuts], axis=1)], pairs)
        sums.halve()
        return sums

    def core(self, *gates):
        if self.parts is None:
            return self.step(*gates)
        goes, gates = tie([terms[0] for terms in self.state], gates)
        stays = [part.reshape(term.shape) for part, term in zip(self.parts, goes)]
        self.state = [[part, self.pairs[-1].shift(term, 1)] for part, term in zip(stays, goes)]
        self.at = 1
        return gates

    def join(self):
        parts = self.state if self.at == 1 else [[sum(terms)] for terms in self.state]
        axis = parts[0][0].ndim - 2
        self.state = [[jnp.concatenate(terms, axis=axis) for terms in zip(*parts)]]

    def halve(self):
        (terms,) = self.state
        half = terms[0].shape[-2] // 2
        self.state = [[term[..., :half, :] for term in terms], [term[..., half:, :] for term in terms]]
        ((*order,),) = self.orders
        self.orders = [order, order[:1] + order[2:0:-1] + order[3:]]
        self.left = [list(self.left[0]), list(self.left[0])]

    def step(self, *gates):
        for k, terms in enumerate(self.state):
            bit = self.orders[k][self.at]
            if self.at >= 3:
                terms = [sum(terms)]
            self.state[k], gates = hop(terms, self.pairs[bit], self.left[k].index(bit), gates)
            self.left[k].remove(bit)
        self.at += 1
        return gates

    def result(self):
        while self.at < len(self.pairs):
            self.step()
        (terms,) = self.state
        return sum(terms)


def beside(sums, work, *inputs):
    for rows in sums:
        inputs = rows.core(*inputs) if rows.at == 0 else rows.step(*inputs)
    out = work(*inputs)
    came, out = tie([[terms[-1] for terms in rows.state] for rows in sums], out)
    for rows, last in zip(sums, came):
        rows.state = [terms[:-1] + [term] for terms, term in zip(rows.state, last)]
    return out


def tie(*groups):
    leaves, tree = jax.tree.flatten(groups)
    return jax.tree.unflatten(tree, lax.optimization_barrier(leaves))


def exchange(*parts):
    devices = parts[0].shape[0]
    parts = [part.reshape(devices, -1) for part in parts]
    sizes = [part.shape[1] for part in parts]
    joined = jnp.concatenate(parts, axis=1)
    joined = jnp.pad(joined, ((0, 0), (0, -joined.shape[1] % 1024))).reshape(devices, -1, 128)
    came = lax.all_to_all(joined, AXIS, split_axis=0, concat_axis=0, tiled=True).reshape(devices, -1)
    out, start = [], 0
    for size in sizes:
        out.append(came[:, start : start + size])
        start += size
    return out


def to_all(part, devices):
    return jnp.broadcast_to(part.reshape(1, -1), (devices, part.size))


def regrouped(whole, share):
    sizes, start, pieces = (3 * share, share, share), 0, []
    for size in sizes:
        pieces.append(whole[:, start : start + size].reshape(PARTS, -1, GATES))
        start += size
    return jnp.concatenate(pieces, axis=1)


def by_column(part, devices):
    cut = part.reshape(part.shape[:-1] + (devices, -1))
    return jnp.moveaxis(cut, -2, 0).reshape(devices, -1)


def head_rows(row):
    head = jnp.arange(WIDTH, dtype=jnp.int32)[None, :] // HEAD_DIM
    own = head == jnp.arange(HEADS, dtype=jnp.int32)[:, None]
    return jnp.where(own, row, 0.0)


def exact_dot(left, right, left_dim=1, right_dim=0):
    return lax.dot_general(
        left, right, (((left_dim,), (right_dim,)), ((), ())), precision=HIGHEST, preferred_element_type=jnp.float32
    )


def split_dot(left, right, left_dim=1, right_dim=0):
    return three_dots(halves_of(left), halves_of(right), left_dim, right_dim)


def head_of(shape, dim, per_head):
    return lax.broadcasted_iota(jnp.int32, shape, dim) // per_head


def attention_back_kernel(
    grad_film, film_w, value_mixing, key_w, probs, keys, absorbed_out, query_out, row_out, mixed_out
):
    film = film_w[...].reshape(WIDTH, GATES)
    value = value_mixing[..., :WIDTH].reshape(WIDTH, WIDTH)
    mixing = value_mixing[..., WIDTH:].reshape(WIDTH, WIDTH)
    grad_mixed = split_dot(jnp.broadcast_to(grad_film[...], (16, GATES)), film, 1, 1)
    grad_row = split_dot(grad_mixed * (1.0 / QUERIES), mixing, 1, 1)
    mixed_out[...] = grad_mixed[:1]
    row_out[...] = grad_row[:1]
    own = head_of((16, WIDTH), 1, HEAD_DIM) == head_of((16, WIDTH), 0, 1)
    grad_pooled = split_dot(jnp.where(own, grad_row, 0.0), value, 1, 1)
    grad_probs = split_dot(grad_pooled, keys[...], 1, 1)
    prob = probs[0]
    weighted = prob * grad_probs[:HEADS][:, None, :]
    row_terms = jnp.sum(weighted, axis=2, keepdims=True)
    grad_scores = (weighted - prob * row_terms) * (1.0 / math.sqrt(HEAD_DIM))
    grad_scores = grad_scores.reshape(HEADS * QUERIES, -1)
    grad_absorbed = split_dot(grad_scores, keys[...])
    absorbed_out[...] = grad_absorbed.T
    grad_query = split_dot(grad_absorbed, key_w[0])
    shape = grad_query.shape
    grad_query = jnp.where(head_of(shape, 1, HEAD_DIM) == head_of(shape, 0, QUERIES), grad_query, 0.0)
    query_out[...] = jnp.sum(grad_query.reshape(HEADS, QUERIES, WIDTH), axis=0)


def attention_back(layer, grad_film, attention_whole, key_w, probs, keys):
    parts, _, _, rows, _ = attention_whole.shape
    count = keys.shape[0]

    def one(shape):
        return pl.BlockSpec((1,) + shape, lambda k: (layer,) + (0,) * len(shape))

    return kernel_call(
        attention_back_kernel,
        (1,),
        [
            fixed(1, GATES),
            pl.BlockSpec((parts, 1, 1, rows, GATES), lambda k: (0, layer, 0, 0, 0)),
            pl.BlockSpec((parts, 1, 1, rows, GATES), lambda k: (0, layer, 1, 0, 0)),
            one((WIDTH, WIDTH)),
            one((HEADS, QUERIES, count)),
            fixed(count, WIDTH),
        ],
        [fixed(WIDTH, HEADS * QUERIES), fixed(QUERIES, WIDTH), fixed(1, WIDTH), fixed(1, WIDTH)],
        [(WIDTH, HEADS * QUERIES), (QUERIES, WIDTH), (1, WIDTH), (1, WIDTH)],
        [],
        10 * WIDTH * HEADS * QUERIES * count // 4,
    )(grad_film, attention_whole, attention_whole, key_w, probs, keys)


def factor_kernel(
    rows, step_rows, pooled, means, mixeds, embeds, absorbed, query_rows, seeds, query_w,
    step_out, seeds_out, query_out, key_out, value_out, mixing_out, film_out, square_out,
):
    share = embeds.shape[1]
    at = {}
    start = 0
    for name, size in (("row", WIDTH), ("mixed", WIDTH), ("film", GATES)):
        for layer in range(LAYERS):
            at[name, layer] = rows[:, start : start + size]
            start += size
    for layer in range(LAYERS):
        at["step", layer] = step_rows[:, layer * WIDTH : (layer + 1) * WIDTH]
    square = jnp.zeros((1, 1), jnp.float32)
    own = head_of((HEADS, share, WIDTH), 2, HEAD_DIM) == head_of((HEADS, share, WIDTH), 0, 1)
    near = head_of((HEADS * QUERIES, WIDTH), 1, HEAD_DIM) == head_of((HEADS * QUERIES, WIDTH), 0, QUERIES)
    for layer in range(LAYERS):
        value = exact_dot(pooled[layer], at["row", layer], 0, 0).reshape(HEADS, share, WIDTH)
        spread = jnp.where(near, jnp.concatenate([query_rows[0, layer]] * HEADS, axis=0), 0.0)
        grads = (
            (step_out, exact_dot(embeds[...], at["step", layer], 0, 0)),
            (seeds_out, exact_dot(query_w[layer], query_rows[1, layer], 1, 1)),
            (query_out, exact_dot(seeds[layer], query_rows[1, layer])),
            (key_out, exact_dot(absorbed[layer], spread)),
            (value_out, QUERIES * jnp.sum(jnp.where(own, value, 0.0), axis=0)),
            (mixing_out, exact_dot(means[layer], at["mixed", layer], 0, 0)),
            (film_out, exact_dot(mixeds[layer], at["film", layer], 0, 0)),
        )
        for out, grad in grads:
            out[layer] = grad
            square = square + jnp.sum(jnp.sum(grad * grad, axis=1, keepdims=True), axis=0, keepdims=True)
    square_out[...] = square


def square_kernel(square, *refs):
    *sums, out = refs
    total = square[...]
    for part in sums:
        total = total + jnp.sum(jnp.sum(part[...] * part[...], axis=1, keepdims=True), axis=0, keepdims=True)
    out[...] = jnp.broadcast_to(total[None], out.shape)


def clip_kernel(squares, sums_0, sums_1, *refs):
    places = squares[:, 0, :1]
    norm_square = jnp.sum(places, axis=0, keepdims=True)
    factor = jnp.minimum(1.0, CLIP_NORM / jnp.sqrt(norm_square))
    count = (len(refs) - 3) // 2
    grads, outs = refs[:count], refs[count : 2 * count]
    conv_out, cond_out, out_out = refs[2 * count :]
    for grad, out in zip(grads, outs):
        for layer in range(LAYERS):
            out[layer] = grad[layer] * factor
    share = cond_out.shape[1]
    for layer, sums in enumerate((sums_0, sums_1)):
        conv_out[layer] = sums[: 3 * share] * factor
        cond_out[layer] = sums[3 * share : 4 * share] * factor
        out_out[layer] = sums[4 * share :] * factor


def shapes_of(*shapes):
    return [jax.ShapeDtypeStruct(shape, jnp.float32) for shape in shapes]


HALF = jnp.bfloat16
PARTS = 32
PLACES = (
    [(pair // 2 % 2) * 8 + pair % 2 * 4 + pair // 4 % 2 * 2 + pair // 8 for pair in range(PARTS // 2)],
    [pair % 2 * 8 + (pair // 2 % 2) * 4 + pair // 4 % 2 * 2 + pair // 8 for pair in range(PARTS // 2)],
)
CONV_ROWS, PART_ROWS = 3 * WIDTH // PARTS, WIDTH // PARTS
TILE = 256


def halves_of(array):
    high = array.astype(HALF)
    return high, (array - high.astype(jnp.float32)).astype(HALF)


def three_dots(left, right, left_dim, right_dim):
    def dot(one, other):
        dims = (((left_dim,), (right_dim,)), ((), ()))
        return lax.dot_general(one, other, dims, preferred_element_type=jnp.float32)

    return dot(left[0], right[0]) + (dot(left[0], right[1]) + dot(left[1], right[0]))


def tile_of(pair, start, dim, size=TILE):
    return tuple(lax.slice_in_dim(half, start, start + size, axis=dim) for half in pair)


def moved(rows, steps):
    count = rows.shape[0]
    place = lax.broadcasted_iota(jnp.int32, rows.shape, 0) - steps
    return jnp.where((place >= 0) & (place < count), pltpu.roll(rows, steps % count, 0), 0.0)


def shape_of(*sizes):
    dtype = jnp.float32 if isinstance(sizes[-1], int) else sizes[-1]
    return jax.ShapeDtypeStruct(tuple(size for size in sizes if isinstance(size, int)), dtype)


def kernel_call(kernel, grid, in_specs, out_specs, out_shapes, scratch, macs, mebibytes=52):
    return pl.pallas_call(
        kernel,
        grid=grid,
        in_specs=in_specs,
        out_specs=out_specs,
        out_shape=[shape_of(*shape) for shape in out_shapes],
        scratch_shapes=scratch,
        compiler_params=pltpu.CompilerParams(vmem_limit_bytes=mebibytes * 2**20),
        cost_estimate=pl.CostEstimate(flops=1 * macs, bytes_accessed=16 * 2**20, transcendentals=0),
    )


def fixed(*shape):
    return pl.BlockSpec(shape, lambda k: (0,) * len(shape))


def part_rows(size, at):
    return pl.BlockSpec((PARTS, size, GATES), lambda k: (0, at, 0))


CONV_SPEC = pl.BlockSpec((PARTS // 2, CONV_ROWS, GATES), lambda k: (jnp.minimum(k, 1), 0, 0))
COND_SPEC = part_rows(PART_ROWS, 3)
OUT_SPEC = part_rows(PART_ROWS, 4)


def gates_kernel(dilation, frames, cond, conv_w, cond_w, step_row, live, tanh, sig, total):
    k = pl.program_id(0)

    def add(left, right, first):
        for start in range(0, GATES, TILE):
            part = three_dots(left, tile_of(right, start, 1), 1, 0)
            total[:, start : start + TILE] = part if first else total[:, start : start + TILE] + part

    @pl.when(k == 0)
    def _():
        hidden = (frames[...] + step_row[...]) * live[...]
        taps = jnp.concatenate([moved(hidden, dilation), hidden[:, : WIDTH // 2]], axis=1)
        add(halves_of(taps), halves_of(conv_w[...].reshape(-1, GATES)), True)

    @pl.when(k == 1)
    def _():
        hidden = (frames[...] + step_row[...]) * live[...]
        taps = jnp.concatenate([hidden[:, WIDTH // 2 :], moved(hidden, -dilation)], axis=1)
        add(halves_of(taps), halves_of(conv_w[...].reshape(-1, GATES)), False)

    @pl.when(k == 2)
    def _():
        left, right = halves_of(cond[...]), halves_of(cond_w[...].reshape(-1, GATES))
        for start in range(0, WIDTH, TILE):
            part = three_dots(left, tile_of(right, start, 1), 1, 0)
            tanh[:, start : start + TILE] = jnp.tanh(total[:, start : start + TILE] + part)
        for start in range(0, WIDTH, TILE):
            part = three_dots(left, tile_of(right, WIDTH + start, 1), 1, 0)
            sig[:, start : start + TILE] = jax.nn.sigmoid(total[:, WIDTH + start : WIDTH + start + TILE] + part)


def layer_gates(whole, frames, cond, step_row, live, dilation):
    count = frames.shape[0]
    return kernel_call(
        functools.partial(gates_kernel, dilation),
        (3,),
        [fixed(count, WIDTH)] * 2 + [CONV_SPEC, COND_SPEC, fixed(1, WIDTH), fixed(count, 1)],
        [fixed(count, WIDTH)] * 2,
        [(count, WIDTH)] * 2,
        [pltpu.VMEM((count, GATES), jnp.float32)],
        4 * count * WIDTH * GATES,
    )(frames, cond, whole, whole, step_row, live)


def post_kernel(tanh, sig, film, out_w, frames, skip, live, frames_next, skip_next, high, low):
    @pl.when(pl.program_id(0) == 0)
    def _():
        high[...], low[...] = halves_of(out_w[...].reshape(-1, GATES))

    modulated = halves_of(tanh[...] * sig[...] * (1.0 + film[:1]) + film[1:])
    for start in range(0, WIDTH, TILE):
        cut = slice(start, start + TILE)
        post = three_dots(modulated, (high[:, cut], low[:, cut]), 1, 0)
        frames_next[:, cut] = (frames[:, cut] + post) * (live[...] * ROOT_HALF)
    for start in range(0, WIDTH, TILE):
        cut, far = slice(start, start + TILE), slice(WIDTH + start, WIDTH + start + TILE)
        post = three_dots(modulated, (high[:, far], low[:, far]), 1, 0)
        skip_next[:, cut] = skip[:, cut] + post * live[...]


def layer_post(whole, tanh, sig, film, frames, skip, live):
    count = frames.shape[0]
    rows = pl.BlockSpec((count // 2, WIDTH), lambda k: (k, 0))
    return kernel_call(
        post_kernel,
        (2,),
        [rows, rows, fixed(2, WIDTH), OUT_SPEC, rows, rows, pl.BlockSpec((count // 2, 1), lambda k: (k, 0))],
        [rows, rows],
        [(count, WIDTH)] * 2,
        [pltpu.VMEM((WIDTH, GATES), HALF)] * 2,
        count * WIDTH * GATES,
    )(tanh, sig, film.reshape(2, WIDTH), whole, frames, skip, live)


def back_gates_kernel(
    grad_frames, grad_skip, live, tanh, sig, film, out_w, pre_high, pre_low, grad_film, grad_out, high, low
):
    k = pl.program_id(0)

    @pl.when(k == 0)
    def _():
        high[...], low[...] = halves_of(out_w[...].reshape(-1, GATES))
        grad_film[...] = jnp.zeros_like(grad_film)

    post = jnp.concatenate([grad_frames[...] * (live[...] * ROOT_HALF), grad_skip[...] * live[...]], axis=1)
    post = halves_of(post)
    for start in range(0, WIDTH, TILE):
        cut, far = slice(start, start + TILE), slice(WIDTH + start, WIDTH + start + TILE)
        grad_mod = three_dots(post, (high[cut, :], low[cut, :]), 1, 1)
        t, s = tanh[:, cut], sig[:, cut]
        gate = t * s
        grad_film[0:1, cut] += jnp.sum(grad_mod * gate, axis=0, keepdims=True)
        grad_film[1:2, cut] += jnp.sum(grad_mod, axis=0, keepdims=True)
        grad_gate = grad_mod * (1.0 + film[:1, cut])
        pre_high[:, cut], pre_low[:, cut] = halves_of(grad_gate * (s * (1.0 - t * t)))
        pre_high[:, far], pre_low[:, far] = halves_of(grad_gate * (gate * (1.0 - s)))
    modulated = tanh[...] * sig[...] * (1.0 + film[:1]) + film[1:]
    modulated = halves_of(modulated.T)

    @pl.when(k == 0)
    def _():
        for start in range(0, GATES, TILE):
            grad_out[:, start : start + TILE] = three_dots(modulated, tile_of(post, start, 1), 1, 0)

    @pl.when(k > 0)
    def _():
        for start in range(0, GATES, TILE):
            grad_out[:, start : start + TILE] += three_dots(modulated, tile_of(post, start, 1), 1, 0)


def layer_back_gates(whole, tanh, sig, film, grad_frames, grad_skip, live):
    count = tanh.shape[0]
    rows = pl.BlockSpec((count // 2, WIDTH), lambda k: (k, 0))
    return kernel_call(
        back_gates_kernel,
        (2,),
        [rows, rows, pl.BlockSpec((count // 2, 1), lambda k: (k, 0)), rows, rows, fixed(2, WIDTH), OUT_SPEC],
        [pl.BlockSpec((count // 2, GATES), lambda k: (k, 0))] * 2 + [fixed(2, WIDTH), fixed(WIDTH, GATES)],
        [(count, GATES, HALF)] * 2 + [(2, WIDTH), (WIDTH, GATES)],
        [pltpu.VMEM((WIDTH, GATES), HALF)] * 2,
        2 * count * WIDTH * GATES,
    )(grad_frames, grad_skip, live, tanh, sig, film.reshape(2, WIDTH), whole)


def back_weights_kernel(
    dilation, core, frames, cond, step_row, live, pre_high, pre_low, grad_out,
    top_stays, low_stays, top_goes, low_goes, high, low, conv_rows, cond_rows,
):
    @pl.when(pl.program_id(0) == 0)
    def _():
        hidden = ((frames[...] + step_row[...]) * live[...]).T
        count = hidden.shape[1]
        for tap, steps in enumerate((dilation, 0, -dilation)):
            moved_rows = hidden
            if steps:
                place = lax.broadcasted_iota(jnp.int32, hidden.shape, 1) - steps
                moved_rows = pltpu.roll(hidden, steps % count, 1)
                moved_rows = jnp.where((place >= 0) & (place < count), moved_rows, 0.0)
            cut = slice(tap * WIDTH, (tap + 1) * WIDTH)
            high[cut, :], low[cut, :] = halves_of(moved_rows)
        cut = slice(3 * WIDTH, 4 * WIDTH)
        high[cut, :], low[cut, :] = halves_of(cond[...].T)

    grad = (pre_high[...], pre_low[...])
    for start in range(0, 4 * WIDTH, 2 * TILE):
        cut = slice(start, start + 2 * TILE)
        part = three_dots((high[cut, :], low[cut, :]), grad, 1, 0)
        if start < 3 * WIDTH:
            conv_rows[cut, :] = part
        else:
            cond_rows[start - 3 * WIDTH : start - 3 * WIDTH + 2 * TILE, :] = part
    half = top_goes.shape[1]
    rest = CONV_ROWS - half
    for top_out, low_out, parity in ((top_stays, low_stays, core[0]), (top_goes, low_goes, 1 - core[0])):
        for pair in range(PARTS // 2):
            part = 2 * pair + parity
            rows = pl.multiple_of(part * CONV_ROWS, 8)
            top_out[PLACES[0][pair]] = conv_rows[pl.ds(rows, half), :]
            place = PLACES[1][pair]
            low_out[place, :rest, :] = conv_rows[pl.ds(rows + half, rest), :]
            rows = pl.multiple_of(part * PART_ROWS, 8)
            low_out[place, rest : rest + PART_ROWS, :] = cond_rows[pl.ds(rows, PART_ROWS), :]
            low_out[place, rest + PART_ROWS :, :] = grad_out[pl.ds(rows, PART_ROWS), :]


def layer_back_weights(core, frames, cond, step_row, live, grad_pre, grad_out, dilation):
    count = frames.shape[0]
    part = (PARTS // 2, (CONV_ROWS + 2 * PART_ROWS) // 2)
    columns = pl.BlockSpec(part + (TILE,), lambda k: (0, 0, k))
    return kernel_call(
        functools.partial(back_weights_kernel, dilation),
        (GATES // TILE,),
        [pl.BlockSpec(memory_space=pltpu.SMEM)]
        + [fixed(count, WIDTH)] * 2
        + [fixed(1, WIDTH), fixed(count, 1)]
        + [pl.BlockSpec((rows, TILE), lambda k: (0, k)) for rows in (count, count, WIDTH)],
        [columns] * 4,
        [part + (GATES,)] * 4,
        [pltpu.VMEM((4 * WIDTH, count), HALF)] * 2
        + [pltpu.VMEM((rows, TILE), jnp.float32) for rows in (3 * WIDTH, WIDTH)],
        4 * count * WIDTH * GATES,
    )(core, frames, cond, step_row, live, *grad_pre, grad_out)


def back_frames_kernel(dilation, pre_high, pre_low, conv_w, grad_frames, live, grad_next, step_sum, total):
    k = pl.program_id(0)
    middle = WIDTH // 2
    grad, weight = (pre_high[...], pre_low[...]), halves_of(conv_w[...].reshape(-1, GATES))

    def taps(start):
        return three_dots(grad, tile_of(weight, start, 0), 1, 1)

    @pl.when(k == 0)
    def _():
        for start in range(0, WIDTH, TILE):
            total[:, start : start + TILE] = moved(taps(start), -dilation)
        total[:, :middle] += taps(WIDTH)

    @pl.when(k == 1)
    def _():
        total[:, middle:] += taps(0)
        for start in range(0, WIDTH, TILE):
            cut = slice(start, start + TILE)
            hidden = (total[:, cut] + moved(taps(middle + start), dilation)) * live[...]
            step_sum[:, cut] = jnp.sum(hidden, axis=0, keepdims=True)
            grad_next[:, cut] = grad_frames[:, cut] * (live[...] * ROOT_HALF) + hidden


def layer_back_frames(whole, grad_pre, grad_frames, live, dilation):
    count = grad_pre[0].shape[0]
    return kernel_call(
        functools.partial(back_frames_kernel, dilation),
        (2,),
        [fixed(count, GATES)] * 2 + [CONV_SPEC, fixed(count, WIDTH), fixed(count, 1)],
        [fixed(count, WIDTH), fixed(1, WIDTH)],
        [(count, WIDTH), (1, WIDTH)],
        [pltpu.VMEM((count, WIDTH), jnp.float32)],
        3 * count * WIDTH * GATES,
    )(*grad_pre, whole, grad_frames, live)


def on_device(
    frames_in,
    conditioning,
    prompt,
    item_lengths,
    prompt_lengths,
    key_mask,
    diffusion_steps,
    step_proj,
    conv_weight,
    cond_proj,
    out_proj,
    query_seeds,
    query_proj,
    key_proj,
    value_proj,
    mixing_proj,
    film_proj,
    cot_frames,
    cot_skip,
    devices,
):
    rings, pairs = rings_of(devices), pairs_of(devices)
    share = step_proj.shape[1]
    key_count = prompt.shape[1]
    extra_size = key_count + LAYERS * share * QUERIES
    extra_rows = -(-(extra_size + 1) // WIDTH)
    key_rows = -(-(key_count + extra_rows) // 8) * 8
    me = lax.axis_index(AXIS)

    frame_packs = [
        jnp.concatenate([conv_weight[layer], cond_proj[layer], out_proj[layer]], axis=0) for layer in range(LAYERS)
    ]
    frame_whole_0 = lax.all_gather(frame_packs[0], AXIS, axis=0, tiled=False)

    extra = (
        key_mask.astype(jnp.float32),
        to_all(query_seeds, devices),
        to_all(diffusion_steps.astype(jnp.float32), devices),
    )
    extra = jnp.concatenate(extra, axis=1)
    extra = jnp.pad(extra, ((0, 0), (0, (key_rows - key_count) * WIDTH - extra.shape[1])))
    sent = jnp.concatenate([prompt, extra.reshape(prompt.shape[0], -1, WIDTH)], axis=1)
    query_key = jnp.concatenate([query_proj, key_proj], axis=2).reshape(LAYERS * share, GATES)
    query_key, sent = tie(query_key, sent)
    keys = lax.all_to_all(sent, AXIS, split_axis=0, concat_axis=0, tiled=True)
    extra = keys[:, key_count : key_count + extra_rows].reshape(devices, -1)
    key_place = (
        jnp.arange(devices, dtype=jnp.int32)[:, None] * key_count
        + jnp.arange(key_rows, dtype=jnp.int32)[None, :]
    )
    masked_in = jnp.pad(extra[:, :key_count], ((0, 0), (0, key_rows - key_count)))
    live_keys = (
        (jnp.arange(key_rows, dtype=jnp.int32)[None, :] < key_count)
        & (key_place < lax.dynamic_index_in_dim(prompt_lengths, me, 0, keepdims=False))
        & ((masked_in == 1.0) | (key_place == 0))
    ).reshape(-1)
    seeds = extra[:, key_count:extra_size]
    seeds = jnp.moveaxis(seeds.reshape(devices, LAYERS, share, QUERIES), 1, 0)
    seeds = seeds.reshape(LAYERS, WIDTH, QUERIES)
    keys = keys.reshape(-1, WIDTH)

    embeds = jax.vmap(step_embedding)(extra[:, extra_size])
    own_embeds = lax.dynamic_slice_in_dim(embeds, me * share, share, 1)
    step_part = jnp.einsum("bw,lwx->blx", own_embeds, step_proj, precision=HIGHEST)

    query_key = gather_rows(query_key, rings).reshape(devices, LAYERS, share, GATES)
    query_key = jnp.moveaxis(query_key, 1, 0).reshape(LAYERS, WIDTH, GATES)
    query_rows = jnp.einsum("lwq,lwx->lqx", seeds, query_key[:, :, :WIDTH], precision=HIGHEST)
    query_heads = query_rows.reshape(LAYERS, QUERIES, HEADS, HEAD_DIM)
    key_heads = query_key[:, :, WIDTH:].reshape(LAYERS, WIDTH, HEADS, HEAD_DIM)
    absorbed = jnp.einsum("lqhe,lwhe->lhqw", query_heads, key_heads, precision=HIGHEST)
    absorbed = absorbed.reshape(LAYERS * HEADS * QUERIES, WIDTH) / math.sqrt(HEAD_DIM)

    scores = jnp.where(live_keys[None, :], small_dot(absorbed, keys, 1, 1), -1e30)
    exps = jnp.exp(scores - jnp.max(scores, axis=1, keepdims=True))
    probs = exps / jnp.sum(exps, axis=1, keepdims=True)
    probs = probs.reshape(LAYERS, HEADS, QUERIES, -1)
    pooled = jnp.mean(probs, axis=2).reshape(LAYERS * HEADS, -1)
    pooled_keys = small_dot(pooled, keys)

    frame_pack_1, frame_whole_0, pooled_keys = tie(frame_packs[1], frame_whole_0, pooled_keys)
    frame_whole_1 = lax.all_gather(frame_pack_1, AXIS, axis=0, tiled=False)

    pooled_cut, step_rows = exchange(by_column(pooled_keys, devices), step_part)
    step_rows = jnp.sum(step_rows, axis=0).reshape(LAYERS, 1, WIDTH)
    pooled_cut = pooled_cut.reshape(devices, LAYERS, HEADS, share)
    pooled_cut, frame_whole_0, frames_in, conditioning = tie(pooled_cut, frame_whole_0, frames_in, conditioning)
    value_heads = value_proj.reshape(LAYERS, share, HEADS, HEAD_DIM)
    mean_part = jnp.einsum("blhw,lwhe->blhe", pooled_cut, value_heads, precision=HIGHEST)
    (mean_cut,) = exchange(by_column(mean_part.reshape(devices, LAYERS, WIDTH), devices))
    mean_cut = jnp.sum(mean_cut, axis=0).reshape(devices, LAYERS, share)
    mixed_part = jnp.einsum("blw,lwx->blx", mean_cut, mixing_proj, precision=HIGHEST)
    (mixed_cut,) = exchange(by_column(mixed_part, devices))
    mixed_cut = jnp.sum(mixed_cut, axis=0).reshape(devices, LAYERS, share)
    film_part = jnp.einsum("blw,lwx->blx", mixed_cut, film_proj, precision=HIGHEST)
    (films,) = exchange(film_part)
    films = jnp.sum(films, axis=0).reshape(LAYERS, 1, GATES)
    films, cot_frames, cot_skip = tie(films, cot_frames, cot_skip)

    live = (jnp.arange(frames_in.shape[1], dtype=jnp.int32) < item_lengths[0]).astype(jnp.float32)[:, None]
    frames, cond, cot, cot_last = frames_in[0], conditioning[0], cot_frames[0], cot_skip[0]
    if devices != PARTS:
        frame_whole_0 = regrouped(frame_whole_0, share)
    tanh_0, sig_0 = layer_gates(frame_whole_0, frames, cond, step_rows[0], live, 1)
    frames_1, skip = layer_post(frame_whole_0, tanh_0, sig_0, films[0], frames, jnp.zeros_like(frames), live)

    attention_pack = jnp.concatenate(
        [
            part
            for layer in range(LAYERS)
            for part in (film_proj[layer], jnp.concatenate([value_proj[layer], mixing_proj[layer]], axis=1))
        ],
        axis=0,
    )
    attention_pack, frame_whole_1, frames_1 = tie(attention_pack, frame_whole_1, frames_1)
    attention_whole = lax.all_gather(attention_pack, AXIS, axis=0, tiled=False)
    attention_whole = attention_whole.reshape(devices, LAYERS, 2, share, GATES)
    if devices != PARTS:
        attention_whole = jnp.transpose(attention_whole, (1, 2, 0, 3, 4)).reshape(1, LAYERS, 2, WIDTH, GATES)
        frame_whole_1 = regrouped(frame_whole_1, share)

    tanh_1, sig_1 = layer_gates(frame_whole_1, frames_1, cond, step_rows[1], live, 2)

    def by_device(grad):
        return grad.reshape(devices, -1, GATES)

    def by_share(grad):
        return grad.reshape(devices, share, -1)

    core = (me % 2 if devices == PARTS else jnp.zeros_like(me)).astype(jnp.int32).reshape(1)
    *grad_pre_1, grad_film_1, grad_out = layer_back_gates(frame_whole_1, tanh_1, sig_1, films[1], cot, cot_last, live)
    parts = layer_back_weights(core, frames_1, cond, step_rows[1], live, grad_pre_1, grad_out, 2)
    sum_1 = RowSum.of_parts(*parts, pairs)

    def post_1(tanh, sig, grad_pre):
        return layer_post(frame_whole_1, tanh, sig, films[1], frames_1, skip, live), grad_pre

    (frames, skip), grad_pre_1 = beside([sum_1], post_1, tanh_1, sig_1, grad_pre_1)

    def frames_and_gates(grad_pre):
        grad_frames, step_sum = layer_back_frames(frame_whole_1, grad_pre, cot, live, 2)
        gates = layer_back_gates(frame_whole_0, tanh_0, sig_0, films[0], grad_frames, cot_last, live)
        return grad_frames, step_sum, *gates

    grad_frames, step_sum_1, *grad_pre_0, grad_film_0, grad_out = beside([sum_1], frames_and_gates, grad_pre_1)

    def weights_0(grad_pre):
        return layer_back_weights(core, frames_in[0], cond, step_rows[0], live, grad_pre, grad_out, 1), grad_pre

    parts, grad_pre_0 = beside([sum_1], weights_0, grad_pre_0)
    sum_1.join()
    sum_b = RowSum.of_parts(*parts, pairs)
    key_w = query_key[:, :, WIDTH:]

    def attentions(grad_film_1, grad_film_0):
        later = attention_back(1, grad_film_1, attention_whole, key_w, probs, keys)
        return *later, *attention_back(0, grad_film_0, attention_whole, key_w, probs, keys)

    grad_film_0, grad_film_1 = grad_film_0.reshape(1, GATES), grad_film_1.reshape(1, GATES)
    absorbed_1, query_1, row_1, mixed_1, absorbed_0, query_0, row_0, mixed_0 = beside(
        [sum_b, sum_1], attentions, grad_film_1, grad_film_0
    )
    sum_d = RowSum([by_share(absorbed_0), by_share(absorbed_1)], pairs, far_first=True)
    query_parts = jnp.stack([query_0, query_1]).reshape(devices, -1)
    first_rows = jnp.concatenate(
        [part.reshape(-1) for part in (row_0, row_1, mixed_0, mixed_1, grad_film_0, grad_film_1)]
    )

    def frames_and_rows(grad_pre, query_parts, first_rows):
        came = exchange(query_parts, to_all(first_rows, devices))
        return *layer_back_frames(frame_whole_0, grad_pre, grad_frames, live, 1), *came

    grad_frames, step_sum_0, query_cut, first_rows = beside(
        [sum_b, sum_1], frames_and_rows, grad_pre_0, query_parts, first_rows
    )
    sum_d.step()
    query_cut = jnp.sum(query_cut, axis=0)
    last_rows = jnp.concatenate([part.reshape(-1) for part in (step_sum_0, step_sum_1, query_cut)])
    (last_rows,) = beside([sum_d, sum_b], exchange, to_all(last_rows, devices))
    sum_b.join()
    (sum_d.state,) = sum_b.step(sum_d.state)
    while sum_d.at < len(pairs):
        sum_d.step()
    sum_d.join()
    query_grads = last_rows[:, LAYERS * WIDTH :].reshape(LAYERS, QUERIES, WIDTH)
    absorbed_sums = sum_d.result().reshape(LAYERS, share, HEADS * QUERIES)

    small = [(LAYERS, share, columns) for columns in (WIDTH, QUERIES, WIDTH, WIDTH, WIDTH, WIDTH, GATES)]
    *factored, square = pl.pallas_call(factor_kernel, out_shape=shapes_of(*small, (1, 1)))(
        first_rows,
        last_rows[:, : LAYERS * WIDTH],
        jnp.moveaxis(pooled_cut.reshape(devices, LAYERS, HEADS * share), 1, 0),
        jnp.moveaxis(mean_cut, 1, 0),
        jnp.moveaxis(mixed_cut, 1, 0),
        own_embeds,
        absorbed_sums,
        jnp.stack([query_rows, query_grads]),
        query_seeds,
        query_proj,
    )
    frame_sums = (sum_b.result(), sum_1.result())
    squares = pl.pallas_call(square_kernel, out_shape=shapes_of((devices, 8, 128))[0])(square, *frame_sums)
    squares = lax.all_to_all(squares, AXIS, split_axis=0, concat_axis=0, tiled=True)
    frame_shapes = [(LAYERS, rows_of * share, GATES) for rows_of in (3, 1, 1)]
    outs = pl.pallas_call(clip_kernel, out_shape=shapes_of(*small, *frame_shapes))(squares, *frame_sums, *factored)
    step_grad, seeds_grad, query_grad, key_grad, value_grad, mixing_grad, film_grad, conv_grad, cond_grad, out_grad = outs
    return (
        frames[None],
        skip[None],
        grad_frames[None],
        step_grad,
        conv_grad,
        cond_grad,
        out_grad,
        seeds_grad,
        query_grad,
        key_grad,
        value_grad,
        mixing_grad,
        film_grad,
    )


def solution(mesh):
    devices = mesh.shape[AXIS]

    def run(*args):
        return on_device(*args, devices=devices)

    items, rows = P(AXIS, None, None), P(None, AXIS, None)
    return jax.shard_map(
        run,
        mesh=mesh,
        in_specs=(items, items, rows, P(AXIS), P(), P(None, AXIS), P(AXIS)) + (rows,) * 10 + (items, items),
        out_specs=(items,) * 3 + (rows,) * 10,
        check_vma=False,
    )
```
